512 devices in a mesh: lat: 16 (over y_hi, x, core), lon: 32 (over z, y_lo).
Axes of the slice: x: 4, y: 4 (y_hi: 2, y_lo: 2; y = y_hi * 2 + y_lo), z: 16, core: 2. Of those that a mesh axis runs over, the one named last changes fastest.
Arguments:
- grid: bfloat16 [2, 96, 384, 192], P(None, 'lat', 'lon'), may hold values from -6 to 6
- region_ids: int32 [2, 96, 384], P(None, 'lat', 'lon'), may hold values from 1 to 8, as said below
- cotangent: bfloat16 [2, 96, 384, 192], P(None, 'lat', 'lon'), may hold values from -6 to 6
- norm_gain: float32 [2, 192], replicated, may hold values from 0.25 to 1.75
- norm_shift: float32 [2, 192], replicated, may hold values from -1.5 to 1.5
- qkv_weight: bfloat16 [192, 576], replicated, may hold values from -0.4375 to 0.4375
- qkv_bias: float32 [576], replicated, may hold values from -1.5 to 1.5
- proj_weight: bfloat16 [192, 192], replicated, may hold values from -0.4375 to 0.4375
- proj_bias: float32 [192], replicated, may hold values from -1.5 to 1.5
- fc1_weight: bfloat16 [192, 768], replicated, may hold values from -0.4375 to 0.4375
- fc1_bias: float32 [768], replicated, may hold values from -1.5 to 1.5
- fc2_weight: bfloat16 [768, 192], replicated, may hold values from -0.21875 to 0.21875
- fc2_bias: float32 [192], replicated, may hold values from -1.5 to 1.5
- bias_table: float32 [1, 16, 6, 3312], P(None, 'lat'), may hold values from -3 to 400
- pair_index: int32 [144, 144], replicated, may hold values from 0 to 3311
Outputs:
- output: bfloat16 [2, 96, 384, 192], P(None, 'lat', 'lon')
- grid_grad: bfloat16 [2, 96, 384, 192], P(None, 'lat', 'lon')
- norm_gain_grad: float32 [2, 192], replicated
- norm_shift_grad: float32 [2, 192], replicated
- qkv_weight_grad: float32 [192, 576], replicated
- qkv_bias_grad: float32 [576], replicated
- proj_weight_grad: float32 [192, 192], replicated
- proj_bias_grad: float32 [192], replicated
- fc1_weight_grad: float32 [192, 768], replicated
- fc1_bias_grad: float32 [768], replicated
- fc2_weight_grad: float32 [768, 192], replicated
- fc2_bias_grad: float32 [192], replicated
- table_grad: float32 [1, 16, 6, 3312], P(None, 'lat')
The draws below stay inside these ranges and needn't reach their ends.
Inputs may be any that keep to these rules, and one draw needn't show every extreme that they name: `region_ids`: labels depend on level and latitude row only, not on longitude.
All inputs are finite; a program needn't handle non-finite values.
Results may differ from the reference program's by a relative error of at most 0.018.
Values may be sent and summed in bfloat16 or wider, within the bound.
A program may use at most 64 MiB of HBM per device.

```python
import math
import jax
import jax.numpy as jnp
from jax import lax

C = 192
HEADS = 6
FF = 768
WZ = 2
WLAT = 6
WLON = 12
WTOK = 144
NBIAS = 3312
LEV = 2
NLAT = 96
NLON = 384
NWZ = 1
NWLAT = 16


def draw_region_ids(key, part):
    key = jax.random.fold_in(key, 11)
    starts = (jax.random.randint(key, (LEV, NLAT), 0, 4) == 0).astype(jnp.int32)
    counted = jnp.cumsum(starts, 1)
    labels = 1 + counted % 8
    row_index = lax.broadcasted_iota(jnp.int32, (LEV, NLAT), 1)
    labels = jnp.where(row_index == 0, 1, jnp.where(row_index == NLAT - 1, 8, labels))
    return jnp.broadcast_to(labels[:, :, None], (LEV, NLAT, NLON)).astype(jnp.int32)


def draw_bias_table(key, part):
    key = jax.random.fold_in(key, 7)
    key_base = jax.random.fold_in(key, 0)
    shape = (NWZ, NWLAT, HEADS, NBIAS)
    values = 0.7 * jax.random.truncated_normal(key_base, -4.0, 4.0, shape, jnp.float32)
    return values.astype(jnp.float32)


def plant(values, stream_key, least, high):
    dims = values.shape
    place = [jax.random.randint(jax.random.fold_in(stream_key, axis), (), 0, dims[axis]) for axis in range(len(dims))]
    values = values.at[tuple(place)].set(least)
    longest = dims.index(max(dims))
    place[longest] = (place[longest] + 1) % dims[longest]
    return values.at[tuple(place)].set(high)


def shard_levels(key, extent, shards, smallest, high):
    loudness = 1.0
    for position, parts in shards:
        heights = jax.random.uniform(jax.random.fold_in(jax.random.fold_in(key, 6), position), (parts,), jnp.float32, smallest / len(shards), high / len(shards))
        loudness = loudness * jnp.repeat(jnp.exp(heights), extent[position] // parts).reshape((-1,) + (1,) * (len(extent) - 1 - position))
    return loudness


def scatter_about(key, shape, width, reach, shards=(), kind=jnp.bfloat16):
    values = jax.random.normal(key, shape, jnp.float32) * width
    if len(shards) > 0:
        values = shard_levels(key, shape, shards, -0.22, 0.18) * values
    return jnp.clip(values, min=-reach, max=reach).astype(kind)


def setup_inputs(seed: int = 0) -> dict:
    key_of = jax.random.split(jax.random.key(seed), 16)
    grid = scatter_about(key_of[0], (LEV, NLAT, NLON, C), 1.0, 6.0, ((1, 16), (2, 32)))
    region_ids = draw_region_ids(jax.random.fold_in(key_of[15], 71), 0)
    cotangent = scatter_about(key_of[2], (LEV, NLAT, NLON, C), 1.0, 6.0, ((1, 16), (2, 32)))
    norm_gain = jnp.clip(1.0 + 0.15 * jax.random.normal(key_of[3], (2, C), jnp.float32), 0.25, 1.75)
    norm_shift = scatter_about(key_of[4], (2, C), 0.3, 1.5, (), jnp.float32)
    qkv_weight = scatter_about(key_of[5], (C, 3 * C), C ** -0.5, 0.4375)
    qkv_bias = scatter_about(key_of[6], (3 * C,), 0.3, 1.5, (), jnp.float32)
    proj_weight = scatter_about(key_of[7], (C, C), C ** -0.5, 0.4375)
    proj_bias = scatter_about(key_of[8], (C,), 0.3, 1.5, (), jnp.float32)
    fc1_weight = scatter_about(key_of[9], (C, FF), C ** -0.5, 0.4375)
    fc1_bias = scatter_about(key_of[10], (FF,), 0.3, 1.5, (), jnp.float32)
    fc2_weight = scatter_about(key_of[11], (FF, C), FF ** -0.5, 0.21875)
    fc2_bias = scatter_about(key_of[12], (C,), 0.3, 1.5, (), jnp.float32)
    bias_table = draw_bias_table(jax.random.fold_in(key_of[15], 71), 0)
    pair_index = plant(jax.random.randint(key_of[14], (WTOK, WTOK), 0, NBIAS), jax.random.fold_in(key_of[14], 1), 0, NBIAS - 1).astype(jnp.int32)
    return dict(grid=grid, region_ids=region_ids, cotangent=cotangent, norm_gain=norm_gain, norm_shift=norm_shift, qkv_weight=qkv_weight, qkv_bias=qkv_bias, proj_weight=proj_weight, proj_bias=proj_bias, fc1_weight=fc1_weight, fc1_bias=fc1_bias, fc2_weight=fc2_weight, fc2_bias=fc2_bias, bias_table=bias_table, pair_index=pair_index)


NEG_FILL = -1e+30
NORM_EPS = 1e-05
ROOT_HALF = 1.0 / math.sqrt(2.0)
ROOT_TWOPI = 1.0 / math.sqrt(2.0 * math.pi)

def mixing(form, left_op, right_op):
    return jnp.einsum(form, left_op.astype(jnp.float32), right_op.astype(jnp.float32))

def layer_norm(values, gain_row, shift_row):
    centred = values - lax.optimization_barrier(jnp.mean(values, -1, keepdims=True))
    inv_std = lax.rsqrt(lax.optimization_barrier(jnp.mean(centred * centred, -1, keepdims=True)) + NORM_EPS)
    normed = centred * inv_std
    return (normed * gain_row + shift_row, normed, inv_std)

def norm_back(incoming, normed, inv_std, gain_row):
    scaled = incoming * gain_row
    outgoing = inv_std * (scaled - lax.optimization_barrier(jnp.mean(scaled, -1, keepdims=True)) - normed * lax.optimization_barrier(jnp.mean(scaled * normed, -1, keepdims=True)))
    return (outgoing, lax.optimization_barrier(jnp.sum(incoming * normed, 0)), lax.optimization_barrier(jnp.sum(incoming, 0)))

def to_windows(field):
    levels, lat_rows, lon_cols = field.shape[:3]
    trailing = field.shape[3:]
    shaped = field.reshape((levels // WZ, WZ, lat_rows // WLAT, WLAT, lon_cols // WLON, WLON) + trailing)
    order_axes = (0, 2, 4, 1, 3, 5) + tuple(range(6, 6 + len(trailing)))
    return shaped.transpose(order_axes).reshape((levels // WZ, lat_rows // WLAT, lon_cols // WLON, WZ * WLAT * WLON) + trailing)

def from_windows(windows, levels, lat_rows, lon_cols):
    channels = windows.shape[-1]
    shaped = windows.reshape(levels // WZ, lat_rows // WLAT, lon_cols // WLON, WZ, WLAT, WLON, channels)
    return shaped.transpose(0, 3, 1, 4, 2, 5, 6).reshape(levels, lat_rows, lon_cols, channels)

def attention_forward(inputs, window_ids, pair_bias, params):
    channels = inputs.shape[-1]
    num_heads = pair_bias.shape[2]
    head_size = channels // num_heads
    flat_in = inputs.reshape(-1, channels).astype(jnp.float32)
    normed_in, hat_one, inv_one = layer_norm(flat_in, params[0][0], params[1][0])
    first_b = normed_in.astype(jnp.bfloat16)
    triple = (jnp.dot(first_b, params[2], preferred_element_type=jnp.float32) + params[3]).astype(jnp.bfloat16)
    triple = triple.reshape(inputs.shape[:4] + (3, num_heads, head_size))
    queries = triple[:, :, :, :, 0]
    keys_b = triple[:, :, :, :, 1]
    values_b = triple[:, :, :, :, 2]
    scores = mixing('xyzihd,xyzjhd->xyzhij', queries, keys_b) * head_size ** (-0.5) + pair_bias[:, :, None]
    allowed = (window_ids[..., :, None] == window_ids[..., None, :])[:, :, :, None]
    scores = jnp.where(allowed, scores, NEG_FILL)
    weights = jnp.exp(scores - lax.optimization_barrier(jnp.max(scores, -1, keepdims=True)))
    softmax_f = weights / lax.optimization_barrier(jnp.sum(weights, -1, keepdims=True))
    softmax_b = softmax_f.astype(jnp.bfloat16)
    mixed_b = mixing('xyzhij,xyzjhd->xyzihd', softmax_b, values_b).astype(jnp.bfloat16).reshape(-1, channels)
    attended = flat_in + jnp.dot(mixed_b, params[4], preferred_element_type=jnp.float32) + params[5]
    return (attended, (hat_one, inv_one, first_b, queries, keys_b, values_b, softmax_f, softmax_b, mixed_b))

def mlp_forward(attended, params):
    normed_two, hat_two, inv_two = layer_norm(attended, params[0][1], params[1][1])
    second_b = normed_two.astype(jnp.bfloat16)
    hidden = jnp.dot(second_b, params[6], preferred_element_type=jnp.float32) + params[7]
    cumul = 0.5 * (1.0 + lax.erf(hidden * ROOT_HALF))
    active_b = (hidden * cumul).astype(jnp.bfloat16)
    result = (attended + jnp.dot(active_b, params[8], preferred_element_type=jnp.float32) + params[9]).astype(jnp.bfloat16)
    return (result, (hat_two, inv_two, second_b, hidden, cumul, active_b))

def mlp_backward(incoming_b, saved, params):
    hat_two, inv_two, second_b, hidden, cumul, active_b = saved
    grad_out = incoming_b.astype(jnp.float32)
    fc2_w_grad = jnp.dot(active_b.T, incoming_b, preferred_element_type=jnp.float32)
    fc2_b_grad = lax.optimization_barrier(jnp.sum(grad_out, 0))
    d_active = jnp.dot(incoming_b, params[8].T, preferred_element_type=jnp.float32)
    d_hidden = d_active * (cumul + hidden * jnp.exp(-0.5 * hidden * hidden) * ROOT_TWOPI)
    d_hidden_b = d_hidden.astype(jnp.bfloat16)
    fc1_w_grad = jnp.dot(second_b.T, d_hidden_b, preferred_element_type=jnp.float32)
    fc1_b_grad = lax.optimization_barrier(jnp.sum(d_hidden, 0))
    d_second = jnp.dot(d_hidden_b, params[6].T, preferred_element_type=jnp.float32)
    back_two, gain_two, shift_two = norm_back(d_second, hat_two, inv_two, params[0][1])
    return (grad_out + back_two, (fc1_w_grad, fc1_b_grad, fc2_w_grad, fc2_b_grad), gain_two, shift_two)

def attention_backward(d_attended, saved, params):
    hat_one, inv_one, first_b, queries, keys_b, values_b, softmax_f, softmax_b, mixed_b = saved
    head_size = queries.shape[-1]
    d_att_b = d_attended.astype(jnp.bfloat16)
    proj_w_grad = jnp.dot(mixed_b.T, d_att_b, preferred_element_type=jnp.float32)
    proj_b_grad = lax.optimization_barrier(jnp.sum(d_attended, 0))
    d_mixed = jnp.dot(d_att_b, params[4].T, preferred_element_type=jnp.float32).astype(jnp.bfloat16).reshape(queries.shape)
    d_softmax = mixing('xyzihd,xyzjhd->xyzhij', d_mixed, values_b)
    d_values = mixing('xyzhij,xyzihd->xyzjhd', softmax_b, d_mixed)
    d_scores = softmax_f * (d_softmax - lax.optimization_barrier(jnp.sum(d_softmax * softmax_f, -1, keepdims=True)))
    d_pairs = lax.optimization_barrier(jnp.sum(d_scores, 2))
    d_scaled = (d_scores * head_size ** (-0.5)).astype(jnp.bfloat16)
    d_queries = mixing('xyzhij,xyzjhd->xyzihd', d_scaled, keys_b)
    d_keys = mixing('xyzhij,xyzihd->xyzjhd', d_scaled, queries)
    d_triple = jnp.stack([d_queries, d_keys, d_values], 4).reshape(first_b.shape[0], -1)
    d_triple_b = d_triple.astype(jnp.bfloat16)
    qkv_w_grad = jnp.dot(first_b.T, d_triple_b, preferred_element_type=jnp.float32)
    qkv_b_grad = lax.optimization_barrier(jnp.sum(d_triple, 0))
    d_first = jnp.dot(d_triple_b, params[2].T, preferred_element_type=jnp.float32)
    back_one, gain_one, shift_one = norm_back(d_first, hat_one, inv_one, params[0][0])
    d_inputs = (d_attended + back_one).astype(jnp.bfloat16)
    return (d_inputs, (qkv_w_grad, qkv_b_grad, proj_w_grad, proj_b_grad), gain_one, shift_one, d_pairs)

def table_gradient(d_pairs, pair_index):
    zwin, latwin, num_heads = d_pairs.shape[:3]
    flat_terms = d_pairs.reshape(zwin * latwin * num_heads, -1)
    summed = jax.ops.segment_sum(flat_terms.T, pair_index.reshape(-1), num_segments=NBIAS)
    return summed.T.reshape(zwin, latwin, num_heads, NBIAS)

def reference(grid, region_ids, cotangent, norm_gain, norm_shift, qkv_weight, qkv_bias, proj_weight, proj_bias, fc1_weight, fc1_bias, fc2_weight, fc2_bias, bias_table, pair_index):
    params = (norm_gain, norm_shift, qkv_weight, qkv_bias, proj_weight, proj_bias, fc1_weight, fc1_bias, fc2_weight, fc2_bias)
    offsets = (-(WZ // 2), -(WLAT // 2), -(WLON // 2))
    returns_by = (WZ // 2, WLAT // 2, WLON // 2)
    all_axes = (0, 1, 2)
    win_grid = jnp.moveaxis(to_windows(jnp.roll(grid, offsets, all_axes)), 2, 0)
    win_ids = jnp.moveaxis(to_windows(jnp.roll(region_ids, offsets, all_axes)), 2, 0)
    win_cot = jnp.moveaxis(to_windows(jnp.roll(cotangent, offsets, all_axes)), 2, 0)
    pair_bias = jnp.take(bias_table, pair_index, axis=3)
    zero_grads = jax.tree.map(lambda member: jnp.zeros(member.shape, jnp.float32), params)
    start_carry = (zero_grads, jnp.zeros(pair_bias.shape, jnp.float32))

    def column_step(carry, column):
        grid_col, ids_col, cot_col = column
        grid_col = grid_col[:, :, None]
        ids_col = ids_col[:, :, None]
        attended, saved_att = attention_forward(grid_col, ids_col, pair_bias, params)
        result, saved_mlp = mlp_forward(attended, params)
        d_attended, mlp_grads, gain_two, shift_two = mlp_backward(cot_col.reshape(-1, cot_col.shape[-1]), saved_mlp, params)
        d_inputs, att_grads, gain_one, shift_one, d_pairs = attention_backward(d_attended, saved_att, params)
        grads = (jnp.stack([gain_one, gain_two]), jnp.stack([shift_one, shift_two])) + att_grads + mlp_grads
        carry = jax.tree.map(jnp.add, carry, (grads, d_pairs))
        return (carry, (result.reshape(cot_col.shape), d_inputs.reshape(cot_col.shape)))
    (grads, d_pairs), (results, d_inputs) = lax.scan(column_step, start_carry, (win_grid, win_ids, win_cot))
    output = jnp.roll(from_windows(jnp.moveaxis(results, 0, 2), LEV, NLAT, NLON), returns_by, all_axes)
    grid_grad = jnp.roll(from_windows(jnp.moveaxis(d_inputs, 0, 2), LEV, NLAT, NLON), returns_by, all_axes)
    gain_grad, shift_grad, qkv_w_grad, qkv_b_grad, proj_w_grad, proj_b_grad, fc1_w_grad, fc1_b_grad, fc2_w_grad, fc2_b_grad = grads
    return (output, grid_grad, gain_grad, shift_grad, qkv_w_grad, qkv_b_grad, proj_w_grad, proj_b_grad, fc1_w_grad, fc1_b_grad, fc2_w_grad, fc2_b_grad, table_gradient(d_pairs, pair_index))
```

```python
import math

import jax
import jax.numpy as jnp
import numpy as np
from jax import lax
from jax.experimental import pallas as pl
from jax.experimental.pallas import tpu as pltpu
from jax.sharding import PartitionSpec as P

F32 = jnp.float32
BF16 = jnp.bfloat16
MESH = pl.DeviceIdType.MESH

C = 192
HEADS = 6
HEAD = 32
FF = 768
TOK = 144
NBIAS = 3312
NHI = 26
NEG_FILL = -1e30
NORM_EPS = 1e-05
ROOT_HALF = 1.0 / math.sqrt(2.0)
ROOT_TWOPI = 1.0 / math.sqrt(2.0 * math.pi)
SCALE = HEAD ** (-0.5)

ROWS = 3584
FC2_ROW = 0
FC1_ROW = 1152
QP_ROW = 2304
SMALL_ROW = 3456
CHUNKS = ((0, 64), (2048, 48))
OWNED = 112
ZROWS = 7


def dot(a, b, ca=1, cb=0):
    return lax.dot_general(a, b, (((ca,), (cb,)), ((), ())), preferred_element_type=F32)


def selectors():
    padded = lambda l, r, q: (l * 6 + r) * 16 + q
    send = np.zeros((144, 192), np.float32)
    gather = np.zeros((144, 336), np.float32)
    send_out = np.zeros((144, 144), np.float32)
    place = np.zeros((192, 288), np.float32)
    for l in range(2):
        for i in range(6):
            for j in range(12):
                tok = l * 72 + i * 12 + j
                lev = (l + 1) % 2
                far_i, far_j = i >= 3, j >= 6
                if not far_i and not far_j:
                    gather[tok, padded(lev, i + 3, j + 6)] = 1
                    place[padded(lev, i + 3, j + 6), tok] = 1
                    continue
                d = 2 if (far_i and far_j) else (1 if far_i else 0)
                m = d * 48 + l * 18 + (i % 3) * 6 + (j % 6)
                r = i - 3 if far_i else i + 3
                q = j - 6 if far_j else j + 6
                send[m, padded(lev, r, q)] = 1
                gather[tok, 192 + m] = 1
                send_out[m, tok] = 1
                place[padded(lev, r, q), 144 + m] = 1
    return [jnp.asarray(a, BF16) for a in (send, gather, send_out, place)]


def bias_kernel(table_ref, index_ref, bias_ref, tab, idx, idx_t, left):
    tab[...] = jnp.zeros_like(tab)
    tab[0:HEADS, 0:NBIAS] = table_ref[0, 0]
    idx[...] = jnp.zeros_like(idx)
    idx[:, 0:TOK] = index_ref[...]
    tail = idx[:, 128:256].astype(F32).T
    idx_t[:, 0:TOK] = tail[0:16].astype(jnp.int32)
    idx_t[:, TOK:256] = jnp.zeros((16, 256 - TOK), jnp.int32)
    left[...] = jnp.zeros_like(left)

    def look(flat, store):
        lo = flat & 127
        hi = flat >> 7
        for h in range(HEADS):
            acc = jnp.zeros((8, 128), F32)
            for t in range(NHI):
                row = jnp.broadcast_to(tab[h : h + 1, t * 128 : (t + 1) * 128], (8, 128))
                got = jnp.take_along_axis(row, lo, axis=1, mode="promise_in_bounds")
                acc = jnp.where(hi == t, got, acc)
            store(h, acc)

    def body(b, carry):
        at = pl.multiple_of(b * 8, 8)

        def store(h, acc):
            bias_ref[h, pl.ds(at, 8), 0:128] = acc

        look(idx[pl.ds(at, 8), 0:128], store)
        return carry

    lax.fori_loop(0, TOK // 8, body, 0)
    for a in range(2):
        for t in range(2):

            def store(h, acc, a=a, t=t):
                left[h, a * 8 : a * 8 + 8, t * 128 : (t + 1) * 128] = acc

            look(idx_t[a * 8 : a * 8 + 8, t * 128 : (t + 1) * 128], store)
    for h in range(HEADS):
        bias_ref[h, :, 128:TOK] = left[h].T[0:TOK, 0:16]


def layer_norm(values, gain_row, shift_row):
    centred = values - jnp.mean(values, -1, keepdims=True)
    inv_std = lax.rsqrt(jnp.mean(centred * centred, -1, keepdims=True) + NORM_EPS)
    normed = centred * inv_std
    return normed * gain_row + shift_row, normed, inv_std


def norm_back(incoming, normed, inv_std, gain_row):
    scaled = incoming * gain_row
    outgoing = inv_std * (
        scaled
        - jnp.mean(scaled, -1, keepdims=True)
        - normed * jnp.mean(scaled * normed, -1, keepdims=True)
    )
    return (
        outgoing,
        jnp.sum(incoming * normed, 0, keepdims=True),
        jnp.sum(incoming, 0, keepdims=True),
    )


def main_kernel(
    grid_ref,
    ids_ref,
    cot_ref,
    gain_ref,
    shift_ref,
    wqkv_ref,
    bqkv_ref,
    wproj_ref,
    bproj_ref,
    w1_ref,
    b1_ref,
    w2_ref,
    b2_ref,
    bias_ref,
    index_ref,
    send_sel,
    gather_sel,
    send_out_sel,
    place_sel,
    out_ref,
    din_ref,
    full_ref,
    tgrad_ref,
    stack,
    halo_msg,
    out_stack,
    out_msg,
    probs,
    act,
    dfac,
    dsc,
    small,
    grads,
    core_in1,
    core_in2,
    plane_in1,
    plane_in2,
    z_out,
    z_in,
    z_all,
    owned,
    t_out,
    t_in,
    halo_s,
    halo_r,
    oh_s,
    oh_r,
    core_s,
    core_r,
    plane_s,
    plane_r,
    zs,
    zr,
    zgs,
    zgr,
    ts,
    tr,
    tgs,
    tgr,
    ags,
    agr,
    fs,
    fr,
):
    lat = lax.axis_index("lat")
    lon = lax.axis_index("lon")
    core = lat % 2
    pair_lat = lat + 1 - 2 * core
    ylo = lon % 2
    z = lon // 2
    k = (lat // 2) * 2 + ylo
    lat_up, lat_dn = (lat + 1) % 16, (lat + 15) % 16
    lon_up, lon_dn = (lon + 1) % 32, (lon + 31) % 32

    def plane_device(kk):
        return ((kk // 2) * 2 + core, z * 2 + kk % 2)

    barrier = pltpu.get_barrier_semaphore()

    def greet(device):
        pl.semaphore_signal(barrier, inc=1, device_id=device, device_id_type=MESH)

    def greet_lon(d, carry):
        greet((lat, (lon + d) % 32))
        return carry

    def greet_plane(d, carry):
        greet(plane_device((k + d) % 16))
        return carry

    lax.fori_loop(1, 32, greet_lon, 0)
    lax.fori_loop(1, 16, greet_plane, 0)
    greet((pair_lat, lon))
    for device in ((lat_up, lon), (lat_dn, lon), (lat_up, lon_up), (lat_dn, lon_dn)):
        greet(device)

    stack[:, 0:192, :] = jnp.zeros((2, 192, 256), BF16)
    for l in range(2):
        for r in range(6):
            at = (l * 6 + r) * 16
            stack[0, at : at + 12, 0:C] = grid_ref[l, r]
            stack[1, at : at + 12, 0:C] = cot_ref[l, r]
            label = ids_ref[l, r : r + 1, 0:1].astype(F32)
            stack[0, at : at + 16, C:256] = jnp.broadcast_to(label, (16, 64)).astype(BF16)
    for n in range(2):
        halo_msg[n] = dot(send_sel[...], stack[n, 0:192, :]).astype(BF16)

    pl.semaphore_wait(barrier, 51)

    halo_to = ((lat, lon_dn), (lat_dn, lon), (lat_dn, lon_dn))
    halo = [
        pltpu.make_async_remote_copy(
            src_ref=halo_msg.at[:, d * 48 : (d + 1) * 48, :],
            dst_ref=stack.at[:, 192 + d * 48 : 192 + (d + 1) * 48, :],
            send_sem=halo_s.at[d],
            recv_sem=halo_r.at[d],
            device_id=halo_to[d],
            device_id_type=MESH,
        )
        for d in range(3)
    ]
    for copy in halo:
        copy.start()
    for copy in halo:
        copy.wait()

    win = dot(gather_sel[...], stack[0])
    g_b = dot(gather_sel[...], stack[1]).astype(BF16)[:, 0:C]
    x = win[:, 0:C]
    label_lane = win[:, 128:256].astype(BF16)
    pick = (lax.broadcasted_iota(jnp.int32, (8, 128), 1) == 64).astype(F32).astype(BF16)
    ids_row = dot(pick, label_lane, 1, 1)[0:1]
    ids_col = win[:, C : C + 1]
    allowed = ids_row == ids_col

    gain0, gain1 = gain_ref[0:1, :], gain_ref[1:2, :]
    shift0, shift1 = shift_ref[0:1, :], shift_ref[1:2, :]
    first, hat1, inv1 = layer_norm(x, gain0, shift0)
    first_b = first.astype(BF16)
    wq = wqkv_ref[:, 0:C]
    wk = wqkv_ref[:, C : 2 * C]
    wv = wqkv_ref[:, 2 * C : 3 * C]
    q = (dot(first_b, wq) + bqkv_ref[:, 0:C]).astype(BF16)
    key = (dot(first_b, wk) + bqkv_ref[:, C : 2 * C]).astype(BF16)
    v = (dot(first_b, wv) + bqkv_ref[:, 2 * C : 3 * C]).astype(BF16)
    lane = lax.broadcasted_iota(jnp.int32, (TOK, C), 1)

    def only(h, values):
        return jnp.where((lane >> 5) == h, values, jnp.zeros_like(values))

    mixed = jnp.zeros((TOK, C), F32)
    for h in range(HEADS):
        s = dot(only(h, q), key, 1, 1) * SCALE + bias_ref[h]
        s = jnp.where(allowed, s, NEG_FILL)
        e = jnp.exp(s - jnp.max(s, -1, keepdims=True))
        p = e * (1.0 / jnp.sum(e, -1, keepdims=True))
        probs[h] = p
        mixed = mixed + dot(p.astype(BF16), only(h, v))
    mixed_b = mixed.astype(BF16)
    attended = x + dot(mixed_b, wproj_ref[...]) + bproj_ref[...]

    second, hat2, inv2 = layer_norm(attended, gain1, shift1)
    second_b = second.astype(BF16)
    for b in range(FF // 128):
        cols = slice(b * 128, (b + 1) * 128)
        hidden = dot(second_b, w1_ref[:, cols]) + b1_ref[:, cols]
        cumul = 0.5 * (1.0 + lax.erf(hidden * ROOT_HALF))
        act[:, cols] = (hidden * cumul).astype(BF16)
        dfac[:, cols] = cumul + hidden * jnp.exp(-0.5 * hidden * hidden) * ROOT_TWOPI
    result = (attended + dot(act[...], w2_ref[...]) + b2_ref[...]).astype(BF16)

    halo_out_to = ((lat, lon_up), (lat_up, lon), (lat_up, lon_up))

    def send_back(n, values):
        out_stack[n, 0:TOK, 0:C] = values
        out_msg[n, :, 0:C] = dot(send_out_sel[...], values).astype(BF16)
        copies = [
            pltpu.make_async_remote_copy(
                src_ref=out_msg.at[n, d * 48 : (d + 1) * 48, :],
                dst_ref=out_stack.at[n, TOK + d * 48 : TOK + (d + 1) * 48, :],
                send_sem=oh_s.at[n, d],
                recv_sem=oh_r.at[n, d],
                device_id=halo_out_to[d],
                device_id_type=MESH,
            )
            for d in range(3)
        ]
        for copy in copies:
            copy.start()
        return copies

    out_copies = send_back(0, result)

    small[...] = jnp.zeros_like(small)

    def keep(row, vector):
        width = vector.shape[1]
        for at in range(0, width, 128):
            n = min(128, width - at)
            small[row + at // 128 : row + at // 128 + 1, 0:n] = vector[:, at : at + n]

    gf = g_b.astype(F32)
    keep(21, jnp.sum(gf, 0, keepdims=True))
    d_second = jnp.zeros((TOK, C), F32)
    for b in range(FF // 128):
        cols = slice(b * 128, (b + 1) * 128)
        grads[FC2_ROW + b * C : FC2_ROW + (b + 1) * C, :] = dot(g_b, act[:, cols], 0, 0).astype(BF16)
        d_hidden = dot(g_b, w2_ref[cols, :], 1, 1) * dfac[:, cols]
        d_hidden_b = d_hidden.astype(BF16)
        keep(15 + b, jnp.sum(d_hidden, 0, keepdims=True))
        grads[FC1_ROW + b * C : FC1_ROW + (b + 1) * C, :] = dot(second_b, d_hidden_b, 0, 0).astype(BF16)
        d_second = d_second + dot(d_hidden_b, w1_ref[:, cols], 1, 1)

    core_in = (core_in1, core_in2)
    plane_in = (plane_in1, plane_in2)

    def core_copy(n):
        base, rows = CHUNKS[n]
        return pltpu.make_async_remote_copy(
            src_ref=grads.at[pl.ds(pl.multiple_of(base + (1 - core) * 16 * rows, 16), 16 * rows), :],
            dst_ref=core_in[n],
            send_sem=core_s.at[n],
            recv_sem=core_r.at[n],
            device_id=(pair_lat, lon),
            device_id_type=MESH,
        )

    def add_core(n):
        base, rows = CHUNKS[n]
        mine = pl.ds(pl.multiple_of(base + core * 16 * rows, 16), 16 * rows)
        grads[mine, :] = (grads[mine, :].astype(F32) + core_in[n][...].astype(F32)).astype(BF16)

    def plane_copy(n, d):
        base, rows = CHUNKS[n]
        kk = (k + d) % 16
        return pltpu.make_async_remote_copy(
            src_ref=grads.at[pl.ds(pl.multiple_of(base + (core * 16 + kk) * rows, 16), rows), :],
            dst_ref=plane_in[n].at[d],
            send_sem=plane_s.at[n, d],
            recv_sem=plane_r.at[n, d],
            device_id=plane_device(kk),
            device_id_type=MESH,
        )

    def each(first_d, last_d, body):
        def step(d, carry):
            body(d)
            return carry

        lax.fori_loop(first_d, last_d, step, 0)

    def add_plane(n):
        base, rows = CHUNKS[n]
        total = grads[pl.ds(pl.multiple_of(base + (core * 16 + k) * rows, 16), rows), :].astype(F32)
        for d in range(1, 16):
            total = total + plane_in[n][d].astype(F32)
        return total

    core_copy(0).start()

    back2, dgain1, dshift1 = norm_back(d_second, hat2, inv2, gain1)
    keep(2, dgain1)
    keep(6, dshift1)
    d_att = gf + back2
    d_att_b = d_att.astype(BF16)
    core_copy(0).wait()
    add_core(0)
    each(1, 16, lambda d: plane_copy(0, d).start())

    def put_pair(at, left, right):
        grads[at : at + C, :] = left[:, 0:128].astype(BF16)
        grads[at + C : at + 2 * C, :] = right[:, 0:128].astype(BF16)
        grads[at + 2 * C : at + 3 * C, :] = jnp.concatenate([left[:, 128:C], right[:, 128:C]], 1).astype(BF16)

    dw_proj = dot(mixed_b, d_att_b, 0, 0)
    keep(13, jnp.sum(d_att, 0, keepdims=True))
    dm = dot(d_att_b, wproj_ref[...], 1, 1).astype(BF16)

    dq = jnp.zeros((TOK, C), F32)
    dk = jnp.zeros((TOK, C), F32)
    dv = jnp.zeros((TOK, C), F32)
    for h in range(HEADS):
        p = probs[h]
        dm_h = only(h, dm)
        dp = dot(dm_h, v, 1, 1)
        ds = p * (dp - jnp.sum(dp * p, -1, keepdims=True))
        dsc[h, :, 0:128] = ds[:, 0:128]
        dsc[h, :, 128:256] = jnp.concatenate([ds[:, 128:TOK], jnp.zeros((TOK, 112), F32)], 1)
        ds_b = (ds * SCALE).astype(BF16)
        dq = dq + dot(ds_b, only(h, key))
        dk = dk + dot(ds_b, only(h, q), 0, 0)
        dv = dv + dot(p.astype(BF16), dm_h, 0, 0)
    dq_b, dk_b, dv_b = dq.astype(BF16), dk.astype(BF16), dv.astype(BF16)
    put_pair(QP_ROW, dot(first_b, dq_b, 0, 0), dot(first_b, dk_b, 0, 0))
    put_pair(QP_ROW + 3 * C, dot(first_b, dv_b, 0, 0), dw_proj)
    d_bias = jnp.concatenate(
        [jnp.sum(dq, 0, keepdims=True), jnp.sum(dk, 0, keepdims=True), jnp.sum(dv, 0, keepdims=True)], 1
    )
    keep(8, d_bias)
    d_first = dot(dq_b, wq, 1, 1) + dot(dk_b, wk, 1, 1) + dot(dv_b, wv, 1, 1)
    back1, dgain0, dshift0 = norm_back(d_first, hat1, inv1, gain0)
    keep(0, dgain0)
    keep(4, dshift0)
    grads[SMALL_ROW : SMALL_ROW + 32, :] = small[...].astype(BF16)
    grads[SMALL_ROW + 32 : ROWS, :] = jnp.zeros((ROWS - SMALL_ROW - 32, 128), BF16)
    core_copy(1).start()
    din_copies = send_back(1, (d_att + back1).astype(BF16))
    core_copy(1).wait()
    add_core(1)
    each(1, 16, lambda d: plane_copy(1, d).start())

    hi_iota = lax.broadcasted_iota(jnp.int32, (32, 256), 0)
    lo_iota = lax.broadcasted_iota(jnp.int32, (128, 256), 0)

    def factors(flat, rows):
        width = flat.shape[1]
        is_hi = hi_iota[:, 0:width] == (flat >> 7)
        lo_hot = jnp.where(lo_iota[:, 0:width] == (flat & 127), 1.0, 0.0).astype(BF16)
        left = jnp.concatenate([jnp.where(is_hi, row, 0.0).astype(BF16) for row in rows], 0)
        return dot(left, lo_hot, 1, 1)

    def pairs(b, total):
        block = pl.ds(pl.multiple_of(b * 8, 8), 8)
        flat = index_ref[block, 0:128]
        rows = [dsc[h, block, 0:128] for h in range(HEADS)]
        two = lambda values, r: jnp.concatenate([values[r : r + 1], values[r + 1 : r + 2]], 1)
        for r in range(0, 8, 2):
            total = total + factors(two(flat, r), [two(values, r) for values in rows])
        return total

    table = lax.fori_loop(0, TOK // 8, pairs, jnp.zeros((HEADS * 32, 128), F32))
    flat_tail = jnp.concatenate([index_ref[:, 128:TOK].astype(F32), jnp.zeros((TOK, 112), F32)], 1).T[0:16]
    flat_tail = flat_tail.astype(jnp.int32)
    ds_tail = [dsc[h, :, 128:256].T for h in range(HEADS)]
    for r in range(16):
        table = table + factors(flat_tail[r : r + 1], [t[r : r + 1] for t in ds_tail])
    for n in range(32):
        t_out[n] = table[n * 6 : (n + 1) * 6]

    def t_copy(d):
        to = (lon + d) % 32
        return pltpu.make_async_remote_copy(
            src_ref=t_out.at[to],
            dst_ref=t_in.at[d],
            send_sem=ts.at[d],
            recv_sem=tr.at[d],
            device_id=(lat, to),
            device_id_type=MESH,
        )

    each(1, 32, lambda d: t_copy(d).start())

    each(1, 16, lambda d: plane_copy(0, d).wait())
    owned[0:64, :] = add_plane(0)
    each(1, 16, lambda d: plane_copy(1, d).wait())
    owned[64:OWNED, :] = add_plane(1)
    for n in range(16):
        z_out[n] = owned[n * ZROWS : (n + 1) * ZROWS, :]

    def z_copy(d):
        to = (z + d) % 16
        return pltpu.make_async_remote_copy(
            src_ref=z_out.at[to],
            dst_ref=z_in.at[d],
            send_sem=zs.at[d],
            recv_sem=zr.at[d],
            device_id=(lat, to * 2 + ylo),
            device_id_type=MESH,
        )

    def z_gather(d):
        to = (z + d) % 16
        return pltpu.make_async_remote_copy(
            src_ref=z_all.at[z],
            dst_ref=z_all.at[z],
            send_sem=zgs.at[d],
            recv_sem=zgr.at[d],
            device_id=(lat, to * 2 + ylo),
            device_id_type=MESH,
        )

    each(1, 16, lambda d: z_copy(d).start())
    each(1, 16, lambda d: z_copy(d).wait())
    total = z_out[z]
    for d in range(1, 16):
        total = total + z_in[d]
    z_all[z] = total
    each(1, 16, lambda d: z_gather(d).start())

    each(1, 32, lambda d: t_copy(d).wait())
    t_total = t_out[lon]
    for d in range(1, 32):
        t_total = t_total + t_in[d]
    tgrad_ref[lon] = t_total

    def t_gather(d):
        return pltpu.make_async_remote_copy(
            src_ref=tgrad_ref.at[lon],
            dst_ref=tgrad_ref.at[lon],
            send_sem=tgs.at[d],
            recv_sem=tgr.at[d],
            device_id=(lat, (lon + d) % 32),
            device_id_type=MESH,
        )

    each(1, 32, lambda d: t_gather(d).start())

    each(1, 16, lambda d: z_gather(d).wait())
    for n in range(16):
        owned[n * ZROWS : (n + 1) * ZROWS, :] = z_all[n]
    full_ref[core, k] = owned[...].astype(BF16)

    def plane_gather(d):
        return pltpu.make_async_remote_copy(
            src_ref=full_ref.at[core, k],
            dst_ref=full_ref.at[core, k],
            send_sem=ags.at[d],
            recv_sem=agr.at[d],
            device_id=plane_device((k + d) % 16),
            device_id_type=MESH,
        )

    def forward(d):
        kk = (k + 16 - d) % 16
        return pltpu.make_async_remote_copy(
            src_ref=full_ref.at[core, kk],
            dst_ref=full_ref.at[core, kk],
            send_sem=fs.at[d],
            recv_sem=fr.at[d],
            device_id=(pair_lat, lon),
            device_id_type=MESH,
        )

    each(1, 16, lambda d: plane_gather(d).start())
    forward(0).start()

    def pass_on(d):
        plane_gather(d).wait()
        forward(d).start()

    each(1, 16, pass_on)

    for n, copies, ref in ((0, out_copies, out_ref), (1, din_copies, din_ref)):
        for copy in copies:
            copy.wait()
        ref[...] = dot(place_sel[...], out_stack[n, :, 0:C]).astype(BF16)
    each(0, 16, lambda d: forward(d).wait())
    each(1, 32, lambda d: t_gather(d).wait())


def final_kernel(
    out_ref,
    din_ref,
    full_ref,
    tgrad_ref,
    output,
    grid_grad,
    gain_grad,
    shift_grad,
    dwqkv,
    dbqkv,
    dwproj,
    dbproj,
    dw1,
    db1,
    dw2,
    db2,
    dtable,
):
    for l in range(2):
        for r in range(6):
            at = (l * 6 + r) * 16
            output[l, r] = out_ref[at : at + 12, :]
            grid_grad[l, r] = din_ref[at : at + 12, :]

    def rows(start, count):
        parts = []
        at = start
        while at < start + count:
            n = 0 if at < CHUNKS[1][0] else 1
            base, size = CHUNKS[n]
            owner, inside = divmod(at - base, size)
            take = min(size - inside, start + count - at)
            first = inside + (0 if n == 0 else CHUNKS[0][1])
            parts.append(full_ref[owner // 16, owner % 16, first : first + take, :])
            at += take
        return jnp.concatenate(parts, 0).astype(F32) if len(parts) > 1 else parts[0].astype(F32)

    for b in range(FF // 128):
        cols = slice(b * 128, (b + 1) * 128)
        dw2[cols, :] = rows(FC2_ROW + b * C, C).T
        dw1[:, cols] = rows(FC1_ROW + b * C, C)
    qa, ka, qk = (rows(QP_ROW + n * C, C) for n in range(3))
    va, pa, vp = (rows(QP_ROW + n * C, C) for n in range(3, 6))
    dwqkv[:, 0:128] = qa
    dwqkv[:, 128:C] = qk[:, 0:64]
    dwqkv[:, C : C + 128] = ka
    dwqkv[:, C + 128 : 2 * C] = qk[:, 64:128]
    dwqkv[:, 2 * C : 2 * C + 128] = va
    dwqkv[:, 2 * C + 128 : 3 * C] = vp[:, 0:64]
    dwproj[:, 0:128] = pa
    dwproj[:, 128:C] = vp[:, 64:128]
    vec = rows(SMALL_ROW, 32)

    def load(row, width, ref, at=0):
        for n in range(0, width, 128):
            m = min(128, width - n)
            ref[at : at + 1, n : n + m] = vec[row + n // 128 : row + n // 128 + 1, 0:m]

    load(0, C, gain_grad, 0)
    load(2, C, gain_grad, 1)
    load(4, C, shift_grad, 0)
    load(6, C, shift_grad, 1)
    load(8, 3 * C, dbqkv)
    load(13, C, dbproj)
    load(15, FF, db1)
    load(21, C, db2)
    for h in range(HEADS):
        for t in range(NHI):
            n = h * 32 + t
            m = min(128, NBIAS - t * 128)
            dtable[0, 0, h : h + 1, t * 128 : t * 128 + m] = tgrad_ref[n // 6, n % 6 : n % 6 + 1, 0:m]


def on_device(
    grid,
    region_ids,
    cotangent,
    norm_gain,
    norm_shift,
    qkv_weight,
    qkv_bias,
    proj_weight,
    proj_bias,
    fc1_weight,
    fc1_bias,
    fc2_weight,
    fc2_bias,
    bias_table,
    pair_index,
):
    vmem = pl.BlockSpec(memory_space=pltpu.VMEM)
    shape = jax.ShapeDtypeStruct
    pair_bias = pl.pallas_call(
        bias_kernel,
        out_shape=shape((HEADS, TOK, TOK), F32),
        in_specs=[vmem] * 2,
        out_specs=vmem,
        scratch_shapes=[
            pltpu.VMEM((8, 3328), F32),
            pltpu.VMEM((TOK, 256), jnp.int32),
            pltpu.VMEM((16, 256), jnp.int32),
            pltpu.VMEM((HEADS, 128, 256), F32),
        ],
        name="pair_bias",
        compiler_params=pltpu.CompilerParams(vmem_limit_bytes=32 * 1024 * 1024),
    )(bias_table, pair_index)

    dma = pltpu.SemaphoreType.DMA
    out, din, full, tgrad = pl.pallas_call(
        main_kernel,
        out_shape=(
            shape((192, C), BF16),
            shape((192, C), BF16),
            shape((2, 16, OWNED, 128), BF16),
            shape((32, 6, 128), F32),
        ),
        in_specs=[vmem] * 19,
        out_specs=(vmem,) * 4,
        scratch_shapes=[
            pltpu.VMEM((2, 336, 256), BF16),
            pltpu.VMEM((2, 144, 256), BF16),
            pltpu.VMEM((2, 288, 256), BF16),
            pltpu.VMEM((2, 144, 256), BF16),
            pltpu.VMEM((HEADS, TOK, TOK), F32),
            pltpu.VMEM((TOK, FF), BF16),
            pltpu.VMEM((TOK, FF), F32),
            pltpu.VMEM((HEADS, TOK, 256), F32),
            pltpu.VMEM((32, 128), F32),
            pltpu.VMEM((ROWS, 128), BF16),
            pltpu.VMEM((1024, 128), BF16),
            pltpu.VMEM((768, 128), BF16),
            pltpu.VMEM((16, 64, 128), BF16),
            pltpu.VMEM((16, 48, 128), BF16),
            pltpu.VMEM((16, ZROWS, 128), F32),
            pltpu.VMEM((16, ZROWS, 128), F32),
            pltpu.VMEM((16, ZROWS, 128), F32),
            pltpu.VMEM((OWNED, 128), F32),
            pltpu.VMEM((32, 6, 128), F32),
            pltpu.VMEM((32, 6, 128), F32),
            dma((3,)),
            dma((3,)),
            dma((2, 3)),
            dma((2, 3)),
            dma((2,)),
            dma((2,)),
            dma((2, 16)),
            dma((2, 16)),
            dma((16,)),
            dma((16,)),
            dma((16,)),
            dma((16,)),
            dma((32,)),
            dma((32,)),
            dma((32,)),
            dma((32,)),
            dma((16,)),
            dma((16,)),
            dma((16,)),
            dma((16,)),
        ],
        name="window_block",
        compiler_params=pltpu.CompilerParams(
            collective_id=0, has_side_effects=True, vmem_limit_bytes=48 * 1024 * 1024
        ),
    )(
        grid,
        region_ids,
        cotangent,
        norm_gain,
        norm_shift,
        qkv_weight,
        qkv_bias[None],
        proj_weight,
        proj_bias[None],
        fc1_weight,
        fc1_bias[None],
        fc2_weight,
        fc2_bias[None],
        pair_bias,
        pair_index,
        *selectors(),
    )
    outs = pl.pallas_call(
        final_kernel,
        out_shape=(
            shape(grid.shape, BF16),
            shape(grid.shape, BF16),
            shape((2, C), F32),
            shape((2, C), F32),
            shape((C, 3 * C), F32),
            shape((1, 3 * C), F32),
            shape((C, C), F32),
            shape((1, C), F32),
            shape((C, FF), F32),
            shape((1, FF), F32),
            shape((FF, C), F32),
            shape((1, C), F32),
            shape(bias_table.shape, F32),
        ),
        in_specs=[vmem] * 4,
        out_specs=(vmem,) * 13,
        name="outputs",
        compiler_params=pltpu.CompilerParams(vmem_limit_bytes=32 * 1024 * 1024),
    )(out, din, full, tgrad)
    outs = list(outs)
    for n in (5, 7, 9, 11):
        outs[n] = outs[n][0]
    return tuple(outs)


def solution(mesh):
    field = P(None, "lat", "lon", None)
    table = P(None, "lat", None, None)
    return jax.shard_map(
        on_device,
        mesh=mesh,
        in_specs=(field, P(None, "lat", "lon"), field) + (P(),) * 10 + (table, P()),
        out_specs=(field, field) + (P(),) * 10 + (table,),
        check_vma=False,
    )
```

```python
import math

import jax
import jax.numpy as jnp
import numpy as np
from jax import lax
from jax.experimental import pallas as pl
from jax.experimental.pallas import tpu as pltpu
from jax.sharding import PartitionSpec as P

F32 = jnp.float32
BF16 = jnp.bfloat16
MESH = pl.DeviceIdType.MESH

C = 192
HEADS = 6
HEAD = 32
FF = 768
TOK = 144
NBIAS = 3312
NHI = 26
NEG_FILL = -1e30
NORM_EPS = 1e-05
ROOT_HALF = 1.0 / math.sqrt(2.0)
ROOT_TWOPI = 1.0 / math.sqrt(2.0 * math.pi)
SCALE = HEAD ** (-0.5)

ROWS = 3584
FC2_ROW = 0
FC1_ROW = 1152
QP_ROW = 2304
SMALL_ROW = 3456
CHUNKS = ((0, 64), (2048, 48))
OWNED = 112
ZROWS = 7


def dot(a, b, ca=1, cb=0):
    return lax.dot_general(a, b, (((ca,), (cb,)), ((), ())), preferred_element_type=F32)


def selectors():
    held = lambda l, r, q: (r * 12 + q) * 2 + l
    send = np.zeros((144, 144), np.float32)
    gather = np.zeros((144, 288), np.float32)
    send_out = np.zeros((144, 144), np.float32)
    place = np.zeros((144, 288), np.float32)
    label = np.zeros((144, 16), np.float32)
    for l in range(2):
        for i in range(6):
            for j in range(12):
                label[held(l, i, j), i * 2 + l] = 1
                tok = l * 72 + i * 12 + j
                lev = (l + 1) % 2
                far_i, far_j = i >= 3, j >= 6
                r = i - 3 if far_i else i + 3
                q = j - 6 if far_j else j + 6
                if not far_i and not far_j:
                    gather[tok, held(lev, r, q)] = 1
                    place[held(lev, r, q), tok] = 1
                    continue
                d = 2 if (far_i and far_j) else (1 if far_i else 0)
                m = d * 48 + l * 18 + (i % 3) * 6 + (j % 6)
                send[m, held(lev, r, q)] = 1
                gather[tok, 144 + m] = 1
                send_out[m, tok] = 1
                place[held(lev, r, q), 144 + m] = 1
    return [jnp.asarray(a, BF16) for a in (send, gather, label, send_out, place)]


def look_up_bias(table_ref, index_ref, bias_ref, tab, idx, idx_t, left):
    tab[...] = jnp.zeros_like(tab)
    for h in range(HEADS):
        tab[h : h + 1, 0:NBIAS] = table_ref[0, h]
    idx[...] = jnp.zeros_like(idx)
    idx[:, 0:TOK] = index_ref[...]
    tail = idx[:, 128:256].astype(F32).T
    idx_t[:, 0:TOK] = tail[0:16].astype(jnp.int32)
    idx_t[:, TOK:256] = jnp.zeros((16, 256 - TOK), jnp.int32)
    left[...] = jnp.zeros_like(left)

    def look(flat, store):
        lo = flat & 127
        hi = flat >> 7
        for h in range(HEADS):
            acc = jnp.zeros((8, 128), F32)
            for t in range(NHI):
                row = jnp.broadcast_to(tab[h : h + 1, t * 128 : (t + 1) * 128], (8, 128))
                got = jnp.take_along_axis(row, lo, axis=1, mode="promise_in_bounds")
                acc = jnp.where(hi == t, got, acc)
            store(h, acc)

    def body(b, carry):
        at = pl.multiple_of(b * 8, 8)

        def store(h, acc):
            bias_ref[h, pl.ds(at, 8), 0:128] = acc

        look(idx[pl.ds(at, 8), 0:128], store)
        return carry

    lax.fori_loop(0, TOK // 8, body, 0)
    for a in range(2):
        for t in range(2):

            def store(h, acc, a=a, t=t):
                left[h, a * 8 : a * 8 + 8, t * 128 : (t + 1) * 128] = acc

            look(idx_t[a * 8 : a * 8 + 8, t * 128 : (t + 1) * 128], store)
    for h in range(HEADS):
        bias_ref[h, :, 128:TOK] = left[h].T[0:TOK, 0:16]


def around():
    lat = lax.axis_index("lat")
    lon = lax.axis_index("lon")
    return lat, lon, (lat + 1) % 16, (lat + 15) % 16, (lon + 1) % 32, (lon + 31) % 32


def greet(device):
    pl.semaphore_signal(pltpu.get_barrier_semaphore(), inc=1, device_id=device, device_id_type=MESH)


def greet_halo():
    lat, lon, lat_up, lat_dn, lon_up, lon_dn = around()
    for device in (
        (lat_up, lon),
        (lat_dn, lon),
        (lat, lon_up),
        (lat, lon_dn),
        (lat_up, lon_up),
        (lat_dn, lon_dn),
    ):
        greet(device)


def halo_kernel(
    grid_ref,
    ids_ref,
    cot_ref,
    table_ref,
    index_ref,
    send_sel,
    gather_sel,
    label_sel,
    bias_ref,
    win_ref,
    stack,
    halo_msg,
    labels,
    tab,
    idx,
    idx_t,
    left,
    halo_s,
    halo_r,
):
    lat, lon, lat_up, lat_dn, lon_up, lon_dn = around()
    greet_halo()
    labels[...] = jnp.zeros_like(labels)
    for r in range(6):
        labels[2 * r : 2 * r + 2, :] = jnp.broadcast_to(ids_ref[r, :, 0:1].astype(F32), (2, 64))
    stack[0, 0:TOK, C:256] = dot(label_sel[...], labels[...].astype(BF16)).astype(BF16)
    stack[1, 0:TOK, C:256] = jnp.zeros((TOK, 64), BF16)
    for r in range(6):
        for q in range(12):
            at = (r * 12 + q) * 2
            stack[0, at : at + 2, 0:C] = grid_ref[r, q]
            stack[1, at : at + 2, 0:C] = cot_ref[r, q]
    for n in range(2):
        halo_msg[n] = dot(send_sel[...], stack[n, 0:TOK, :]).astype(BF16)
    pl.semaphore_wait(pltpu.get_barrier_semaphore(), 6)
    halo_to = ((lat, lon_dn), (lat_dn, lon), (lat_dn, lon_dn))
    halo = [
        pltpu.make_async_remote_copy(
            src_ref=halo_msg.at[:, d * 48 : (d + 1) * 48, :],
            dst_ref=stack.at[:, TOK + d * 48 : TOK + (d + 1) * 48, :],
            send_sem=halo_s.at[d],
            recv_sem=halo_r.at[d],
            device_id=halo_to[d],
            device_id_type=MESH,
        )
        for d in range(3)
    ]
    for copy in halo:
        copy.start()
    look_up_bias(table_ref, index_ref, bias_ref, tab, idx, idx_t, left)
    for copy in halo:
        copy.wait()
    for n in range(2):
        win_ref[n] = dot(gather_sel[...], stack[n]).astype(BF16)


def layer_norm(values, gain_row, shift_row):
    centred = values - jnp.mean(values, -1, keepdims=True)
    inv_std = lax.rsqrt(jnp.mean(centred * centred, -1, keepdims=True) + NORM_EPS)
    normed = centred * inv_std
    return normed * gain_row + shift_row, normed, inv_std


def norm_back(incoming, normed, inv_std, gain_row):
    scaled = incoming * gain_row
    outgoing = inv_std * (
        scaled
        - jnp.mean(scaled, -1, keepdims=True)
        - normed * jnp.mean(scaled * normed, -1, keepdims=True)
    )
    return (
        outgoing,
        jnp.sum(incoming * normed, 0, keepdims=True),
        jnp.sum(incoming, 0, keepdims=True),
    )


def main_kernel(
    win_ref,
    gain_ref,
    shift_ref,
    wqkv_ref,
    bqkv_ref,
    wproj_ref,
    bproj_ref,
    w1_ref,
    b1_ref,
    w2_ref,
    b2_ref,
    bias_ref,
    index_ref,
    send_out_sel,
    place_sel,
    out_ref,
    din_ref,
    full_ref,
    tgrad_ref,
    out_stack,
    out_msg,
    probs,
    act,
    dfac,
    dsc,
    small,
    grads,
    core_in1,
    core_in2,
    plane_in1,
    plane_in2,
    z_out,
    z_in,
    z_all,
    owned,
    t_out,
    t_in,
    oh_s,
    oh_r,
    core_s,
    core_r,
    plane_s,
    plane_r,
    zs,
    zr,
    zgs,
    zgr,
    ts,
    tr,
    tgs,
    tgr,
    ags,
    agr,
    fs,
    fr,
):
    lat, lon, lat_up, lat_dn, lon_up, lon_dn = around()
    core = lat % 2
    pair_lat = lat + 1 - 2 * core
    ylo = lon % 2
    z = lon // 2
    k = (lat // 2) * 2 + ylo

    def plane_device(kk):
        return ((kk // 2) * 2 + core, z * 2 + kk % 2)

    def each(first_d, last_d, body):
        def step(d, carry):
            body(d)
            return carry

        lax.fori_loop(first_d, last_d, step, 0)

    each(1, 32, lambda d: greet((lat, (lon + d) % 32)))
    each(1, 16, lambda d: greet(plane_device((k + d) % 16)))
    greet((pair_lat, lon))
    greet_halo()

    x = win_ref[0, :, 0:C].astype(F32)
    g_b = win_ref[1, :, 0:C]
    label_lane = win_ref[0, :, 128:256]
    pick = (lax.broadcasted_iota(jnp.int32, (8, 128), 1) == 64).astype(F32).astype(BF16)
    ids_row = dot(pick, label_lane, 1, 1)[0:1]
    ids_col = label_lane[:, 64:65].astype(F32)
    allowed = ids_row == ids_col

    gain0, gain1 = gain_ref[0:1, :], gain_ref[1:2, :]
    shift0, shift1 = shift_ref[0:1, :], shift_ref[1:2, :]
    first, hat1, inv1 = layer_norm(x, gain0, shift0)
    first_b = first.astype(BF16)
    bqkv = bqkv_ref[...].reshape(1, 3 * C)
    b1 = b1_ref[...].reshape(1, FF)
    wq = wqkv_ref[:, 0:C]
    wk = wqkv_ref[:, C : 2 * C]
    wv = wqkv_ref[:, 2 * C : 3 * C]
    q = (dot(first_b, wq) + bqkv[:, 0:C]).astype(BF16)
    key = (dot(first_b, wk) + bqkv[:, C : 2 * C]).astype(BF16)
    v = (dot(first_b, wv) + bqkv[:, 2 * C : 3 * C]).astype(BF16)
    lane = lax.broadcasted_iota(jnp.int32, (TOK, C), 1)

    def only(h, values):
        return jnp.where((lane >> 5) == h, values, jnp.zeros_like(values))

    mixed = jnp.zeros((TOK, C), F32)
    for h in range(HEADS):
        s = dot(only(h, q), key, 1, 1) * SCALE + bias_ref[h]
        s = jnp.where(allowed, s, NEG_FILL)
        e = jnp.exp(s - jnp.max(s, -1, keepdims=True))
        p = e * (1.0 / jnp.sum(e, -1, keepdims=True))
        probs[h] = p
        mixed = mixed + dot(p.astype(BF16), only(h, v))
    mixed_b = mixed.astype(BF16)
    attended = x + dot(mixed_b, wproj_ref[...]) + bproj_ref[...].reshape(1, C)

    second, hat2, inv2 = layer_norm(attended, gain1, shift1)
    second_b = second.astype(BF16)
    for b in range(FF // 128):
        cols = slice(b * 128, (b + 1) * 128)
        hidden = dot(second_b, w1_ref[:, cols]) + b1[:, cols]
        cumul = 0.5 * (1.0 + lax.erf(hidden * ROOT_HALF))
        act[:, cols] = (hidden * cumul).astype(BF16)
        dfac[:, cols] = cumul + hidden * jnp.exp(-0.5 * hidden * hidden) * ROOT_TWOPI
    result = (attended + dot(act[...], w2_ref[...], 1, 1) + b2_ref[...].reshape(1, C)).astype(BF16)

    halo_out_to = ((lat, lon_up), (lat_up, lon), (lat_up, lon_up))

    def send_back(n, values):
        out_stack[n, 0:TOK, 0:C] = values
        out_msg[n, :, 0:C] = dot(send_out_sel[...], values).astype(BF16)
        copies = [
            pltpu.make_async_remote_copy(
                src_ref=out_msg.at[n, d * 48 : (d + 1) * 48, :],
                dst_ref=out_stack.at[n, TOK + d * 48 : TOK + (d + 1) * 48, :],
                send_sem=oh_s.at[n, d],
                recv_sem=oh_r.at[n, d],
                device_id=halo_out_to[d],
                device_id_type=MESH,
            )
            for d in range(3)
        ]
        for copy in copies:
            copy.start()
        return copies

    small[...] = jnp.zeros_like(small)

    def keep(row, vector):
        width = vector.shape[1]
        for at in range(0, width, 128):
            n = min(128, width - at)
            small[row + at // 128 : row + at // 128 + 1, 0:n] = vector[:, at : at + n]

    gf = g_b.astype(F32)
    keep(21, jnp.sum(gf, 0, keepdims=True))
    d_second = jnp.zeros((TOK, C), F32)
    for b in range(FF // 128):
        cols = slice(b * 128, (b + 1) * 128)
        grads[FC2_ROW + b * C : FC2_ROW + (b + 1) * C, :] = dot(g_b, act[:, cols], 0, 0).astype(BF16)
        d_hidden = dot(g_b, w2_ref[:, cols]) * dfac[:, cols]
        d_hidden_b = d_hidden.astype(BF16)
        keep(15 + b, jnp.sum(d_hidden, 0, keepdims=True))
        grads[FC1_ROW + b * C : FC1_ROW + (b + 1) * C, :] = dot(second_b, d_hidden_b, 0, 0).astype(BF16)
        d_second = d_second + dot(d_hidden_b, w1_ref[:, cols], 1, 1)

    core_in = (core_in1, core_in2)
    plane_in = (plane_in1, plane_in2)

    def core_copy(n):
        base, rows = CHUNKS[n]
        return pltpu.make_async_remote_copy(
            src_ref=grads.at[pl.ds(pl.multiple_of(base + (1 - core) * 16 * rows, 16), 16 * rows), :],
            dst_ref=core_in[n],
            send_sem=core_s.at[n],
            recv_sem=core_r.at[n],
            device_id=(pair_lat, lon),
            device_id_type=MESH,
        )

    def add_core(n):
        base, rows = CHUNKS[n]
        mine = pl.ds(pl.multiple_of(base + core * 16 * rows, 16), 16 * rows)
        grads[mine, :] = (grads[mine, :].astype(F32) + core_in[n][...].astype(F32)).astype(BF16)

    def plane_copy(n, d):
        base, rows = CHUNKS[n]
        kk = (k + d) % 16
        return pltpu.make_async_remote_copy(
            src_ref=grads.at[pl.ds(pl.multiple_of(base + (core * 16 + kk) * rows, 16), rows), :],
            dst_ref=plane_in[n].at[d],
            send_sem=plane_s.at[n, d],
            recv_sem=plane_r.at[n, d],
            device_id=plane_device(kk),
            device_id_type=MESH,
        )

    def add_plane(n):
        base, rows = CHUNKS[n]
        total = grads[pl.ds(pl.multiple_of(base + (core * 16 + k) * rows, 16), rows), :].astype(F32)
        for d in range(1, 16):
            total = total + plane_in[n][d].astype(F32)
        return total

    pl.semaphore_wait(pltpu.get_barrier_semaphore(), 53)
    core_copy(0).start()
    out_copies = send_back(0, result)

    back2, dgain1, dshift1 = norm_back(d_second, hat2, inv2, gain1)
    keep(2, dgain1)
    keep(6, dshift1)
    d_att = gf + back2
    d_att_b = d_att.astype(BF16)
    core_copy(0).wait()
    add_core(0)
    each(1, 16, lambda d: plane_copy(0, d).start())

    def put_pair(at, left, right):
        grads[at : at + C, :] = left[:, 0:128].astype(BF16)
        grads[at + C : at + 2 * C, :] = right[:, 0:128].astype(BF16)
        grads[at + 2 * C : at + 3 * C, :] = jnp.concatenate([left[:, 128:C], right[:, 128:C]], 1).astype(BF16)

    dw_proj = dot(mixed_b, d_att_b, 0, 0)
    keep(13, jnp.sum(d_att, 0, keepdims=True))
    dm = dot(d_att_b, wproj_ref[...], 1, 1).astype(BF16)

    dq = jnp.zeros((TOK, C), F32)
    dk = jnp.zeros((TOK, C), F32)
    dv = jnp.zeros((TOK, C), F32)
    for h in range(HEADS):
        p = probs[h]
        dm_h = only(h, dm)
        dp = dot(dm_h, v, 1, 1)
        ds = p * (dp - jnp.sum(dp * p, -1, keepdims=True))
        dsc[h, :, 0:128] = ds[:, 0:128]
        dsc[h, :, 128:256] = jnp.concatenate([ds[:, 128:TOK], jnp.zeros((TOK, 112), F32)], 1)
        ds_b = (ds * SCALE).astype(BF16)
        dq = dq + dot(ds_b, only(h, key))
        dk = dk + dot(ds_b, only(h, q), 0, 0)
        dv = dv + dot(p.astype(BF16), dm_h, 0, 0)
    dq_b, dk_b, dv_b = dq.astype(BF16), dk.astype(BF16), dv.astype(BF16)
    put_pair(QP_ROW, dot(first_b, dq_b, 0, 0), dot(first_b, dk_b, 0, 0))
    put_pair(QP_ROW + 3 * C, dot(first_b, dv_b, 0, 0), dw_proj)
    d_bias = jnp.concatenate(
        [jnp.sum(dq, 0, keepdims=True), jnp.sum(dk, 0, keepdims=True), jnp.sum(dv, 0, keepdims=True)], 1
    )
    keep(8, d_bias)
    d_first = dot(dq_b, wq, 1, 1) + dot(dk_b, wk, 1, 1) + dot(dv_b, wv, 1, 1)
    back1, dgain0, dshift0 = norm_back(d_first, hat1, inv1, gain0)
    keep(0, dgain0)
    keep(4, dshift0)
    grads[SMALL_ROW : SMALL_ROW + 32, :] = small[...].astype(BF16)
    grads[SMALL_ROW + 32 : ROWS, :] = jnp.zeros((ROWS - SMALL_ROW - 32, 128), BF16)
    core_copy(1).start()
    din_copies = send_back(1, (d_att + back1).astype(BF16))
    core_copy(1).wait()
    add_core(1)
    each(1, 16, lambda d: plane_copy(1, d).start())

    hi_iota = lax.broadcasted_iota(jnp.int32, (32, 256), 0)
    lo_iota = lax.broadcasted_iota(jnp.int32, (128, 256), 0)

    def factors(flat, rows):
        width = flat.shape[1]
        is_hi = hi_iota[:, 0:width] == (flat >> 7)
        lo_hot = jnp.where(lo_iota[:, 0:width] == (flat & 127), 1.0, 0.0).astype(BF16)
        left = jnp.concatenate([jnp.where(is_hi, row, 0.0).astype(BF16) for row in rows], 0)
        return dot(left, lo_hot, 1, 1)

    def pairs(b, total):
        block = pl.ds(pl.multiple_of(b * 8, 8), 8)
        flat = index_ref[block, 0:128]
        rows = [dsc[h, block, 0:128] for h in range(HEADS)]
        two = lambda values, r: jnp.concatenate([values[r : r + 1], values[r + 1 : r + 2]], 1)
        for r in range(0, 8, 2):
            total = total + factors(two(flat, r), [two(values, r) for values in rows])
        return total

    table = lax.fori_loop(0, TOK // 8, pairs, jnp.zeros((HEADS * 32, 128), F32))
    flat_tail = jnp.concatenate([index_ref[:, 128:TOK].astype(F32), jnp.zeros((TOK, 112), F32)], 1).T[0:16]
    flat_tail = flat_tail.astype(jnp.int32)
    ds_tail = [dsc[h, :, 128:256].T for h in range(HEADS)]
    for r in range(16):
        table = table + factors(flat_tail[r : r + 1], [t[r : r + 1] for t in ds_tail])
    for n in range(32):
        t_out[n] = table[n * 6 : (n + 1) * 6]

    def t_copy(d):
        to = (lon + d) % 32
        return pltpu.make_async_remote_copy(
            src_ref=t_out.at[to],
            dst_ref=t_in.at[d],
            send_sem=ts.at[d],
            recv_sem=tr.at[d],
            device_id=(lat, to),
            device_id_type=MESH,
        )

    each(1, 32, lambda d: t_copy(d).start())

    each(1, 16, lambda d: plane_copy(0, d).wait())
    owned[0:64, :] = add_plane(0)
    each(1, 16, lambda d: plane_copy(1, d).wait())
    owned[64:OWNED, :] = add_plane(1)
    for n in range(16):
        z_out[n] = owned[n * ZROWS : (n + 1) * ZROWS, :]

    def z_copy(d):
        to = (z + d) % 16
        return pltpu.make_async_remote_copy(
            src_ref=z_out.at[to],
            dst_ref=z_in.at[d],
            send_sem=zs.at[d],
            recv_sem=zr.at[d],
            device_id=(lat, to * 2 + ylo),
            device_id_type=MESH,
        )

    def z_gather(d):
        to = (z + d) % 16
        return pltpu.make_async_remote_copy(
            src_ref=z_all.at[z],
            dst_ref=z_all.at[z],
            send_sem=zgs.at[d],
            recv_sem=zgr.at[d],
            device_id=(lat, to * 2 + ylo),
            device_id_type=MESH,
        )

    each(1, 16, lambda d: z_copy(d).start())
    each(1, 16, lambda d: z_copy(d).wait())
    total = z_out[z]
    for d in range(1, 16):
        total = total + z_in[d]
    z_all[z] = total
    each(1, 16, lambda d: z_gather(d).start())

    each(1, 32, lambda d: t_copy(d).wait())
    t_total = t_out[lon]
    for d in range(1, 32):
        t_total = t_total + t_in[d]
    tgrad_ref[lon] = t_total

    def t_gather(d):
        return pltpu.make_async_remote_copy(
            src_ref=tgrad_ref.at[lon],
            dst_ref=tgrad_ref.at[lon],
            send_sem=tgs.at[d],
            recv_sem=tgr.at[d],
            device_id=(lat, (lon + d) % 32),
            device_id_type=MESH,
        )

    each(1, 32, lambda d: t_gather(d).start())

    each(1, 16, lambda d: z_gather(d).wait())
    for n in range(16):
        owned[n * ZROWS : (n + 1) * ZROWS, :] = z_all[n]
    full_ref[core, k] = owned[...].astype(BF16)

    def plane_gather(d):
        return pltpu.make_async_remote_copy(
            src_ref=full_ref.at[core, k],
            dst_ref=full_ref.at[core, k],
            send_sem=ags.at[d],
            recv_sem=agr.at[d],
            device_id=plane_device((k + d) % 16),
            device_id_type=MESH,
        )

    def forward(d):
        kk = (k + 16 - d) % 16
        return pltpu.make_async_remote_copy(
            src_ref=full_ref.at[core, kk],
            dst_ref=full_ref.at[core, kk],
            send_sem=fs.at[d],
            recv_sem=fr.at[d],
            device_id=(pair_lat, lon),
            device_id_type=MESH,
        )

    each(1, 16, lambda d: plane_gather(d).start())
    forward(0).start()

    def pass_on(d):
        plane_gather(d).wait()
        forward(d).start()

    each(1, 16, pass_on)

    for n, copies, ref in ((0, out_copies, out_ref), (1, din_copies, din_ref)):
        for copy in copies:
            copy.wait()
        ref[...] = dot(place_sel[...], out_stack[n, :, 0:C]).astype(BF16)
    each(0, 16, lambda d: forward(d).wait())
    each(1, 32, lambda d: t_gather(d).wait())


def final_kernel(
    out_ref,
    din_ref,
    full_ref,
    tgrad_ref,
    output,
    grid_grad,
    gain_grad,
    shift_grad,
    dwqkv,
    dbqkv,
    dwproj,
    dbproj,
    dw1,
    db1,
    dw2,
    db2,
    dtable,
):
    for r in range(6):
        for q in range(12):
            at = (r * 12 + q) * 2
            output[r, q] = out_ref[at : at + 2, :]
            grid_grad[r, q] = din_ref[at : at + 2, :]

    def rows(start, count):
        parts = []
        at = start
        while at < start + count:
            n = 0 if at < CHUNKS[1][0] else 1
            base, size = CHUNKS[n]
            owner, inside = divmod(at - base, size)
            take = min(size - inside, start + count - at)
            first = inside + (0 if n == 0 else CHUNKS[0][1])
            parts.append(full_ref[owner // 16, owner % 16, first : first + take, :])
            at += take
        return jnp.concatenate(parts, 0).astype(F32) if len(parts) > 1 else parts[0].astype(F32)

    for b in range(FF // 128):
        cols = slice(b * 128, (b + 1) * 128)
        dw2[:, cols] = rows(FC2_ROW + b * C, C)
        dw1[:, cols] = rows(FC1_ROW + b * C, C)
    qa, ka, qk = (rows(QP_ROW + n * C, C) for n in range(3))
    va, pa, vp = (rows(QP_ROW + n * C, C) for n in range(3, 6))
    dwqkv[:, 0:128] = qa
    dwqkv[:, 128:C] = qk[:, 0:64]
    dwqkv[:, C : C + 128] = ka
    dwqkv[:, C + 128 : 2 * C] = qk[:, 64:128]
    dwqkv[:, 2 * C : 2 * C + 128] = va
    dwqkv[:, 2 * C + 128 : 3 * C] = vp[:, 0:64]
    dwproj[:, 0:128] = pa
    dwproj[:, 128:C] = vp[:, 64:128]
    vec = rows(SMALL_ROW, 32)

    def load(row, width, ref, at=0):
        for n in range(0, width, 128):
            m = min(128, width - n)
            ref[at : at + 1, n : n + m] = vec[row + n // 128 : row + n // 128 + 1, 0:m]

    load(0, C, gain_grad, 0)
    load(2, C, gain_grad, 1)
    load(4, C, shift_grad, 0)
    load(6, C, shift_grad, 1)
    for row, ref in ((8, dbqkv), (13, dbproj), (15, db1), (21, db2)):
        width = ref.shape[0]
        for n in range(0, width, 128):
            m = min(128, width - n)
            ref[n : n + m] = vec[row + n // 128, 0:m]
    for h in range(HEADS):
        for t in range(NHI):
            n = h * 32 + t
            m = min(128, NBIAS - t * 128)
            dtable[0, h, :, t * 128 : t * 128 + m] = tgrad_ref[n // 6, n % 6 : n % 6 + 1, 0:m]


def on_device(
    grid,
    region_ids,
    cotangent,
    norm_gain,
    norm_shift,
    qkv_weight,
    qkv_bias,
    proj_weight,
    proj_bias,
    fc1_weight,
    fc1_bias,
    fc2_weight,
    fc2_bias,
    bias_table,
    pair_index,
):
    vmem = pl.BlockSpec(memory_space=pltpu.VMEM)
    shape = jax.ShapeDtypeStruct
    dma = pltpu.SemaphoreType.DMA
    send_sel, gather_sel, label_sel, send_out_sel, place_sel = selectors()
    by_tile = lambda field: field.transpose(1, 2, 0, 3)
    bias, win = pl.pallas_call(
        halo_kernel,
        out_shape=(shape((HEADS, TOK, TOK), F32), shape((2, TOK, 256), BF16)),
        in_specs=[vmem] * 8,
        out_specs=(vmem,) * 2,
        scratch_shapes=[
            pltpu.VMEM((2, 288, 256), BF16),
            pltpu.VMEM((2, 144, 256), BF16),
            pltpu.VMEM((16, 64), F32),
            pltpu.VMEM((8, 3328), F32),
            pltpu.VMEM((TOK, 256), jnp.int32),
            pltpu.VMEM((16, 256), jnp.int32),
            pltpu.VMEM((HEADS, 128, 256), F32),
            dma((3,)),
            dma((3,)),
        ],
        name="halo_and_bias",
        compiler_params=pltpu.CompilerParams(
            collective_id=0, has_side_effects=True, vmem_limit_bytes=32 * 1024 * 1024
        ),
    )(
        by_tile(grid),
        region_ids.transpose(1, 0, 2),
        by_tile(cotangent),
        bias_table.transpose(0, 2, 1, 3),
        pair_index,
        send_sel,
        gather_sel,
        label_sel,
    )
    out, din, full, tgrad = pl.pallas_call(
        main_kernel,
        out_shape=(
            shape((TOK, C), BF16),
            shape((TOK, C), BF16),
            shape((2, 16, OWNED, 128), BF16),
            shape((32, 6, 128), F32),
        ),
        in_specs=[vmem] * 15,
        out_specs=(vmem,) * 4,
        scratch_shapes=[
            pltpu.VMEM((2, 288, 256), BF16),
            pltpu.VMEM((2, 144, 256), BF16),
            pltpu.VMEM((HEADS, TOK, TOK), F32),
            pltpu.VMEM((TOK, FF), BF16),
            pltpu.VMEM((TOK, FF), F32),
            pltpu.VMEM((HEADS, TOK, 256), F32),
            pltpu.VMEM((32, 128), F32),
            pltpu.VMEM((ROWS, 128), BF16),
            pltpu.VMEM((1024, 128), BF16),
            pltpu.VMEM((768, 128), BF16),
            pltpu.VMEM((16, 64, 128), BF16),
            pltpu.VMEM((16, 48, 128), BF16),
            pltpu.VMEM((16, ZROWS, 128), F32),
            pltpu.VMEM((16, ZROWS, 128), F32),
            pltpu.VMEM((16, ZROWS, 128), F32),
            pltpu.VMEM((OWNED, 128), F32),
            pltpu.VMEM((32, 6, 128), F32),
            pltpu.VMEM((32, 6, 128), F32),
            dma((2, 3)),
            dma((2, 3)),
            dma((2,)),
            dma((2,)),
            dma((2, 16)),
            dma((2, 16)),
            dma((16,)),
            dma((16,)),
            dma((16,)),
            dma((16,)),
            dma((32,)),
            dma((32,)),
            dma((32,)),
            dma((32,)),
            dma((16,)),
            dma((16,)),
            dma((16,)),
            dma((16,)),
        ],
        name="window_block",
        compiler_params=pltpu.CompilerParams(
            collective_id=1, has_side_effects=True, vmem_limit_bytes=48 * 1024 * 1024
        ),
    )(
        win,
        norm_gain,
        norm_shift,
        qkv_weight,
        qkv_bias,
        proj_weight,
        proj_bias,
        fc1_weight,
        fc1_bias,
        fc2_weight.T,
        fc2_bias,
        bias,
        pair_index,
        send_out_sel,
        place_sel,
    )
    outs = pl.pallas_call(
        final_kernel,
        out_shape=(
            shape((6, 12, 2, C), BF16),
            shape((6, 12, 2, C), BF16),
            shape((2, C), F32),
            shape((2, C), F32),
            shape((C, 3 * C), F32),
            shape((3 * C,), F32),
            shape((C, C), F32),
            shape((C,), F32),
            shape((C, FF), F32),
            shape((FF,), F32),
            shape((C, FF), F32),
            shape((C,), F32),
            shape((1, HEADS, 1, NBIAS), F32),
        ),
        in_specs=[vmem] * 4,
        out_specs=(vmem,) * 13,
        name="outputs",
        compiler_params=pltpu.CompilerParams(vmem_limit_bytes=32 * 1024 * 1024),
    )(out, din, full, tgrad)
    outs = list(outs)
    for n in (0, 1):
        outs[n] = outs[n].transpose(2, 0, 1, 3)
    outs[10] = outs[10].T
    outs[12] = outs[12].transpose(0, 2, 1, 3)
    return tuple(outs)


def solution(mesh):
    field = P(None, "lat", "lon", None)
    table = P(None, "lat", None, None)
    return jax.shard_map(
        on_device,
        mesh=mesh,
        in_specs=(field, P(None, "lat", "lon"), field) + (P(),) * 10 + (table, P()),
        out_specs=(field, field) + (P(),) * 10 + (table,),
        check_vma=False,
    )
```

```python
import math

import jax
import jax.numpy as jnp
import numpy as np
from jax import lax
from jax.experimental import pallas as pl
from jax.experimental.pallas import tpu as pltpu
from jax.sharding import PartitionSpec as P

F32 = jnp.float32
BF16 = jnp.bfloat16
MESH = pl.DeviceIdType.MESH

C = 192
HEADS = 6
HEAD = 32
FF = 768
TOK = 144
NBIAS = 3312
NHI = 26
NEG_FILL = -1e30
NORM_EPS = 1e-05
ROOT_HALF = 1.0 / math.sqrt(2.0)
ROOT_TWOPI = 1.0 / math.sqrt(2.0 * math.pi)
SCALE = HEAD ** (-0.5)

ROWS = 3584
FC2_ROW = 0
FC1_ROW = 1152
QP_ROW = 2304
SMALL_ROW = 3456
CHUNKS = ((0, 64), (2048, 48))
OWNED = 112
PASSED = 12


def dot(a, b, ca=1, cb=0):
    return lax.dot_general(a, b, (((ca,), (cb,)), ((), ())), preferred_element_type=F32)


def selectors():
    held = lambda l, r, q: (r * 12 + q) * 2 + l
    send = np.zeros((144, 144), np.float32)
    gather = np.zeros((144, 288), np.float32)
    send_out = np.zeros((144, 144), np.float32)
    place = np.zeros((144, 288), np.float32)
    label = np.zeros((144, 16), np.float32)
    for l in range(2):
        for i in range(6):
            for j in range(12):
                label[held(l, i, j), i * 2 + l] = 1
                tok = l * 72 + i * 12 + j
                lev = (l + 1) % 2
                far_i, far_j = i >= 3, j >= 6
                r = i - 3 if far_i else i + 3
                q = j - 6 if far_j else j + 6
                if not far_i and not far_j:
                    gather[tok, held(lev, r, q)] = 1
                    place[held(lev, r, q), tok] = 1
                    continue
                d = 2 if (far_i and far_j) else (1 if far_i else 0)
                m = d * 48 + l * 18 + (i % 3) * 6 + (j % 6)
                send[m, held(lev, r, q)] = 1
                gather[tok, 144 + m] = 1
                send_out[m, tok] = 1
                place[held(lev, r, q), 144 + m] = 1
    return [jnp.asarray(a, BF16) for a in (send, gather, label, send_out, place)]


def look_up_bias(table_ref, index_ref, bias_ref, tab, idx, idx_t, left):
    tab[...] = jnp.zeros_like(tab)
    for h in range(HEADS):
        tab[h : h + 1, 0:NBIAS] = table_ref[0, h]
    idx[...] = jnp.zeros_like(idx)
    idx[:, 0:TOK] = index_ref[...]
    tail = idx[:, 128:256].astype(F32).T
    idx_t[:, 0:TOK] = tail[0:16].astype(jnp.int32)
    idx_t[:, TOK:256] = jnp.zeros((16, 256 - TOK), jnp.int32)
    left[...] = jnp.zeros_like(left)

    def look(flat, store):
        lo = flat & 127
        hi = flat >> 7
        for h in range(HEADS):
            acc = jnp.zeros((8, 128), F32)
            for t in range(NHI):
                row = jnp.broadcast_to(tab[h : h + 1, t * 128 : (t + 1) * 128], (8, 128))
                got = jnp.take_along_axis(row, lo, axis=1, mode="promise_in_bounds")
                acc = jnp.where(hi == t, got, acc)
            store(h, acc)

    def body(b, carry):
        at = pl.multiple_of(b * 8, 8)

        def store(h, acc):
            bias_ref[h, pl.ds(at, 8), 0:128] = acc

        look(idx[pl.ds(at, 8), 0:128], store)
        return carry

    lax.fori_loop(0, TOK // 8, body, 0)
    for a in range(2):
        for t in range(2):

            def store(h, acc, a=a, t=t):
                left[h, a * 8 : a * 8 + 8, t * 128 : (t + 1) * 128] = acc

            look(idx_t[a * 8 : a * 8 + 8, t * 128 : (t + 1) * 128], store)
    for h in range(HEADS):
        bias_ref[h, :, 128:TOK] = left[h].T[0:TOK, 0:16]


def around():
    lat = lax.axis_index("lat")
    lon = lax.axis_index("lon")
    return lat, lon, (lat + 1) % 16, (lat + 15) % 16, (lon + 1) % 32, (lon + 31) % 32


def greet(device):
    pl.semaphore_signal(pltpu.get_barrier_semaphore(), inc=1, device_id=device, device_id_type=MESH)


def greet_halo():
    lat, lon, lat_up, lat_dn, lon_up, lon_dn = around()
    for device in (
        (lat_up, lon),
        (lat_dn, lon),
        (lat, lon_up),
        (lat, lon_dn),
        (lat_up, lon_up),
        (lat_dn, lon_dn),
    ):
        greet(device)


def halo_kernel(*refs):
    grid_hbm, cot_hbm, ids_hbm, send_hbm, label_hbm, table_hbm, index_hbm, gather_hbm = refs[0:8]
    weights_hbm = refs[8 : 8 + PASSED]
    bias_ref, win_ref, index_ref = refs[8 + PASSED : 11 + PASSED]
    weights_ref = refs[11 + PASSED : 11 + 2 * PASSED]
    (
        grid_ref,
        cot_ref,
        ids_ref,
        send_sel,
        label_sel,
        table_ref,
        gather_sel,
        stack,
        halo_msg,
        labels,
        tab,
        idx,
        idx_t,
        left,
        halo_s,
        halo_r,
        load_s,
    ) = refs[11 + 2 * PASSED :]
    loads = [
        pltpu.make_async_copy(src, dst, load_s.at[n])
        for n, (src, dst) in enumerate(
            (
                (grid_hbm, grid_ref),
                (cot_hbm, cot_ref),
                (ids_hbm, ids_ref),
                (send_hbm, send_sel),
                (label_hbm, label_sel),
                (table_hbm, table_ref),
                (index_hbm, index_ref),
                (gather_hbm, gather_sel),
                *zip(weights_hbm, weights_ref),
            )
        )
    ]
    for load in loads[0:8]:
        load.start()
    lat, lon, lat_up, lat_dn, lon_up, lon_dn = around()
    greet_halo()
    for load in loads[8:]:
        load.start()
    for load in loads[0:5]:
        load.wait()
    labels[...] = jnp.zeros_like(labels)
    for r in range(6):
        labels[2 * r : 2 * r + 2, :] = jnp.broadcast_to(ids_ref[r, :, 0:1].astype(F32), (2, 64))
    stack[0, 0:TOK, C:256] = dot(label_sel[...], labels[...].astype(BF16)).astype(BF16)
    stack[1, 0:TOK, C:256] = jnp.zeros((TOK, 64), BF16)
    for r in range(6):
        for q in range(12):
            at = (r * 12 + q) * 2
            stack[0, at : at + 2, 0:C] = grid_ref[r, q]
            stack[1, at : at + 2, 0:C] = cot_ref[r, q]
    for n in range(2):
        halo_msg[n] = dot(send_sel[...], stack[n, 0:TOK, :]).astype(BF16)
    pl.semaphore_wait(pltpu.get_barrier_semaphore(), 6)
    halo_to = ((lat, lon_dn), (lat_dn, lon), (lat_dn, lon_dn))
    halo = [
        pltpu.make_async_remote_copy(
            src_ref=halo_msg.at[:, d * 48 : (d + 1) * 48, :],
            dst_ref=stack.at[:, TOK + d * 48 : TOK + (d + 1) * 48, :],
            send_sem=halo_s.at[d],
            recv_sem=halo_r.at[d],
            device_id=halo_to[d],
            device_id_type=MESH,
        )
        for d in range(3)
    ]
    for copy in halo:
        copy.start()
    for load in loads[5:8]:
        load.wait()
    look_up_bias(table_ref, index_ref, bias_ref, tab, idx, idx_t, left)
    for load in loads[8:]:
        load.wait()
    for copy in halo:
        copy.wait()
    for n in range(2):
        win_ref[n] = dot(gather_sel[...], stack[n]).astype(BF16)


def layer_norm(values, gain_row, shift_row):
    centred = values - jnp.mean(values, -1, keepdims=True)
    inv_std = lax.rsqrt(jnp.mean(centred * centred, -1, keepdims=True) + NORM_EPS)
    normed = centred * inv_std
    return normed * gain_row + shift_row, normed, inv_std


def norm_back(incoming, normed, inv_std, gain_row):
    scaled = incoming * gain_row
    outgoing = inv_std * (
        scaled
        - jnp.mean(scaled, -1, keepdims=True)
        - normed * jnp.mean(scaled * normed, -1, keepdims=True)
    )
    return (
        outgoing,
        jnp.sum(incoming * normed, 0, keepdims=True),
        jnp.sum(incoming, 0, keepdims=True),
    )


def main_kernel(
    win_ref,
    gain_ref,
    shift_ref,
    wqkv_ref,
    bqkv_ref,
    wproj_ref,
    bproj_ref,
    w1_ref,
    b1_ref,
    w2_ref,
    b2_ref,
    bias_ref,
    index_ref,
    send_out_sel,
    place_sel,
    out_ref,
    din_ref,
    full_ref,
    tgrad_ref,
    out_stack,
    out_msg,
    probs,
    act,
    dfac,
    dsc,
    small,
    grads,
    core_in1,
    core_in2,
    plane_in1,
    plane_in2,
    z_out,
    z_in,
    z_all,
    owned,
    t_out,
    t_in,
    oh_s,
    oh_r,
    core_s,
    core_r,
    plane_s,
    plane_r,
    zs,
    zr,
    zgs,
    zgr,
    ts,
    tr,
    tgs,
    tgr,
    ags,
    agr,
    fs,
    fr,
):
    lat, lon, lat_up, lat_dn, lon_up, lon_dn = around()
    core = lat % 2
    pair_lat = lat + 1 - 2 * core
    ylo = lon % 2
    z = lon // 2
    k = (lat // 2) * 2 + ylo

    def plane_device(kk):
        return ((kk // 2) * 2 + core, z * 2 + kk % 2)

    def each(first_d, last_d, body):
        def step(d, carry):
            body(d)
            return carry

        lax.fori_loop(first_d, last_d, step, 0)

    each(1, 32, lambda d: greet((lat, (lon + d) % 32)))
    each(1, 16, lambda d: greet(plane_device((k + d) % 16)))
    greet((pair_lat, lon))
    greet_halo()

    x = win_ref[0, :, 0:C].astype(F32)
    g_b = win_ref[1, :, 0:C]
    label_lane = win_ref[0, :, 128:256]
    pick = (lax.broadcasted_iota(jnp.int32, (8, 128), 1) == 64).astype(F32).astype(BF16)
    ids_row = dot(pick, label_lane, 1, 1)[0:1]
    ids_col = label_lane[:, 64:65].astype(F32)
    allowed = ids_row == ids_col

    gain0, gain1 = gain_ref[0:1, :], gain_ref[1:2, :]
    shift0, shift1 = shift_ref[0:1, :], shift_ref[1:2, :]
    first, hat1, inv1 = layer_norm(x, gain0, shift0)
    first_b = first.astype(BF16)
    bqkv = bqkv_ref[...].reshape(1, 3 * C)
    b1 = b1_ref[...].reshape(1, FF)
    wq = wqkv_ref[:, 0:C]
    wk = wqkv_ref[:, C : 2 * C]
    wv = wqkv_ref[:, 2 * C : 3 * C]
    q = (dot(first_b, wq) + bqkv[:, 0:C]).astype(BF16)
    key = (dot(first_b, wk) + bqkv[:, C : 2 * C]).astype(BF16)
    v = (dot(first_b, wv) + bqkv[:, 2 * C : 3 * C]).astype(BF16)
    lane = lax.broadcasted_iota(jnp.int32, (TOK, C), 1)

    def only(h, values):
        return jnp.where((lane >> 5) == h, values, jnp.zeros_like(values))

    mixed = jnp.zeros((TOK, C), F32)
    for h in range(HEADS):
        s = dot(only(h, q), key, 1, 1) * SCALE + bias_ref[h]
        s = jnp.where(allowed, s, NEG_FILL)
        e = jnp.exp(s - jnp.max(s, -1, keepdims=True))
        p = e * (1.0 / jnp.sum(e, -1, keepdims=True))
        probs[h] = p
        mixed = mixed + dot(p.astype(BF16), only(h, v))
    mixed_b = mixed.astype(BF16)
    attended = x + dot(mixed_b, wproj_ref[...]) + bproj_ref[...].reshape(1, C)

    second, hat2, inv2 = layer_norm(attended, gain1, shift1)
    second_b = second.astype(BF16)
    for b in range(FF // 128):
        cols = slice(b * 128, (b + 1) * 128)
        hidden = dot(second_b, w1_ref[:, cols]) + b1[:, cols]
        cumul = 0.5 * (1.0 + lax.erf(hidden * ROOT_HALF))
        act[:, cols] = (hidden * cumul).astype(BF16)
        dfac[:, cols] = cumul + hidden * jnp.exp(-0.5 * hidden * hidden) * ROOT_TWOPI
    result = (attended + dot(act[...], w2_ref[...], 1, 1) + b2_ref[...].reshape(1, C)).astype(BF16)

    halo_out_to = ((lat, lon_up), (lat_up, lon), (lat_up, lon_up))

    def send_back(n, values):
        out_stack[n, 0:TOK, 0:C] = values
        out_msg[n, :, 0:C] = dot(send_out_sel[...], values).astype(BF16)
        copies = [
            pltpu.make_async_remote_copy(
                src_ref=out_msg.at[n, d * 48 : (d + 1) * 48, :],
                dst_ref=out_stack.at[n, TOK + d * 48 : TOK + (d + 1) * 48, :],
                send_sem=oh_s.at[n, d],
                recv_sem=oh_r.at[n, d],
                device_id=halo_out_to[d],
                device_id_type=MESH,
            )
            for d in range(3)
        ]
        for copy in copies:
            copy.start()
        return copies

    small[...] = jnp.zeros_like(small)

    def keep(row, vector):
        width = vector.shape[1]
        for at in range(0, width, 128):
            n = min(128, width - at)
            small[row + at // 128 : row + at // 128 + 1, 0:n] = vector[:, at : at + n]

    gf = g_b.astype(F32)
    keep(21, jnp.sum(gf, 0, keepdims=True))
    d_second = jnp.zeros((TOK, C), F32)
    for b in range(FF // 128):
        cols = slice(b * 128, (b + 1) * 128)
        grads[FC2_ROW + b * C : FC2_ROW + (b + 1) * C, :] = dot(g_b, act[:, cols], 0, 0).astype(BF16)
        d_hidden = dot(g_b, w2_ref[:, cols]) * dfac[:, cols]
        d_hidden_b = d_hidden.astype(BF16)
        keep(15 + b, jnp.sum(d_hidden, 0, keepdims=True))
        grads[FC1_ROW + b * C : FC1_ROW + (b + 1) * C, :] = dot(second_b, d_hidden_b, 0, 0).astype(BF16)
        d_second = d_second + dot(d_hidden_b, w1_ref[:, cols], 1, 1)

    z_out[...] = jnp.zeros_like(z_out)
    core_in = (core_in1, core_in2)
    plane_in = (plane_in1, plane_in2)

    def core_copy(n):
        base, rows = CHUNKS[n]
        return pltpu.make_async_remote_copy(
            src_ref=grads.at[pl.ds(pl.multiple_of(base + (1 - core) * 16 * rows, 16), 16 * rows), :],
            dst_ref=core_in[n],
            send_sem=core_s.at[n],
            recv_sem=core_r.at[n],
            device_id=(pair_lat, lon),
            device_id_type=MESH,
        )

    def plane_copy(n, d):
        base, rows = CHUNKS[n]
        kk = (k + d) % 16
        return pltpu.make_async_remote_copy(
            src_ref=grads.at[pl.ds(pl.multiple_of(base + (core * 16 + kk) * rows, 16), rows), :],
            dst_ref=plane_in[n].at[d],
            send_sem=plane_s.at[n, d],
            recv_sem=plane_r.at[n, d],
            device_id=plane_device(kk),
            device_id_type=MESH,
        )

    def z_copy(n, d):
        to = (z + d) % 16
        return pltpu.make_async_remote_copy(
            src_ref=z_out.at[n, to],
            dst_ref=z_in.at[n, d],
            send_sem=zs.at[n, d],
            recv_sem=zr.at[n, d],
            device_id=(lat, to * 2 + ylo),
            device_id_type=MESH,
        )

    def z_gather(n, d):
        to = (z + d) % 16
        return pltpu.make_async_remote_copy(
            src_ref=z_all.at[n, z],
            dst_ref=z_all.at[n, z],
            send_sem=zgs.at[n, d],
            recv_sem=zgr.at[n, d],
            device_id=(lat, to * 2 + ylo),
            device_id_type=MESH,
        )

    def owner_rows(n):
        return slice(0, 64) if n == 0 else slice(64, OWNED)

    def plane_gather(n, d):
        return pltpu.make_async_remote_copy(
            src_ref=full_ref.at[core, k, owner_rows(n)],
            dst_ref=full_ref.at[core, k, owner_rows(n)],
            send_sem=ags.at[n, d],
            recv_sem=agr.at[n, d],
            device_id=plane_device((k + d) % 16),
            device_id_type=MESH,
        )

    def forward(n, d):
        kk = (k + 16 - d) % 16
        return pltpu.make_async_remote_copy(
            src_ref=full_ref.at[core, kk, owner_rows(n)],
            dst_ref=full_ref.at[core, kk, owner_rows(n)],
            send_sem=fs.at[n, d],
            recv_sem=fr.at[n, d],
            device_id=(pair_lat, lon),
            device_id_type=MESH,
        )

    def scatter_plane(n):
        base, rows = CHUNKS[n]
        core_copy(n).wait()
        mine = pl.ds(pl.multiple_of(base + core * 16 * rows, 16), 16 * rows)
        grads[mine, :] = (grads[mine, :].astype(F32) + core_in[n][...].astype(F32)).astype(BF16)
        each(1, 16, lambda d: plane_copy(n, d).start())

    def scatter_z(n):
        base, rows = CHUNKS[n]
        per = rows // 16
        each(1, 16, lambda d: plane_copy(n, d).wait())
        total = grads[pl.ds(pl.multiple_of(base + (core * 16 + k) * rows, 16), rows), :].astype(F32)
        for d in range(1, 16):
            total = total + plane_in[n][d].astype(F32)
        for m in range(16):
            z_out[n, m, 0:per] = total[m * per : (m + 1) * per]
        each(1, 16, lambda d: z_copy(n, d).start())

    def gather_z(n):
        each(1, 16, lambda d: z_copy(n, d).wait())
        total = z_out[n, z]
        for d in range(1, 16):
            total = total + z_in[n, d]
        z_all[n, z] = total
        each(1, 16, lambda d: z_gather(n, d).start())

    def gather_plane(n):
        per = CHUNKS[n][1] // 16
        each(1, 16, lambda d: z_gather(n, d).wait())
        for m in range(16):
            owned[m * per : (m + 1) * per, :] = z_all[n, m, 0:per]
        full_ref[core, k, owner_rows(n)] = owned[0 : CHUNKS[n][1], :].astype(BF16)
        each(1, 16, lambda d: plane_gather(n, d).start())
        forward(n, 0).start()

    def pass_on(n):
        def step(d):
            plane_gather(n, d).wait()
            forward(n, d).start()

        each(1, 16, step)

    pl.semaphore_wait(pltpu.get_barrier_semaphore(), 53)
    core_copy(0).start()
    out_copies = send_back(0, result)

    back2, dgain1, dshift1 = norm_back(d_second, hat2, inv2, gain1)
    keep(2, dgain1)
    keep(6, dshift1)
    d_att = gf + back2
    d_att_b = d_att.astype(BF16)
    scatter_plane(0)

    def put_pair(at, left, right):
        grads[at : at + C, :] = left[:, 0:128].astype(BF16)
        grads[at + C : at + 2 * C, :] = right[:, 0:128].astype(BF16)
        grads[at + 2 * C : at + 3 * C, :] = jnp.concatenate([left[:, 128:C], right[:, 128:C]], 1).astype(BF16)

    dw_proj = dot(mixed_b, d_att_b, 0, 0)
    keep(13, jnp.sum(d_att, 0, keepdims=True))
    dm = dot(d_att_b, wproj_ref[...], 1, 1).astype(BF16)

    dq = jnp.zeros((TOK, C), F32)
    dk = jnp.zeros((TOK, C), F32)
    dv = jnp.zeros((TOK, C), F32)
    for h in range(HEADS):
        p = probs[h]
        dm_h = only(h, dm)
        dp = dot(dm_h, v, 1, 1)
        ds = p * (dp - jnp.sum(dp * p, -1, keepdims=True))
        dsc[h, :, 0:128] = ds[:, 0:128]
        dsc[h, :, 128:256] = jnp.concatenate([ds[:, 128:TOK], jnp.zeros((TOK, 112), F32)], 1)
        ds_b = (ds * SCALE).astype(BF16)
        dq = dq + dot(ds_b, only(h, key))
        dk = dk + dot(ds_b, only(h, q), 0, 0)
        dv = dv + dot(p.astype(BF16), dm_h, 0, 0)
    dq_b, dk_b, dv_b = dq.astype(BF16), dk.astype(BF16), dv.astype(BF16)
    put_pair(QP_ROW, dot(first_b, dq_b, 0, 0), dot(first_b, dk_b, 0, 0))
    put_pair(QP_ROW + 3 * C, dot(first_b, dv_b, 0, 0), dw_proj)
    d_bias = jnp.concatenate(
        [jnp.sum(dq, 0, keepdims=True), jnp.sum(dk, 0, keepdims=True), jnp.sum(dv, 0, keepdims=True)], 1
    )
    keep(8, d_bias)
    d_first = dot(dq_b, wq, 1, 1) + dot(dk_b, wk, 1, 1) + dot(dv_b, wv, 1, 1)
    back1, dgain0, dshift0 = norm_back(d_first, hat1, inv1, gain0)
    keep(0, dgain0)
    keep(4, dshift0)
    grads[SMALL_ROW : SMALL_ROW + 32, :] = small[...].astype(BF16)
    grads[SMALL_ROW + 32 : ROWS, :] = jnp.zeros((ROWS - SMALL_ROW - 32, 128), BF16)
    core_copy(1).start()
    din_copies = send_back(1, (d_att + back1).astype(BF16))
    scatter_plane(1)
    scatter_z(0)

    hi_iota = lax.broadcasted_iota(jnp.int32, (32, 256), 0)
    lo_iota = lax.broadcasted_iota(jnp.int32, (128, 256), 0)

    def factors(flat, rows):
        width = flat.shape[1]
        is_hi = hi_iota[:, 0:width] == (flat >> 7)
        lo_hot = jnp.where(lo_iota[:, 0:width] == (flat & 127), 1.0, 0.0).astype(BF16)
        left = jnp.concatenate([jnp.where(is_hi, row, 0.0).astype(BF16) for row in rows], 0)
        return dot(left, lo_hot, 1, 1)

    def pairs(b, total):
        block = pl.ds(pl.multiple_of(b * 8, 8), 8)
        flat = index_ref[block, 0:128]
        rows = [dsc[h, block, 0:128] for h in range(HEADS)]
        two = lambda values, r: jnp.concatenate([values[r : r + 1], values[r + 1 : r + 2]], 1)
        for r in range(0, 8, 2):
            total = total + factors(two(flat, r), [two(values, r) for values in rows])
        return total

    table = lax.fori_loop(0, 12, pairs, jnp.zeros((HEADS * 32, 128), F32))
    scatter_z(1)
    table = lax.fori_loop(12, TOK // 8, pairs, table)
    flat_tail = jnp.concatenate([index_ref[:, 128:TOK].astype(F32), jnp.zeros((TOK, 112), F32)], 1).T[0:16]
    flat_tail = flat_tail.astype(jnp.int32)
    ds_tail = [dsc[h, :, 128:256].T for h in range(HEADS)]
    for r in range(16):
        table = table + factors(flat_tail[r : r + 1], [t[r : r + 1] for t in ds_tail])
    for n in range(32):
        t_out[n] = table[n * 6 : (n + 1) * 6]

    def t_copy(d):
        to = (lon + d) % 32
        return pltpu.make_async_remote_copy(
            src_ref=t_out.at[to],
            dst_ref=t_in.at[d],
            send_sem=ts.at[d],
            recv_sem=tr.at[d],
            device_id=(lat, to),
            device_id_type=MESH,
        )

    def t_gather(d):
        return pltpu.make_async_remote_copy(
            src_ref=tgrad_ref.at[lon],
            dst_ref=tgrad_ref.at[lon],
            send_sem=tgs.at[d],
            recv_sem=tgr.at[d],
            device_id=(lat, (lon + d) % 32),
            device_id_type=MESH,
        )

    each(1, 32, lambda d: t_copy(d).start())
    gather_z(0)
    gather_z(1)
    each(1, 32, lambda d: t_copy(d).wait())
    t_total = t_out[lon]
    for d in range(1, 32):
        t_total = t_total + t_in[d]
    tgrad_ref[lon] = t_total
    each(1, 32, lambda d: t_gather(d).start())
    gather_plane(0)
    gather_plane(1)
    for n, copies, ref in ((0, out_copies, out_ref), (1, din_copies, din_ref)):
        for copy in copies:
            copy.wait()
        ref[...] = dot(place_sel[...], out_stack[n, :, 0:C]).astype(BF16)
    pass_on(0)
    pass_on(1)
    each(1, 32, lambda d: t_gather(d).wait())
    for n in range(2):
        each(0, 16, lambda d: forward(n, d).wait())


def final_kernel(
    out_ref,
    din_ref,
    full_ref,
    tgrad_ref,
    output,
    grid_grad,
    gain_grad,
    shift_grad,
    dwqkv,
    dbqkv,
    dwproj,
    dbproj,
    dw1,
    db1,
    dw2,
    db2,
    dtable,
):
    for r in range(6):
        for q in range(12):
            at = (r * 12 + q) * 2
            output[r, q] = out_ref[at : at + 2, :]
            grid_grad[r, q] = din_ref[at : at + 2, :]

    def rows(start, count):
        parts = []
        at = start
        while at < start + count:
            n = 0 if at < CHUNKS[1][0] else 1
            base, size = CHUNKS[n]
            owner, inside = divmod(at - base, size)
            take = min(size - inside, start + count - at)
            first = inside + (0 if n == 0 else CHUNKS[0][1])
            parts.append(full_ref[owner // 16, owner % 16, first : first + take, :])
            at += take
        return jnp.concatenate(parts, 0).astype(F32) if len(parts) > 1 else parts[0].astype(F32)

    for b in range(FF // 128):
        cols = slice(b * 128, (b + 1) * 128)
        dw2[:, cols] = rows(FC2_ROW + b * C, C)
        dw1[:, cols] = rows(FC1_ROW + b * C, C)
    qa, ka, qk = (rows(QP_ROW + n * C, C) for n in range(3))
    va, pa, vp = (rows(QP_ROW + n * C, C) for n in range(3, 6))
    dwqkv[:, 0:128] = qa
    dwqkv[:, 128:C] = qk[:, 0:64]
    dwqkv[:, C : C + 128] = ka
    dwqkv[:, C + 128 : 2 * C] = qk[:, 64:128]
    dwqkv[:, 2 * C : 2 * C + 128] = va
    dwqkv[:, 2 * C + 128 : 3 * C] = vp[:, 0:64]
    dwproj[:, 0:128] = pa
    dwproj[:, 128:C] = vp[:, 64:128]
    vec = rows(SMALL_ROW, 32)

    def load(row, width, ref, at=0):
        for n in range(0, width, 128):
            m = min(128, width - n)
            ref[at : at + 1, n : n + m] = vec[row + n // 128 : row + n // 128 + 1, 0:m]

    load(0, C, gain_grad, 0)
    load(2, C, gain_grad, 1)
    load(4, C, shift_grad, 0)
    load(6, C, shift_grad, 1)
    for row, ref in ((8, dbqkv), (13, dbproj), (15, db1), (21, db2)):
        width = ref.shape[0]
        for n in range(0, width, 128):
            m = min(128, width - n)
            ref[n : n + m] = vec[row + n // 128, 0:m]
    for h in range(HEADS):
        for t in range(NHI):
            n = h * 32 + t
            m = min(128, NBIAS - t * 128)
            dtable[0, h, :, t * 128 : t * 128 + m] = tgrad_ref[n // 6, n % 6 : n % 6 + 1, 0:m]


def on_device(
    grid,
    region_ids,
    cotangent,
    norm_gain,
    norm_shift,
    qkv_weight,
    qkv_bias,
    proj_weight,
    proj_bias,
    fc1_weight,
    fc1_bias,
    fc2_weight,
    fc2_bias,
    bias_table,
    pair_index,
):
    vmem = pl.BlockSpec(memory_space=pltpu.VMEM)
    shape = jax.ShapeDtypeStruct
    dma = pltpu.SemaphoreType.DMA
    hbm = pl.BlockSpec(memory_space=pltpu.HBM)
    send_sel, gather_sel, label_sel, send_out_sel, place_sel = selectors()
    by_tile = lambda field: field.transpose(1, 2, 0, 3)
    fields = (by_tile(grid), by_tile(cotangent), region_ids.transpose(1, 0, 2))
    table = bias_table.transpose(0, 2, 1, 3)
    passed = (
        norm_gain,
        norm_shift,
        qkv_weight,
        qkv_bias,
        proj_weight,
        proj_bias,
        fc1_weight,
        fc1_bias,
        fc2_weight.T,
        fc2_bias,
        send_out_sel,
        place_sel,
    )
    held = lambda a: pltpu.VMEM(a.shape, a.dtype)
    bias, win, index, *passed = pl.pallas_call(
        halo_kernel,
        out_shape=(
            shape((HEADS, TOK, TOK), F32),
            shape((2, TOK, 256), BF16),
            shape((TOK, TOK), jnp.int32),
            *(shape(a.shape, a.dtype) for a in passed),
        ),
        in_specs=[hbm] * (8 + PASSED),
        out_specs=(vmem,) * (3 + PASSED),
        scratch_shapes=[
            *map(held, fields),
            held(send_sel),
            held(label_sel),
            held(table),
            held(gather_sel),
            pltpu.VMEM((2, 288, 256), BF16),
            pltpu.VMEM((2, 144, 256), BF16),
            pltpu.VMEM((16, 64), F32),
            pltpu.VMEM((8, 3328), F32),
            pltpu.VMEM((TOK, 256), jnp.int32),
            pltpu.VMEM((16, 256), jnp.int32),
            pltpu.VMEM((HEADS, 128, 256), F32),
            dma((3,)),
            dma((3,)),
            dma((8 + PASSED,)),
        ],
        name="halo_and_bias",
        compiler_params=pltpu.CompilerParams(
            collective_id=0, has_side_effects=True, vmem_limit_bytes=32 * 1024 * 1024
        ),
    )(
        *(
            pltpu.with_memory_space_constraint(a, pltpu.HBM)
            for a in (*fields, send_sel, label_sel, table, pair_index, gather_sel, *passed)
        )
    )
    out, din, full, tgrad = pl.pallas_call(
        main_kernel,
        out_shape=(
            shape((TOK, C), BF16),
            shape((TOK, C), BF16),
            shape((2, 16, OWNED, 128), BF16),
            shape((32, 6, 128), F32),
        ),
        in_specs=[vmem] * 15,
        out_specs=(vmem,) * 4,
        scratch_shapes=[
            pltpu.VMEM((2, 288, 256), BF16),
            pltpu.VMEM((2, 144, 256), BF16),
            pltpu.VMEM((HEADS, TOK, TOK), F32),
            pltpu.VMEM((TOK, FF), BF16),
            pltpu.VMEM((TOK, FF), F32),
            pltpu.VMEM((HEADS, TOK, 256), F32),
            pltpu.VMEM((32, 128), F32),
            pltpu.VMEM((ROWS, 128), BF16),
            pltpu.VMEM((1024, 128), BF16),
            pltpu.VMEM((768, 128), BF16),
            pltpu.VMEM((16, 64, 128), BF16),
            pltpu.VMEM((16, 48, 128), BF16),
            pltpu.VMEM((2, 16, 4, 128), F32),
            pltpu.VMEM((2, 16, 4, 128), F32),
            pltpu.VMEM((2, 16, 4, 128), F32),
            pltpu.VMEM((64, 128), F32),
            pltpu.VMEM((32, 6, 128), F32),
            pltpu.VMEM((32, 6, 128), F32),
            dma((2, 3)),
            dma((2, 3)),
            dma((2,)),
            dma((2,)),
            dma((2, 16)),
            dma((2, 16)),
            dma((2, 16)),
            dma((2, 16)),
            dma((2, 16)),
            dma((2, 16)),
            dma((32,)),
            dma((32,)),
            dma((32,)),
            dma((32,)),
            dma((2, 16)),
            dma((2, 16)),
            dma((2, 16)),
            dma((2, 16)),
        ],
        name="window_block",
        compiler_params=pltpu.CompilerParams(
            collective_id=1, has_side_effects=True, vmem_limit_bytes=48 * 1024 * 1024
        ),
    )(
        win,
        *passed[0:10],
        bias,
        index,
        *passed[10:],
    )
    outs = pl.pallas_call(
        final_kernel,
        out_shape=(
            shape((6, 12, 2, C), BF16),
            shape((6, 12, 2, C), BF16),
            shape((2, C), F32),
            shape((2, C), F32),
            shape((C, 3 * C), F32),
            shape((3 * C,), F32),
            shape((C, C), F32),
            shape((C,), F32),
            shape((C, FF), F32),
            shape((FF,), F32),
            shape((C, FF), F32),
            shape((C,), F32),
            shape((1, HEADS, 1, NBIAS), F32),
        ),
        in_specs=[vmem] * 4,
        out_specs=(vmem,) * 13,
        name="outputs",
        compiler_params=pltpu.CompilerParams(vmem_limit_bytes=32 * 1024 * 1024),
    )(out, din, full, tgrad)
    outs = list(outs)
    for n in (0, 1):
        outs[n] = outs[n].transpose(2, 0, 1, 3)
    outs[10] = outs[10].T
    outs[12] = outs[12].transpose(0, 2, 1, 3)
    return tuple(outs)


def solution(mesh):
    field = P(None, "lat", "lon", None)
    table = P(None, "lat", None, None)
    return jax.shard_map(
        on_device,
        mesh=mesh,
        in_specs=(field, P(None, "lat", "lon"), field) + (P(),) * 10 + (table, P()),
        out_specs=(field, field) + (P(),) * 10 + (table,),
        check_vma=False,
    )
```

```python
import math

import jax
import jax.numpy as jnp
import numpy as np
from jax import lax
from jax.experimental import pallas as pl
from jax.experimental.pallas import tpu as pltpu
from jax.sharding import PartitionSpec as P

F32 = jnp.float32
BF16 = jnp.bfloat16
MESH = pl.DeviceIdType.MESH

C = 192
HEADS = 6
HEAD = 32
FF = 768
TOK = 144
NBIAS = 3312
NHI = 26
NEG_FILL = -1e30
NORM_EPS = 1e-05
ROOT_HALF = 1.0 / math.sqrt(2.0)
ROOT_TWOPI = 1.0 / math.sqrt(2.0 * math.pi)
SCALE = HEAD ** (-0.5)

ROWS = 3584
FC2_ROW = 0
FC1_ROW = 1152
QP_ROW = 2304
SMALL_ROW = 3456
CHUNKS = ((0, 64), (2048, 48))
OWNED = 112
STEPS = (
    ((1, 0), (3, 0), (0, 1), (0, 3))
    + ((1, 1), (1, 3), (3, 1), (3, 3), (2, 0), (0, 2))
    + ((2, 1), (2, 3), (1, 2), (3, 2), (2, 2))
)
PASSED = 12


def dot(a, b, ca=1, cb=0):
    return lax.dot_general(a, b, (((ca,), (cb,)), ((), ())), preferred_element_type=F32)


def selectors():
    held = lambda l, r, q: (r * 12 + q) * 2 + l
    send = np.zeros((144, 144), np.float32)
    gather = np.zeros((144, 288), np.float32)
    send_out = np.zeros((144, 144), np.float32)
    place = np.zeros((144, 288), np.float32)
    label = np.zeros((144, 16), np.float32)
    for l in range(2):
        for i in range(6):
            for j in range(12):
                label[held(l, i, j), i * 2 + l] = 1
                tok = l * 72 + i * 12 + j
                lev = (l + 1) % 2
                far_i, far_j = i >= 3, j >= 6
                r = i - 3 if far_i else i + 3
                q = j - 6 if far_j else j + 6
                if not far_i and not far_j:
                    gather[tok, held(lev, r, q)] = 1
                    place[held(lev, r, q), tok] = 1
                    continue
                d = 2 if (far_i and far_j) else (1 if far_i else 0)
                m = d * 48 + l * 18 + (i % 3) * 6 + (j % 6)
                send[m, held(lev, r, q)] = 1
                gather[tok, 144 + m] = 1
                send_out[m, tok] = 1
                place[held(lev, r, q), 144 + m] = 1
    return [jnp.asarray(a, BF16) for a in (send, gather, label, send_out, place)]


def look_up_bias(table_ref, index_ref, bias_ref, tab, idx, idx_t, left):
    for h in range(HEADS):
        for t in range(NHI):
            n = min(128, NBIAS - t * 128)
            row = table_ref[0, h, :, t * 128 : t * 128 + n]
            if n < 128:
                row = jnp.concatenate([row, jnp.zeros((1, 128 - n), F32)], 1)
            tab[t, h] = jnp.broadcast_to(row, (8, 128))
    idx[...] = jnp.zeros_like(idx)
    idx[:, 0:TOK] = index_ref[...]
    tail = idx[:, 128:256].astype(F32).T
    idx_t[:, 0:TOK] = tail[0:16].astype(jnp.int32)
    idx_t[:, TOK:256] = jnp.zeros((16, 256 - TOK), jnp.int32)
    left[...] = jnp.zeros_like(left)

    def look(flat, store):
        lo = flat & 127
        hi = flat >> 7
        acc = [jnp.zeros((8, 128), F32)] * HEADS
        for t in range(NHI):
            here = hi == t
            for h in range(HEADS):
                got = jnp.take_along_axis(tab[t, h], lo, axis=1, mode="promise_in_bounds")
                acc[h] = jnp.where(here, got, acc[h])
        for h in range(HEADS):
            store(h, acc[h])

    def body(b, carry):
        at = pl.multiple_of(b * 8, 8)

        def store(h, acc):
            bias_ref[h, pl.ds(at, 8), 0:128] = acc

        look(idx[pl.ds(at, 8), 0:128], store)
        return carry

    lax.fori_loop(0, TOK // 8, body, 0)
    for a in range(2):
        for t in range(2):

            def store(h, acc, a=a, t=t):
                left[h, a * 8 : a * 8 + 8, t * 128 : (t + 1) * 128] = acc

            look(idx_t[a * 8 : a * 8 + 8, t * 128 : (t + 1) * 128], store)
    for h in range(HEADS):
        bias_ref[h, :, 128:TOK] = left[h].T[0:TOK, 0:16]


def around():
    lat = lax.axis_index("lat")
    lon = lax.axis_index("lon")
    return lat, lon, (lat + 1) % 16, (lat + 15) % 16, (lon + 1) % 32, (lon + 31) % 32


def greet(device):
    pl.semaphore_signal(pltpu.get_barrier_semaphore(), inc=1, device_id=device, device_id_type=MESH)


def greet_halo():
    lat, lon, lat_up, lat_dn, lon_up, lon_dn = around()
    for device in (
        (lat_up, lon),
        (lat_dn, lon),
        (lat, lon_up),
        (lat, lon_dn),
        (lat_up, lon_up),
        (lat_dn, lon_dn),
    ):
        greet(device)


def halo_kernel(*refs):
    grid_hbm, cot_hbm, ids_hbm, send_hbm, label_hbm, table_hbm, index_hbm, gather_hbm = refs[0:8]
    weights_hbm = refs[8 : 8 + PASSED]
    bias_ref, win_ref, index_ref = refs[8 + PASSED : 11 + PASSED]
    weights_ref = refs[11 + PASSED : 11 + 2 * PASSED]
    (
        grid_ref,
        cot_ref,
        ids_ref,
        send_sel,
        label_sel,
        table_ref,
        gather_sel,
        stack,
        halo_msg,
        labels,
        tab,
        idx,
        idx_t,
        left,
        halo_s,
        halo_r,
        load_s,
    ) = refs[11 + 2 * PASSED :]
    loads = [
        pltpu.make_async_copy(src, dst, load_s.at[n])
        for n, (src, dst) in enumerate(
            (
                (grid_hbm, grid_ref),
                (cot_hbm, cot_ref),
                (ids_hbm, ids_ref),
                (send_hbm, send_sel),
                (label_hbm, label_sel),
                (table_hbm, table_ref),
                (index_hbm, index_ref),
                (gather_hbm, gather_sel),
                *zip(weights_hbm, weights_ref),
            )
        )
    ]
    for load in loads[0:8]:
        load.start()
    lat, lon, lat_up, lat_dn, lon_up, lon_dn = around()
    greet_halo()
    for load in loads[8:]:
        load.start()
    for load in loads[0:5]:
        load.wait()
    labels[...] = jnp.zeros_like(labels)
    for r in range(6):
        labels[2 * r : 2 * r + 2, :] = jnp.broadcast_to(ids_ref[r, :, 0:1].astype(F32), (2, 64))
    stack[0, 0:TOK, C:256] = dot(label_sel[...], labels[...].astype(BF16)).astype(BF16)
    stack[1, 0:TOK, C:256] = jnp.zeros((TOK, 64), BF16)
    for r in range(6):
        for q in range(12):
            at = (r * 12 + q) * 2
            stack[0, at : at + 2, 0:C] = grid_ref[r, q]
            stack[1, at : at + 2, 0:C] = cot_ref[r, q]
    for n in range(2):
        halo_msg[n] = dot(send_sel[...], stack[n, 0:TOK, :]).astype(BF16)
    pl.semaphore_wait(pltpu.get_barrier_semaphore(), 6)
    halo_to = ((lat, lon_dn), (lat_dn, lon), (lat_dn, lon_dn))
    halo = [
        pltpu.make_async_remote_copy(
            src_ref=halo_msg.at[:, d * 48 : (d + 1) * 48, :],
            dst_ref=stack.at[:, TOK + d * 48 : TOK + (d + 1) * 48, :],
            send_sem=halo_s.at[d],
            recv_sem=halo_r.at[d],
            device_id=halo_to[d],
            device_id_type=MESH,
        )
        for d in range(3)
    ]
    for copy in halo:
        copy.start()
    for load in loads[5:8]:
        load.wait()
    look_up_bias(table_ref, index_ref, bias_ref, tab, idx, idx_t, left)
    for load in loads[8:]:
        load.wait()
    for copy in halo:
        copy.wait()
    for n in range(2):
        win_ref[n] = dot(gather_sel[...], stack[n]).astype(BF16)


def layer_norm(values, gain_row, shift_row):
    centred = values - jnp.mean(values, -1, keepdims=True)
    inv_std = lax.rsqrt(jnp.mean(centred * centred, -1, keepdims=True) + NORM_EPS)
    normed = centred * inv_std
    return normed * gain_row + shift_row, normed, inv_std


def norm_back(incoming, normed, inv_std, gain_row):
    scaled = incoming * gain_row
    outgoing = inv_std * (
        scaled
        - jnp.mean(scaled, -1, keepdims=True)
        - normed * jnp.mean(scaled * normed, -1, keepdims=True)
    )
    return (
        outgoing,
        jnp.sum(incoming * normed, 0, keepdims=True),
        jnp.sum(incoming, 0, keepdims=True),
    )


def main_kernel(
    win_ref,
    gain_ref,
    shift_ref,
    wqkv_ref,
    bqkv_ref,
    wproj_ref,
    bproj_ref,
    w1_ref,
    b1_ref,
    w2_ref,
    b2_ref,
    bias_ref,
    index_ref,
    send_out_sel,
    place_sel,
    out_ref,
    din_ref,
    full_ref,
    tgrad_ref,
    out_stack,
    out_msg,
    probs,
    act,
    dfac,
    dsc,
    small,
    grads,
    core_in1,
    core_in2,
    plane_in1,
    plane_in2,
    z_out,
    z_in,
    z_all,
    z_part,
    owned,
    t_out,
    t_in,
    oh_s,
    oh_r,
    core_s,
    core_r,
    plane_s,
    plane_r,
    zs,
    zr,
    zgs,
    zgr,
    zps,
    zpr,
    ts,
    tr,
    tgs,
    tgr,
    ags,
    agr,
    fs,
    fr,
):
    lat, lon, lat_up, lat_dn, lon_up, lon_dn = around()
    core = lat % 2
    pair_lat = lat + 1 - 2 * core
    ylo = lon % 2
    z = lon // 2
    k = (lat // 2) * 2 + ylo

    def plane_device(kk):
        return ((kk // 2) * 2 + core, z * 2 + kk % 2)

    def each(first_d, last_d, body):
        def step(d, carry):
            body(d)
            return carry

        lax.fori_loop(first_d, last_d, step, 0)

    for first, last in ((10, 23), (1, 10), (23, 32)):
        each(first, last, lambda d: greet((lat, (lon + d) % 32)))
    each(1, 16, lambda d: greet(plane_device((k + d) % 16)))
    greet((pair_lat, lon))
    greet_halo()

    x = win_ref[0, :, 0:C].astype(F32)
    g_b = win_ref[1, :, 0:C]
    label_lane = win_ref[0, :, 128:256]
    pick = (lax.broadcasted_iota(jnp.int32, (8, 128), 1) == 64).astype(F32).astype(BF16)
    ids_row = dot(pick, label_lane, 1, 1)[0:1]
    ids_col = label_lane[:, 64:65].astype(F32)
    allowed = ids_row == ids_col

    gain0, gain1 = gain_ref[0:1, :], gain_ref[1:2, :]
    shift0, shift1 = shift_ref[0:1, :], shift_ref[1:2, :]
    first, hat1, inv1 = layer_norm(x, gain0, shift0)
    first_b = first.astype(BF16)
    bqkv = bqkv_ref[...].reshape(1, 3 * C)
    b1 = b1_ref[...].reshape(1, FF)
    wq = wqkv_ref[:, 0:C]
    wk = wqkv_ref[:, C : 2 * C]
    wv = wqkv_ref[:, 2 * C : 3 * C]
    q = (dot(first_b, wq) + bqkv[:, 0:C]).astype(BF16)
    key = (dot(first_b, wk) + bqkv[:, C : 2 * C]).astype(BF16)
    v = (dot(first_b, wv) + bqkv[:, 2 * C : 3 * C]).astype(BF16)
    lane = lax.broadcasted_iota(jnp.int32, (TOK, C), 1)

    def only(h, values):
        return jnp.where((lane >> 5) == h, values, jnp.zeros_like(values))

    mixed = jnp.zeros((TOK, C), F32)
    for h in range(HEADS):
        s = dot(only(h, q), key, 1, 1) * SCALE + bias_ref[h]
        s = jnp.where(allowed, s, NEG_FILL)
        e = jnp.exp(s - jnp.max(s, -1, keepdims=True))
        p = e * (1.0 / jnp.sum(e, -1, keepdims=True))
        probs[h] = p
        mixed = mixed + dot(p.astype(BF16), only(h, v))
    mixed_b = mixed.astype(BF16)
    attended = x + dot(mixed_b, wproj_ref[...]) + bproj_ref[...].reshape(1, C)

    second, hat2, inv2 = layer_norm(attended, gain1, shift1)
    second_b = second.astype(BF16)
    for b in range(FF // 128):
        cols = slice(b * 128, (b + 1) * 128)
        hidden = dot(second_b, w1_ref[:, cols]) + b1[:, cols]
        cumul = 0.5 * (1.0 + lax.erf(hidden * ROOT_HALF))
        act[:, cols] = (hidden * cumul).astype(BF16)
        dfac[:, cols] = cumul + hidden * jnp.exp(-0.5 * hidden * hidden) * ROOT_TWOPI
    result = (attended + dot(act[...], w2_ref[...], 1, 1) + b2_ref[...].reshape(1, C)).astype(BF16)

    halo_out_to = ((lat, lon_up), (lat_up, lon), (lat_up, lon_up))

    def send_back(n, values):
        out_stack[n, 0:TOK, 0:C] = values
        out_msg[n, :, 0:C] = dot(send_out_sel[...], values).astype(BF16)
        copies = [
            pltpu.make_async_remote_copy(
                src_ref=out_msg.at[n, d * 48 : (d + 1) * 48, :],
                dst_ref=out_stack.at[n, TOK + d * 48 : TOK + (d + 1) * 48, :],
                send_sem=oh_s.at[n, d],
                recv_sem=oh_r.at[n, d],
                device_id=halo_out_to[d],
                device_id_type=MESH,
            )
            for d in range(3)
        ]
        for copy in copies:
            copy.start()
        return copies

    small[...] = jnp.zeros_like(small)

    def keep(row, vector):
        width = vector.shape[1]
        for at in range(0, width, 128):
            n = min(128, width - at)
            small[row + at // 128 : row + at // 128 + 1, 0:n] = vector[:, at : at + n]

    gf = g_b.astype(F32)
    keep(21, jnp.sum(gf, 0, keepdims=True))
    d_second = jnp.zeros((TOK, C), F32)
    for b in range(FF // 128):
        cols = slice(b * 128, (b + 1) * 128)
        grads[FC2_ROW + b * C : FC2_ROW + (b + 1) * C, :] = dot(g_b, act[:, cols], 0, 0).astype(BF16)
        d_hidden = dot(g_b, w2_ref[:, cols]) * dfac[:, cols]
        d_hidden_b = d_hidden.astype(BF16)
        keep(15 + b, jnp.sum(d_hidden, 0, keepdims=True))
        grads[FC1_ROW + b * C : FC1_ROW + (b + 1) * C, :] = dot(second_b, d_hidden_b, 0, 0).astype(BF16)
        d_second = d_second + dot(d_hidden_b, w1_ref[:, cols], 1, 1)

    core_in = (core_in1, core_in2)
    plane_in = (plane_in1, plane_in2)

    def core_copy(n):
        base, rows = CHUNKS[n]
        return pltpu.make_async_remote_copy(
            src_ref=grads.at[pl.ds(pl.multiple_of(base + (1 - core) * 16 * rows, 16), 16 * rows), :],
            dst_ref=core_in[n],
            send_sem=core_s.at[n],
            recv_sem=core_r.at[n],
            device_id=(pair_lat, lon),
            device_id_type=MESH,
        )

    def plane_copy(n, d):
        base, rows = CHUNKS[n]
        kk = (k + d) % 16
        return pltpu.make_async_remote_copy(
            src_ref=grads.at[pl.ds(pl.multiple_of(base + (core * 16 + kk) * rows, 16), rows), :],
            dst_ref=plane_in[n].at[d],
            send_sem=plane_s.at[n, d],
            recv_sem=plane_r.at[n, d],
            device_id=plane_device(kk),
            device_id_type=MESH,
        )

    def z_device(d):
        return (lat, ((z + d) % 16) * 2 + ylo)

    def z_copy(d):
        return pltpu.make_async_remote_copy(
            src_ref=z_out.at[(z + d) % 16],
            dst_ref=z_in.at[d],
            send_sem=zs.at[d],
            recv_sem=zr.at[d],
            device_id=z_device(d),
            device_id_type=MESH,
        )

    def z_gather(d):
        return pltpu.make_async_remote_copy(
            src_ref=z_all.at[z],
            dst_ref=z_all.at[z],
            send_sem=zgs.at[d],
            recv_sem=zgr.at[d],
            device_id=z_device(d),
            device_id_type=MESH,
        )

    def z_share(d):
        return pltpu.make_async_remote_copy(
            src_ref=z_part.at[z],
            dst_ref=z_part.at[z],
            send_sem=zps.at[d],
            recv_sem=zpr.at[d],
            device_id=z_device(d),
            device_id_type=MESH,
        )

    def owner_rows(n):
        return slice(0, 64) if n == 0 else slice(64, OWNED)

    x_at, y_at = (lat // 2) % 4, (lat // 8) * 2 + ylo

    def plane_gather(n, d):
        xx, yy = (x_at + STEPS[d][0]) % 4, (y_at + STEPS[d][1]) % 4
        return pltpu.make_async_remote_copy(
            src_ref=full_ref.at[core, k, owner_rows(n)],
            dst_ref=full_ref.at[core, k, owner_rows(n)],
            send_sem=ags.at[n, d],
            recv_sem=agr.at[n, d],
            device_id=(((yy // 2) * 4 + xx) * 2 + core, z * 2 + yy % 2),
            device_id_type=MESH,
        )

    def forward(n, d):
        dx, dy = STEPS[d] if d < 15 else (0, 0)
        xx, yy = (x_at + 4 - dx) % 4, (y_at + 4 - dy) % 4
        kk = ((yy // 2) * 4 + xx) * 2 + yy % 2
        return pltpu.make_async_remote_copy(
            src_ref=full_ref.at[core, kk, owner_rows(n)],
            dst_ref=full_ref.at[core, kk, owner_rows(n)],
            send_sem=fs.at[n, d],
            recv_sem=fr.at[n, d],
            device_id=(pair_lat, lon),
            device_id_type=MESH,
        )

    def scatter_plane(n):
        base, rows = CHUNKS[n]
        core_copy(n).wait()
        mine = pl.ds(pl.multiple_of(base + core * 16 * rows, 16), 16 * rows)
        grads[mine, :] = (grads[mine, :].astype(F32) + core_in[n][...].astype(F32)).astype(BF16)
        each(1, 16, lambda d: plane_copy(n, d).start())

    def plane_total(n):
        base, rows = CHUNKS[n]
        each(1, 16, lambda d: plane_copy(n, d).wait())
        total = grads[pl.ds(pl.multiple_of(base + (core * 16 + k) * rows, 16), rows), :].astype(F32)
        for d in range(1, 16):
            total = total + plane_in[n][d].astype(F32)
        return total

    def scatter_z():
        total = plane_total(0)
        for m in range(16):
            z_out[m] = total[m * 4 : (m + 1) * 4]
        each(1, 16, lambda d: z_copy(d).start())

    def gather_z():
        each(1, 16, lambda d: z_copy(d).wait())
        total = z_out[z]
        for d in range(1, 16):
            total = total + z_in[d]
        z_all[z] = total
        each(1, 16, lambda d: z_gather(d).start())

    def share_z():
        z_part[z] = plane_total(1).astype(BF16)
        each(1, 16, lambda d: z_share(d).start())

    def start_plane(n):
        for d in reversed(range(15)):
            plane_gather(n, d).start()
        forward(n, 15).start()

    def gather_plane():
        each(1, 16, lambda d: z_gather(d).wait())
        for m in range(16):
            owned[m * 4 : (m + 1) * 4, :] = z_all[m]
        full_ref[core, k, owner_rows(0)] = owned[...].astype(BF16)
        start_plane(0)

    def gather_plane_shared():
        each(1, 16, lambda d: z_share(d).wait())
        total = z_part[0].astype(F32)
        for m in range(1, 16):
            total = total + z_part[m].astype(F32)
        full_ref[core, k, owner_rows(1)] = total.astype(BF16)
        start_plane(1)

    def pass_on(n):
        for d in range(15):
            plane_gather(n, d).wait()
            forward(n, d).start()

    pl.semaphore_wait(pltpu.get_barrier_semaphore(), 53)
    core_copy(0).start()
    out_copies = send_back(0, result)

    back2, dgain1, dshift1 = norm_back(d_second, hat2, inv2, gain1)
    keep(2, dgain1)
    keep(6, dshift1)
    d_att = gf + back2
    d_att_b = d_att.astype(BF16)
    scatter_plane(0)

    def put_pair(at, left, right):
        grads[at : at + C, :] = left[:, 0:128].astype(BF16)
        grads[at + C : at + 2 * C, :] = right[:, 0:128].astype(BF16)
        grads[at + 2 * C : at + 3 * C, :] = jnp.concatenate([left[:, 128:C], right[:, 128:C]], 1).astype(BF16)

    dw_proj = dot(mixed_b, d_att_b, 0, 0)
    keep(13, jnp.sum(d_att, 0, keepdims=True))
    dm = dot(d_att_b, wproj_ref[...], 1, 1).astype(BF16)

    dq = jnp.zeros((TOK, C), F32)
    dk = jnp.zeros((TOK, C), F32)
    dv = jnp.zeros((TOK, C), F32)
    for h in range(HEADS):
        p = probs[h]
        dm_h = only(h, dm)
        dp = dot(dm_h, v, 1, 1)
        ds = p * (dp - jnp.sum(dp * p, -1, keepdims=True))
        dsc[h, :, 0:128] = ds[:, 0:128]
        dsc[h, :, 128:256] = jnp.concatenate([ds[:, 128:TOK], jnp.zeros((TOK, 112), F32)], 1)
        ds_b = (ds * SCALE).astype(BF16)
        dq = dq + dot(ds_b, only(h, key))
        dk = dk + dot(ds_b, only(h, q), 0, 0)
        dv = dv + dot(p.astype(BF16), dm_h, 0, 0)
    dq_b, dk_b, dv_b = dq.astype(BF16), dk.astype(BF16), dv.astype(BF16)
    put_pair(QP_ROW, dot(first_b, dq_b, 0, 0), dot(first_b, dk_b, 0, 0))
    put_pair(QP_ROW + 3 * C, dot(first_b, dv_b, 0, 0), dw_proj)
    d_bias = jnp.concatenate(
        [jnp.sum(dq, 0, keepdims=True), jnp.sum(dk, 0, keepdims=True), jnp.sum(dv, 0, keepdims=True)], 1
    )
    keep(8, d_bias)
    d_first = dot(dq_b, wq, 1, 1) + dot(dk_b, wk, 1, 1) + dot(dv_b, wv, 1, 1)
    back1, dgain0, dshift0 = norm_back(d_first, hat1, inv1, gain0)
    keep(0, dgain0)
    keep(4, dshift0)
    grads[SMALL_ROW : SMALL_ROW + 32, :] = small[...].astype(BF16)
    grads[SMALL_ROW + 32 : ROWS, :] = jnp.zeros((ROWS - SMALL_ROW - 32, 128), BF16)
    core_copy(1).start()
    din_copies = send_back(1, (d_att + back1).astype(BF16))
    scatter_plane(1)
    scatter_z()

    hi_iota = lax.broadcasted_iota(jnp.int32, (32, 256), 0).astype(F32).astype(BF16)
    lo_iota = lax.broadcasted_iota(jnp.int32, (128, 256), 0).astype(F32).astype(BF16)

    def spread(row, count):
        return jnp.concatenate([jnp.broadcast_to(row, (16, row.shape[1])).astype(BF16)] * (count // 16), 0)

    def factors(flat, rows):
        width = flat.shape[1]
        is_hi = hi_iota[:, 0:width] == spread((flat >> 7).astype(F32), 32)
        is_lo = lo_iota[:, 0:width] == spread((flat & 127).astype(F32), 128)
        zero = jnp.zeros((), BF16)
        left = jnp.concatenate([jnp.where(is_hi, spread(row, 32), zero) for row in rows], 0)
        return left, jnp.where(is_lo, jnp.ones((), BF16), zero)

    def pairs(b, total):
        block = pl.ds(pl.multiple_of(b * 8, 8), 8)
        flat = index_ref[block, 0:128]
        rows = [dsc[h, block, 0:128] for h in range(HEADS)]
        two = lambda values, r: jnp.concatenate([values[r : r + 1], values[r + 1 : r + 2]], 1)
        parts = [factors(two(flat, r), [two(values, r) for values in rows]) for r in range(0, 8, 2)]
        left = jnp.concatenate([part[0] for part in parts], 1)
        right = jnp.concatenate([part[1] for part in parts], 1)
        return total + dot(left, right, 1, 1)

    table = lax.fori_loop(0, 10, pairs, jnp.zeros((HEADS * 32, 128), F32))
    share_z()
    table = lax.fori_loop(10, TOK // 8, pairs, table)
    flat_tail = jnp.concatenate([index_ref[:, 128:TOK].astype(F32), jnp.zeros((TOK, 112), F32)], 1).T[0:16]
    flat_tail = flat_tail.astype(jnp.int32)
    ds_tail = [dsc[h, :, 128:256].T for h in range(HEADS)]
    for r in range(16):
        table = table + dot(*factors(flat_tail[r : r + 1], [t[r : r + 1] for t in ds_tail]), 1, 1)
    for n in range(32):
        t_out[n] = table[n * 6 : (n + 1) * 6]

    def t_copy(d):
        to = (lon + d) % 32
        return pltpu.make_async_remote_copy(
            src_ref=t_out.at[to],
            dst_ref=t_in.at[d],
            send_sem=ts.at[d],
            recv_sem=tr.at[d],
            device_id=(lat, to),
            device_id_type=MESH,
        )

    def t_gather(d):
        return pltpu.make_async_remote_copy(
            src_ref=tgrad_ref.at[lon],
            dst_ref=tgrad_ref.at[lon],
            send_sem=tgs.at[d],
            recv_sem=tgr.at[d],
            device_id=(lat, (lon + d) % 32),
            device_id_type=MESH,
        )

    each(1, 32, lambda d: t_copy(d).start())
    gather_z()
    each(1, 32, lambda d: t_copy(d).wait())
    t_total = t_out[lon]
    for d in range(1, 32):
        t_total = t_total + t_in[d]
    tgrad_ref[lon] = t_total
    each(1, 32, lambda d: t_gather(d).start())
    gather_plane()
    gather_plane_shared()
    for n, copies, ref in ((0, out_copies, out_ref), (1, din_copies, din_ref)):
        for copy in copies:
            copy.wait()
        ref[...] = dot(place_sel[...], out_stack[n, :, 0:C]).astype(BF16)
    pass_on(0)
    pass_on(1)
    each(1, 32, lambda d: t_gather(d).wait())
    for n in range(2):
        for d in range(16):
            forward(n, d).wait()


def final_kernel(
    out_ref,
    din_ref,
    full_ref,
    tgrad_ref,
    output,
    grid_grad,
    gain_grad,
    shift_grad,
    dwqkv,
    dbqkv,
    dwproj,
    dbproj,
    dw1,
    db1,
    dw2,
    db2,
    dtable,
):
    for r in range(6):
        for q in range(12):
            at = (r * 12 + q) * 2
            output[r, q] = out_ref[at : at + 2, :]
            grid_grad[r, q] = din_ref[at : at + 2, :]

    def rows(start, count):
        parts = []
        at = start
        while at < start + count:
            n = 0 if at < CHUNKS[1][0] else 1
            base, size = CHUNKS[n]
            owner, inside = divmod(at - base, size)
            take = min(size - inside, start + count - at)
            first = inside + (0 if n == 0 else CHUNKS[0][1])
            parts.append(full_ref[owner // 16, owner % 16, first : first + take, :])
            at += take
        return jnp.concatenate(parts, 0).astype(F32) if len(parts) > 1 else parts[0].astype(F32)

    for b in range(FF // 128):
        cols = slice(b * 128, (b + 1) * 128)
        dw2[:, cols] = rows(FC2_ROW + b * C, C)
        dw1[:, cols] = rows(FC1_ROW + b * C, C)
    qa, ka, qk = (rows(QP_ROW + n * C, C) for n in range(3))
    va, pa, vp = (rows(QP_ROW + n * C, C) for n in range(3, 6))
    dwqkv[:, 0:128] = qa
    dwqkv[:, 128:C] = qk[:, 0:64]
    dwqkv[:, C : C + 128] = ka
    dwqkv[:, C + 128 : 2 * C] = qk[:, 64:128]
    dwqkv[:, 2 * C : 2 * C + 128] = va
    dwqkv[:, 2 * C + 128 : 3 * C] = vp[:, 0:64]
    dwproj[:, 0:128] = pa
    dwproj[:, 128:C] = vp[:, 64:128]
    vec = rows(SMALL_ROW, 32)

    def load(row, width, ref, at=0):
        for n in range(0, width, 128):
            m = min(128, width - n)
            ref[at : at + 1, n : n + m] = vec[row + n // 128 : row + n // 128 + 1, 0:m]

    load(0, C, gain_grad, 0)
    load(2, C, gain_grad, 1)
    load(4, C, shift_grad, 0)
    load(6, C, shift_grad, 1)
    for row, ref in ((8, dbqkv), (13, dbproj), (15, db1), (21, db2)):
        width = ref.shape[0]
        for n in range(0, width, 128):
            m = min(128, width - n)
            ref[n : n + m] = vec[row + n // 128, 0:m]
    for h in range(HEADS):
        for t in range(NHI):
            n = h * 32 + t
            m = min(128, NBIAS - t * 128)
            dtable[0, h, :, t * 128 : t * 128 + m] = tgrad_ref[n // 6, n % 6 : n % 6 + 1, 0:m]


def on_device(
    grid,
    region_ids,
    cotangent,
    norm_gain,
    norm_shift,
    qkv_weight,
    qkv_bias,
    proj_weight,
    proj_bias,
    fc1_weight,
    fc1_bias,
    fc2_weight,
    fc2_bias,
    bias_table,
    pair_index,
):
    vmem = pl.BlockSpec(memory_space=pltpu.VMEM)
    shape = jax.ShapeDtypeStruct
    dma = pltpu.SemaphoreType.DMA
    hbm = pl.BlockSpec(memory_space=pltpu.HBM)
    send_sel, gather_sel, label_sel, send_out_sel, place_sel = selectors()
    by_tile = lambda field: field.transpose(1, 2, 0, 3)
    fields = (by_tile(grid), by_tile(cotangent), region_ids.transpose(1, 0, 2))
    table = bias_table.transpose(0, 2, 1, 3)
    passed = (
        norm_gain,
        norm_shift,
        qkv_weight,
        qkv_bias,
        proj_weight,
        proj_bias,
        fc1_weight,
        fc1_bias,
        fc2_weight.T,
        fc2_bias,
        send_out_sel,
        place_sel,
    )
    held = lambda a: pltpu.VMEM(a.shape, a.dtype)
    bias, win, index, *passed = pl.pallas_call(
        halo_kernel,
        out_shape=(
            shape((HEADS, TOK, TOK), F32),
            shape((2, TOK, 256), BF16),
            shape((TOK, TOK), jnp.int32),
            *(shape(a.shape, a.dtype) for a in passed),
        ),
        in_specs=[hbm] * (8 + PASSED),
        out_specs=(vmem,) * (3 + PASSED),
        scratch_shapes=[
            *map(held, fields),
            held(send_sel),
            held(label_sel),
            held(table),
            held(gather_sel),
            pltpu.VMEM((2, 288, 256), BF16),
            pltpu.VMEM((2, 144, 256), BF16),
            pltpu.VMEM((16, 64), F32),
            pltpu.VMEM((NHI, HEADS, 8, 128), F32),
            pltpu.VMEM((TOK, 256), jnp.int32),
            pltpu.VMEM((16, 256), jnp.int32),
            pltpu.VMEM((HEADS, 128, 256), F32),
            dma((3,)),
            dma((3,)),
            dma((8 + PASSED,)),
        ],
        name="halo_and_bias",
        compiler_params=pltpu.CompilerParams(
            collective_id=0, has_side_effects=True, vmem_limit_bytes=32 * 1024 * 1024
        ),
    )(
        *(
            pltpu.with_memory_space_constraint(a, pltpu.HBM)
            for a in (*fields, send_sel, label_sel, table, pair_index, gather_sel, *passed)
        )
    )
    out, din, full, tgrad = pl.pallas_call(
        main_kernel,
        out_shape=(
            shape((TOK, C), BF16),
            shape((TOK, C), BF16),
            shape((2, 16, OWNED, 128), BF16),
            shape((32, 6, 128), F32),
        ),
        in_specs=[vmem] * 15,
        out_specs=(vmem,) * 4,
        scratch_shapes=[
            pltpu.VMEM((2, 288, 256), BF16),
            pltpu.VMEM((2, 144, 256), BF16),
            pltpu.VMEM((HEADS, TOK, TOK), F32),
            pltpu.VMEM((TOK, FF), BF16),
            pltpu.VMEM((TOK, FF), F32),
            pltpu.VMEM((HEADS, TOK, 256), F32),
            pltpu.VMEM((32, 128), F32),
            pltpu.VMEM((ROWS, 128), BF16),
            pltpu.VMEM((1024, 128), BF16),
            pltpu.VMEM((768, 128), BF16),
            pltpu.VMEM((16, 64, 128), BF16),
            pltpu.VMEM((16, 48, 128), BF16),
            pltpu.VMEM((16, 4, 128), F32),
            pltpu.VMEM((16, 4, 128), F32),
            pltpu.VMEM((16, 4, 128), F32),
            pltpu.VMEM((16, 48, 128), BF16),
            pltpu.VMEM((64, 128), F32),
            pltpu.VMEM((32, 6, 128), F32),
            pltpu.VMEM((32, 6, 128), F32),
            dma((2, 3)),
            dma((2, 3)),
            dma((2,)),
            dma((2,)),
            dma((2, 16)),
            dma((2, 16)),
            dma((16,)),
            dma((16,)),
            dma((16,)),
            dma((16,)),
            dma((16,)),
            dma((16,)),
            dma((32,)),
            dma((32,)),
            dma((32,)),
            dma((32,)),
            dma((2, 16)),
            dma((2, 16)),
            dma((2, 16)),
            dma((2, 16)),
        ],
        name="window_block",
        compiler_params=pltpu.CompilerParams(
            collective_id=1, has_side_effects=True, vmem_limit_bytes=48 * 1024 * 1024
        ),
    )(
        win,
        *passed[0:10],
        bias,
        index,
        *passed[10:],
    )
    outs = pl.pallas_call(
        final_kernel,
        out_shape=(
            shape((6, 12, 2, C), BF16),
            shape((6, 12, 2, C), BF16),
            shape((2, C), F32),
            shape((2, C), F32),
            shape((C, 3 * C), F32),
            shape((3 * C,), F32),
            shape((C, C), F32),
            shape((C,), F32),
            shape((C, FF), F32),
            shape((FF,), F32),
            shape((C, FF), F32),
            shape((C,), F32),
            shape((1, HEADS, 1, NBIAS), F32),
        ),
        in_specs=[vmem] * 4,
        out_specs=(vmem,) * 13,
        name="outputs",
        compiler_params=pltpu.CompilerParams(vmem_limit_bytes=32 * 1024 * 1024),
    )(out, din, full, tgrad)
    outs = list(outs)
    for n in (0, 1):
        outs[n] = outs[n].transpose(2, 0, 1, 3)
    outs[10] = outs[10].T
    outs[12] = outs[12].transpose(0, 2, 1, 3)
    return tuple(outs)


def solution(mesh):
    field = P(None, "lat", "lon", None)
    table = P(None, "lat", None, None)
    return jax.shard_map(
        on_device,
        mesh=mesh,
        in_specs=(field, P(None, "lat", "lon"), field) + (P(),) * 10 + (table, P()),
        out_specs=(field, field) + (P(),) * 10 + (table,),
        check_vma=False,
    )
```

```python
import math

import jax
import jax.numpy as jnp
import numpy as np
from jax import lax
from jax.experimental import pallas as pl
from jax.experimental.pallas import tpu as pltpu
from jax.sharding import PartitionSpec as P

F32 = jnp.float32
BF16 = jnp.bfloat16
MESH = pl.DeviceIdType.MESH

C = 192
HEADS = 6
HEAD = 32
FF = 768
TOK = 144
NBIAS = 3312
NHI = 26
NEG_FILL = -1e30
NORM_EPS = 1e-05
ROOT_HALF = 1.0 / math.sqrt(2.0)
ROOT_TWOPI = 1.0 / math.sqrt(2.0 * math.pi)
SCALE = HEAD ** (-0.5)

ROWS = 3584
FC2_ROW = 0
FC1_ROW = 1152
QP_ROW = 2304
SMALL_ROW = 3456
CHUNKS = ((0, 64), (2048, 48))
OWNED = 112
STEPS = (
    ((1, 0), (3, 0), (0, 1), (0, 3))
    + ((1, 1), (1, 3), (3, 1), (3, 3), (2, 0), (0, 2))
    + ((2, 1), (2, 3), (1, 2), (3, 2), (2, 2))
)
PASSED = 12


def dot(a, b, ca=1, cb=0):
    return lax.dot_general(a, b, (((ca,), (cb,)), ((), ())), preferred_element_type=F32)


def selectors():
    held = lambda l, r, q: (r * 12 + q) * 2 + l
    send = np.zeros((144, 144), np.float32)
    gather = np.zeros((144, 288), np.float32)
    send_out = np.zeros((144, 144), np.float32)
    place = np.zeros((144, 288), np.float32)
    label = np.zeros((144, 16), np.float32)
    for l in range(2):
        for i in range(6):
            for j in range(12):
                label[held(l, i, j), i * 2 + l] = 1
                tok = l * 72 + i * 12 + j
                lev = (l + 1) % 2
                far_i, far_j = i >= 3, j >= 6
                r = i - 3 if far_i else i + 3
                q = j - 6 if far_j else j + 6
                if not far_i and not far_j:
                    gather[tok, held(lev, r, q)] = 1
                    place[held(lev, r, q), tok] = 1
                    continue
                d = 2 if (far_i and far_j) else (1 if far_i else 0)
                m = d * 48 + l * 18 + (i % 3) * 6 + (j % 6)
                send[m, held(lev, r, q)] = 1
                gather[tok, 144 + m] = 1
                send_out[m, tok] = 1
                place[held(lev, r, q), 144 + m] = 1
    return [jnp.asarray(a, BF16) for a in (send, gather, label, send_out, place)]


def look_up_bias(table_ref, index_ref, bias_ref, tab, idx, idx_t, left):
    for h in range(HEADS):
        for t in range(NHI):
            n = min(128, NBIAS - t * 128)
            row = table_ref[0, h, :, t * 128 : t * 128 + n]
            if n < 128:
                row = jnp.concatenate([row, jnp.zeros((1, 128 - n), F32)], 1)
            tab[t, h] = jnp.broadcast_to(row, (8, 128))
    idx[...] = jnp.zeros_like(idx)
    idx[:, 0:TOK] = index_ref[...]
    tail = idx[:, 128:256].astype(F32).T
    idx_t[:, 0:TOK] = tail[0:16].astype(jnp.int32)
    idx_t[:, TOK:256] = jnp.zeros((16, 256 - TOK), jnp.int32)
    left[...] = jnp.zeros_like(left)

    def look(flat, store):
        lo = flat & 127
        hi = flat >> 7
        acc = [jnp.zeros((8, 128), F32)] * HEADS
        for t in range(NHI):
            here = hi == t
            for h in range(HEADS):
                got = jnp.take_along_axis(tab[t, h], lo, axis=1, mode="promise_in_bounds")
                acc[h] = jnp.where(here, got, acc[h])
        for h in range(HEADS):
            store(h, acc[h])

    def body(b, carry):
        at = pl.multiple_of(b * 8, 8)

        def store(h, acc):
            bias_ref[h, pl.ds(at, 8), 0:128] = acc

        look(idx[pl.ds(at, 8), 0:128], store)
        return carry

    lax.fori_loop(0, TOK // 8, body, 0)
    for a in range(2):
        for t in range(2):

            def store(h, acc, a=a, t=t):
                left[h, a * 8 : a * 8 + 8, t * 128 : (t + 1) * 128] = acc

            look(idx_t[a * 8 : a * 8 + 8, t * 128 : (t + 1) * 128], store)
    for h in range(HEADS):
        bias_ref[h, :, 128:TOK] = left[h].T[0:TOK, 0:16]


def around():
    lat = lax.axis_index("lat")
    lon = lax.axis_index("lon")
    return lat, lon, (lat + 1) % 16, (lat + 15) % 16, (lon + 1) % 32, (lon + 31) % 32


def greet(device):
    pl.semaphore_signal(pltpu.get_barrier_semaphore(), inc=1, device_id=device, device_id_type=MESH)


def greet_halo():
    lat, lon, lat_up, lat_dn, lon_up, lon_dn = around()
    for device in (
        (lat_up, lon),
        (lat_dn, lon),
        (lat, lon_up),
        (lat, lon_dn),
        (lat_up, lon_up),
        (lat_dn, lon_dn),
    ):
        greet(device)


def halo_kernel(*refs):
    grid_hbm, cot_hbm, ids_hbm, send_hbm, label_hbm, table_hbm, index_hbm, gather_hbm = refs[0:8]
    weights_hbm = refs[8 : 8 + PASSED]
    bias_ref, win_ref, index_ref = refs[8 + PASSED : 11 + PASSED]
    weights_ref = refs[11 + PASSED : 11 + 2 * PASSED]
    (
        grid_ref,
        cot_ref,
        ids_ref,
        send_sel,
        label_sel,
        table_ref,
        gather_sel,
        stack,
        halo_msg,
        labels,
        tab,
        idx,
        idx_t,
        left,
        halo_s,
        halo_r,
        load_s,
    ) = refs[11 + 2 * PASSED :]
    loads = [
        pltpu.make_async_copy(src, dst, load_s.at[n])
        for n, (src, dst) in enumerate(
            (
                (grid_hbm, grid_ref),
                (cot_hbm, cot_ref),
                (ids_hbm, ids_ref),
                (send_hbm, send_sel),
                (label_hbm, label_sel),
                (table_hbm, table_ref),
                (index_hbm, index_ref),
                (gather_hbm, gather_sel),
                *zip(weights_hbm, weights_ref),
            )
        )
    ]
    for load in loads[0:8]:
        load.start()
    lat, lon, lat_up, lat_dn, lon_up, lon_dn = around()
    greet_halo()
    for load in loads[8:]:
        load.start()
    for load in loads[0:5]:
        load.wait()
    labels[...] = jnp.zeros_like(labels)
    for r in range(6):
        labels[2 * r : 2 * r + 2, :] = jnp.broadcast_to(ids_ref[r, :, 0:1].astype(F32), (2, 64))
    stack[0, 0:TOK, C:256] = dot(label_sel[...], labels[...].astype(BF16)).astype(BF16)
    stack[1, 0:TOK, C:256] = jnp.zeros((TOK, 64), BF16)
    for r in range(6):
        for q in range(12):
            at = (r * 12 + q) * 2
            stack[0, at : at + 2, 0:C] = grid_ref[r, q]
            stack[1, at : at + 2, 0:C] = cot_ref[r, q]
    for n in range(2):
        halo_msg[n] = dot(send_sel[...], stack[n, 0:TOK, :]).astype(BF16)
    pl.semaphore_wait(pltpu.get_barrier_semaphore(), 6)
    halo_to = ((lat, lon_dn), (lat_dn, lon), (lat_dn, lon_dn))
    halo = [
        pltpu.make_async_remote_copy(
            src_ref=halo_msg.at[:, d * 48 : (d + 1) * 48, :],
            dst_ref=stack.at[:, TOK + d * 48 : TOK + (d + 1) * 48, :],
            send_sem=halo_s.at[d],
            recv_sem=halo_r.at[d],
            device_id=halo_to[d],
            device_id_type=MESH,
        )
        for d in range(3)
    ]
    for copy in halo:
        copy.start()
    for load in loads[5:8]:
        load.wait()
    look_up_bias(table_ref, index_ref, bias_ref, tab, idx, idx_t, left)
    for load in loads[8:]:
        load.wait()
    for copy in halo:
        copy.wait()
    for n in range(2):
        win_ref[n] = dot(gather_sel[...], stack[n]).astype(BF16)


def layer_norm(values, gain_row, shift_row):
    centred = values - jnp.mean(values, -1, keepdims=True)
    inv_std = lax.rsqrt(jnp.mean(centred * centred, -1, keepdims=True) + NORM_EPS)
    normed = centred * inv_std
    return normed * gain_row + shift_row, normed, inv_std


def norm_back(incoming, normed, inv_std, gain_row):
    scaled = incoming * gain_row
    outgoing = inv_std * (
        scaled
        - jnp.mean(scaled, -1, keepdims=True)
        - normed * jnp.mean(scaled * normed, -1, keepdims=True)
    )
    return (
        outgoing,
        jnp.sum(incoming * normed, 0, keepdims=True),
        jnp.sum(incoming, 0, keepdims=True),
    )


def main_kernel(
    win_ref,
    gain_ref,
    shift_ref,
    wqkv_ref,
    bqkv_ref,
    wproj_ref,
    bproj_ref,
    w1_ref,
    b1_ref,
    w2_ref,
    b2_ref,
    bias_ref,
    index_ref,
    send_out_sel,
    place_sel,
    out_ref,
    din_ref,
    full_ref,
    tgrad_ref,
    out_stack,
    out_msg,
    probs,
    act,
    dfac,
    dsc,
    small,
    grads,
    core_in1,
    core_in2,
    plane_in1,
    plane_in2,
    z_out,
    z_in,
    z_all,
    owned,
    t_out,
    t_in,
    oh_s,
    oh_r,
    core_s,
    core_r,
    plane_s,
    plane_r,
    zs,
    zr,
    zgs,
    zgr,
    ts,
    tr,
    tgs,
    tgr,
    ags,
    agr,
    fs,
    fr,
):
    lat, lon, lat_up, lat_dn, lon_up, lon_dn = around()
    core = lat % 2
    pair_lat = lat + 1 - 2 * core
    ylo = lon % 2
    z = lon // 2
    k = (lat // 2) * 2 + ylo

    def plane_device(kk):
        return ((kk // 2) * 2 + core, z * 2 + kk % 2)

    def each(first_d, last_d, body):
        def step(d, carry):
            body(d)
            return carry

        lax.fori_loop(first_d, last_d, step, 0)

    for first, last in ((10, 23), (1, 10), (23, 32)):
        each(first, last, lambda d: greet((lat, (lon + d) % 32)))
    each(1, 16, lambda d: greet(plane_device((k + d) % 16)))
    greet((pair_lat, lon))
    greet_halo()

    x = win_ref[0, :, 0:C].astype(F32)
    g_b = win_ref[1, :, 0:C]
    label_lane = win_ref[0, :, 128:256]
    pick = (lax.broadcasted_iota(jnp.int32, (8, 128), 1) == 64).astype(F32).astype(BF16)
    ids_row = dot(pick, label_lane, 1, 1)[0:1]
    ids_col = label_lane[:, 64:65].astype(F32)
    allowed = ids_row == ids_col

    gain0, gain1 = gain_ref[0:1, :], gain_ref[1:2, :]
    shift0, shift1 = shift_ref[0:1, :], shift_ref[1:2, :]
    first, hat1, inv1 = layer_norm(x, gain0, shift0)
    first_b = first.astype(BF16)
    bqkv = bqkv_ref[...].reshape(1, 3 * C)
    b1 = b1_ref[...].reshape(1, FF)
    wq = wqkv_ref[:, 0:C]
    wk = wqkv_ref[:, C : 2 * C]
    wv = wqkv_ref[:, 2 * C : 3 * C]
    q = (dot(first_b, wq) + bqkv[:, 0:C]).astype(BF16)
    key = (dot(first_b, wk) + bqkv[:, C : 2 * C]).astype(BF16)
    v = (dot(first_b, wv) + bqkv[:, 2 * C : 3 * C]).astype(BF16)
    lane = lax.broadcasted_iota(jnp.int32, (TOK, C), 1)

    def only(h, values):
        return jnp.where((lane >> 5) == h, values, jnp.zeros_like(values))

    mixed = jnp.zeros((TOK, C), F32)
    for h in range(HEADS):
        s = dot(only(h, q), key, 1, 1) * SCALE + bias_ref[h]
        s = jnp.where(allowed, s, NEG_FILL)
        e = jnp.exp(s - jnp.max(s, -1, keepdims=True))
        p = e * (1.0 / jnp.sum(e, -1, keepdims=True))
        probs[h] = p
        mixed = mixed + dot(p.astype(BF16), only(h, v))
    mixed_b = mixed.astype(BF16)
    attended = x + dot(mixed_b, wproj_ref[...]) + bproj_ref[...].reshape(1, C)

    second, hat2, inv2 = layer_norm(attended, gain1, shift1)
    second_b = second.astype(BF16)
    for b in range(FF // 128):
        cols = slice(b * 128, (b + 1) * 128)
        hidden = dot(second_b, w1_ref[:, cols]) + b1[:, cols]
        cumul = 0.5 * (1.0 + lax.erf(hidden * ROOT_HALF))
        act[:, cols] = (hidden * cumul).astype(BF16)
        dfac[:, cols] = cumul + hidden * jnp.exp(-0.5 * hidden * hidden) * ROOT_TWOPI
    result = (attended + dot(act[...], w2_ref[...], 1, 1) + b2_ref[...].reshape(1, C)).astype(BF16)

    halo_out_to = ((lat, lon_up), (lat_up, lon), (lat_up, lon_up))

    def send_back(n, values):
        out_stack[n, 0:TOK, 0:C] = values
        out_msg[n, :, 0:C] = dot(send_out_sel[...], values).astype(BF16)
        copies = [
            pltpu.make_async_remote_copy(
                src_ref=out_msg.at[n, d * 48 : (d + 1) * 48, :],
                dst_ref=out_stack.at[n, TOK + d * 48 : TOK + (d + 1) * 48, :],
                send_sem=oh_s.at[n, d],
                recv_sem=oh_r.at[n, d],
                device_id=halo_out_to[d],
                device_id_type=MESH,
            )
            for d in range(3)
        ]
        for copy in copies:
            copy.start()
        return copies

    small[...] = jnp.zeros_like(small)

    def keep(row, vector):
        width = vector.shape[1]
        for at in range(0, width, 128):
            n = min(128, width - at)
            small[row + at // 128 : row + at // 128 + 1, 0:n] = vector[:, at : at + n]

    gf = g_b.astype(F32)
    keep(21, jnp.sum(gf, 0, keepdims=True))
    d_second = jnp.zeros((TOK, C), F32)
    for b in range(FF // 128):
        cols = slice(b * 128, (b + 1) * 128)
        grads[FC2_ROW + b * C : FC2_ROW + (b + 1) * C, :] = dot(g_b, act[:, cols], 0, 0).astype(BF16)
        d_hidden = dot(g_b, w2_ref[:, cols]) * dfac[:, cols]
        d_hidden_b = d_hidden.astype(BF16)
        keep(15 + b, jnp.sum(d_hidden, 0, keepdims=True))
        grads[FC1_ROW + b * C : FC1_ROW + (b + 1) * C, :] = dot(second_b, d_hidden_b, 0, 0).astype(BF16)
        d_second = d_second + dot(d_hidden_b, w1_ref[:, cols], 1, 1)

    z_out[...] = jnp.zeros_like(z_out)
    core_in = (core_in1, core_in2)
    plane_in = (plane_in1, plane_in2)

    def core_copy(n):
        base, rows = CHUNKS[n]
        return pltpu.make_async_remote_copy(
            src_ref=grads.at[pl.ds(pl.multiple_of(base + (1 - core) * 16 * rows, 16), 16 * rows), :],
            dst_ref=core_in[n],
            send_sem=core_s.at[n],
            recv_sem=core_r.at[n],
            device_id=(pair_lat, lon),
            device_id_type=MESH,
        )

    def plane_copy(n, d):
        base, rows = CHUNKS[n]
        kk = (k + d) % 16
        return pltpu.make_async_remote_copy(
            src_ref=grads.at[pl.ds(pl.multiple_of(base + (core * 16 + kk) * rows, 16), rows), :],
            dst_ref=plane_in[n].at[d],
            send_sem=plane_s.at[n, d],
            recv_sem=plane_r.at[n, d],
            device_id=plane_device(kk),
            device_id_type=MESH,
        )

    def z_device(d):
        return (lat, ((z + d) % 16) * 2 + ylo)

    def z_copy(n, d):
        return pltpu.make_async_remote_copy(
            src_ref=z_out.at[n, (z + d) % 16],
            dst_ref=z_in.at[n, d],
            send_sem=zs.at[n, d],
            recv_sem=zr.at[n, d],
            device_id=z_device(d),
            device_id_type=MESH,
        )

    def z_gather(n, d):
        return pltpu.make_async_remote_copy(
            src_ref=z_all.at[n, z],
            dst_ref=z_all.at[n, z],
            send_sem=zgs.at[n, d],
            recv_sem=zgr.at[n, d],
            device_id=z_device(d),
            device_id_type=MESH,
        )

    def owner_rows(n):
        return slice(0, 64) if n == 0 else slice(64, OWNED)

    x_at, y_at = (lat // 2) % 4, (lat // 8) * 2 + ylo

    def plane_gather(n, d):
        xx, yy = (x_at + STEPS[d][0]) % 4, (y_at + STEPS[d][1]) % 4
        return pltpu.make_async_remote_copy(
            src_ref=full_ref.at[core, k, owner_rows(n)],
            dst_ref=full_ref.at[core, k, owner_rows(n)],
            send_sem=ags.at[n, d],
            recv_sem=agr.at[n, d],
            device_id=(((yy // 2) * 4 + xx) * 2 + core, z * 2 + yy % 2),
            device_id_type=MESH,
        )

    def forward(n, d):
        dx, dy = STEPS[d] if d < 15 else (0, 0)
        xx, yy = (x_at + 4 - dx) % 4, (y_at + 4 - dy) % 4
        kk = ((yy // 2) * 4 + xx) * 2 + yy % 2
        return pltpu.make_async_remote_copy(
            src_ref=full_ref.at[core, kk, owner_rows(n)],
            dst_ref=full_ref.at[core, kk, owner_rows(n)],
            send_sem=fs.at[n, d],
            recv_sem=fr.at[n, d],
            device_id=(pair_lat, lon),
            device_id_type=MESH,
        )

    def scatter_plane(n):
        base, rows = CHUNKS[n]
        core_copy(n).wait()
        mine = pl.ds(pl.multiple_of(base + core * 16 * rows, 16), 16 * rows)
        grads[mine, :] = (grads[mine, :].astype(F32) + core_in[n][...].astype(F32)).astype(BF16)
        each(1, 16, lambda d: plane_copy(n, d).start())

    def plane_total(n):
        base, rows = CHUNKS[n]
        each(1, 16, lambda d: plane_copy(n, d).wait())
        total = grads[pl.ds(pl.multiple_of(base + (core * 16 + k) * rows, 16), rows), :].astype(F32)
        for d in range(1, 16):
            total = total + plane_in[n][d].astype(F32)
        return total

    def scatter_z(n):
        per = CHUNKS[n][1] // 16
        total = plane_total(n)
        for m in range(16):
            z_out[n, m, 0:per] = total[m * per : (m + 1) * per]
        each(1, 16, lambda d: z_copy(n, d).start())

    def gather_z(n):
        each(1, 16, lambda d: z_copy(n, d).wait())
        total = z_out[n, z]
        for d in range(1, 16):
            total = total + z_in[n, d]
        z_all[n, z] = total
        each(1, 16, lambda d: z_gather(n, d).start())

    def gather_plane(n):
        rows = CHUNKS[n][1]
        per = rows // 16
        each(1, 16, lambda d: z_gather(n, d).wait())
        for m in range(16):
            owned[m * per : (m + 1) * per, :] = z_all[n, m, 0:per]
        full_ref[core, k, owner_rows(n)] = owned[0:rows, :].astype(BF16)
        for d in reversed(range(15)):
            plane_gather(n, d).start()
        forward(n, 15).start()

    def pass_on(n):
        for d in range(15):
            plane_gather(n, d).wait()
            forward(n, d).start()

    back2, dgain1, dshift1 = norm_back(d_second, hat2, inv2, gain1)
    keep(2, dgain1)
    keep(6, dshift1)
    d_att = gf + back2
    d_att_b = d_att.astype(BF16)

    def put_pair(at, left, right):
        grads[at : at + C, :] = left[:, 0:128].astype(BF16)
        grads[at + C : at + 2 * C, :] = right[:, 0:128].astype(BF16)
        grads[at + 2 * C : at + 3 * C, :] = jnp.concatenate([left[:, 128:C], right[:, 128:C]], 1).astype(BF16)

    dw_proj = dot(mixed_b, d_att_b, 0, 0)
    keep(13, jnp.sum(d_att, 0, keepdims=True))
    dm = dot(d_att_b, wproj_ref[...], 1, 1).astype(BF16)

    dq = jnp.zeros((TOK, C), F32)
    dk = jnp.zeros((TOK, C), F32)
    dv = jnp.zeros((TOK, C), F32)
    for h in range(HEADS):
        p = probs[h]
        dm_h = only(h, dm)
        dp = dot(dm_h, v, 1, 1)
        ds = p * (dp - jnp.sum(dp * p, -1, keepdims=True))
        dsc[h, :, 0:128] = ds[:, 0:128]
        dsc[h, :, 128:256] = jnp.concatenate([ds[:, 128:TOK], jnp.zeros((TOK, 112), F32)], 1)
        ds_b = (ds * SCALE).astype(BF16)
        dq = dq + dot(ds_b, only(h, key))
        dk = dk + dot(ds_b, only(h, q), 0, 0)
        dv = dv + dot(p.astype(BF16), dm_h, 0, 0)
    dq_b, dk_b, dv_b = dq.astype(BF16), dk.astype(BF16), dv.astype(BF16)
    put_pair(QP_ROW, dot(first_b, dq_b, 0, 0), dot(first_b, dk_b, 0, 0))
    put_pair(QP_ROW + 3 * C, dot(first_b, dv_b, 0, 0), dw_proj)
    d_bias = jnp.concatenate(
        [jnp.sum(dq, 0, keepdims=True), jnp.sum(dk, 0, keepdims=True), jnp.sum(dv, 0, keepdims=True)], 1
    )
    keep(8, d_bias)
    d_first = dot(dq_b, wq, 1, 1) + dot(dk_b, wk, 1, 1) + dot(dv_b, wv, 1, 1)
    back1, dgain0, dshift0 = norm_back(d_first, hat1, inv1, gain0)
    keep(0, dgain0)
    keep(4, dshift0)
    grads[SMALL_ROW : SMALL_ROW + 32, :] = small[...].astype(BF16)
    grads[SMALL_ROW + 32 : ROWS, :] = jnp.zeros((ROWS - SMALL_ROW - 32, 128), BF16)
    pl.semaphore_wait(pltpu.get_barrier_semaphore(), 53)
    core_copy(0).start()
    core_copy(1).start()
    out_copies = send_back(0, result)
    scatter_plane(0)
    din_copies = send_back(1, (d_att + back1).astype(BF16))
    scatter_plane(1)

    hi_iota = lax.broadcasted_iota(jnp.int32, (32, 256), 0).astype(F32).astype(BF16)
    lo_iota = lax.broadcasted_iota(jnp.int32, (128, 256), 0).astype(F32).astype(BF16)

    def spread(row, count):
        return jnp.concatenate([jnp.broadcast_to(row, (16, row.shape[1])).astype(BF16)] * (count // 16), 0)

    def factors(flat, rows):
        width = flat.shape[1]
        is_hi = hi_iota[:, 0:width] == spread((flat >> 7).astype(F32), 32)
        is_lo = lo_iota[:, 0:width] == spread((flat & 127).astype(F32), 128)
        zero = jnp.zeros((), BF16)
        left = jnp.concatenate([jnp.where(is_hi, spread(row, 32), zero) for row in rows], 0)
        return left, jnp.where(is_lo, jnp.ones((), BF16), zero)

    def pairs(b, total):
        block = pl.ds(pl.multiple_of(b * 8, 8), 8)
        flat = index_ref[block, 0:128]
        rows = [dsc[h, block, 0:128] for h in range(HEADS)]
        two = lambda values, r: jnp.concatenate([values[r : r + 1], values[r + 1 : r + 2]], 1)
        parts = [factors(two(flat, r), [two(values, r) for values in rows]) for r in range(0, 8, 2)]
        left = jnp.concatenate([part[0] for part in parts], 1)
        right = jnp.concatenate([part[1] for part in parts], 1)
        return total + dot(left, right, 1, 1)

    table = lax.fori_loop(0, 11, pairs, jnp.zeros((HEADS * 32, 128), F32))
    scatter_z(0)
    table = lax.fori_loop(11, 14, pairs, table)
    scatter_z(1)
    table = lax.fori_loop(14, TOK // 8, pairs, table)
    flat_tail = jnp.concatenate([index_ref[:, 128:TOK].astype(F32), jnp.zeros((TOK, 112), F32)], 1).T[0:16]
    flat_tail = flat_tail.astype(jnp.int32)
    ds_tail = [dsc[h, :, 128:256].T for h in range(HEADS)]
    for r in range(16):
        table = table + dot(*factors(flat_tail[r : r + 1], [t[r : r + 1] for t in ds_tail]), 1, 1)
    for n in range(32):
        t_out[n] = table[n * 6 : (n + 1) * 6]

    def t_copy(d):
        to = (lon + d) % 32
        return pltpu.make_async_remote_copy(
            src_ref=t_out.at[to],
            dst_ref=t_in.at[d],
            send_sem=ts.at[d],
            recv_sem=tr.at[d],
            device_id=(lat, to),
            device_id_type=MESH,
        )

    def t_gather(d):
        return pltpu.make_async_remote_copy(
            src_ref=tgrad_ref.at[lon],
            dst_ref=tgrad_ref.at[lon],
            send_sem=tgs.at[d],
            recv_sem=tgr.at[d],
            device_id=(lat, (lon + d) % 32),
            device_id_type=MESH,
        )

    each(1, 32, lambda d: t_copy(d).start())
    gather_z(0)
    gather_z(1)
    each(1, 32, lambda d: t_copy(d).wait())
    t_total = t_out[lon]
    for d in range(1, 32):
        t_total = t_total + t_in[d]
    tgrad_ref[lon] = t_total
    each(1, 32, lambda d: t_gather(d).start())
    gather_plane(0)
    gather_plane(1)
    for n, copies, ref in ((0, out_copies, out_ref), (1, din_copies, din_ref)):
        for copy in copies:
            copy.wait()
        ref[...] = dot(place_sel[...], out_stack[n, :, 0:C]).astype(BF16)
    pass_on(0)
    pass_on(1)
    each(1, 32, lambda d: t_gather(d).wait())
    for n in range(2):
        for d in range(16):
            forward(n, d).wait()


def final_kernel(
    out_ref,
    din_ref,
    full_ref,
    tgrad_ref,
    output,
    grid_grad,
    gain_grad,
    shift_grad,
    dwqkv,
    dbqkv,
    dwproj,
    dbproj,
    dw1,
    db1,
    dw2,
    db2,
    dtable,
):
    for r in range(6):
        for q in range(12):
            at = (r * 12 + q) * 2
            output[r, q] = out_ref[at : at + 2, :]
            grid_grad[r, q] = din_ref[at : at + 2, :]

    def rows(start, count):
        parts = []
        at = start
        while at < start + count:
            n = 0 if at < CHUNKS[1][0] else 1
            base, size = CHUNKS[n]
            owner, inside = divmod(at - base, size)
            take = min(size - inside, start + count - at)
            first = inside + (0 if n == 0 else CHUNKS[0][1])
            parts.append(full_ref[owner // 16, owner % 16, first : first + take, :])
            at += take
        return jnp.concatenate(parts, 0).astype(F32) if len(parts) > 1 else parts[0].astype(F32)

    for b in range(FF // 128):
        cols = slice(b * 128, (b + 1) * 128)
        dw2[:, cols] = rows(FC2_ROW + b * C, C)
        dw1[:, cols] = rows(FC1_ROW + b * C, C)
    qa, ka, qk = (rows(QP_ROW + n * C, C) for n in range(3))
    va, pa, vp = (rows(QP_ROW + n * C, C) for n in range(3, 6))
    dwqkv[:, 0:128] = qa
    dwqkv[:, 128:C] = qk[:, 0:64]
    dwqkv[:, C : C + 128] = ka
    dwqkv[:, C + 128 : 2 * C] = qk[:, 64:128]
    dwqkv[:, 2 * C : 2 * C + 128] = va
    dwqkv[:, 2 * C + 128 : 3 * C] = vp[:, 0:64]
    dwproj[:, 0:128] = pa
    dwproj[:, 128:C] = vp[:, 64:128]
    vec = rows(SMALL_ROW, 32)

    def load(row, width, ref, at=0):
        for n in range(0, width, 128):
            m = min(128, width - n)
            ref[at : at + 1, n : n + m] = vec[row + n // 128 : row + n // 128 + 1, 0:m]

    load(0, C, gain_grad, 0)
    load(2, C, gain_grad, 1)
    load(4, C, shift_grad, 0)
    load(6, C, shift_grad, 1)
    for row, ref in ((8, dbqkv), (13, dbproj), (15, db1), (21, db2)):
        width = ref.shape[0]
        for n in range(0, width, 128):
            m = min(128, width - n)
            ref[n : n + m] = vec[row + n // 128, 0:m]
    for h in range(HEADS):
        for t in range(NHI):
            n = h * 32 + t
            m = min(128, NBIAS - t * 128)
            dtable[0, h, :, t * 128 : t * 128 + m] = tgrad_ref[n // 6, n % 6 : n % 6 + 1, 0:m]


def on_device(
    grid,
    region_ids,
    cotangent,
    norm_gain,
    norm_shift,
    qkv_weight,
    qkv_bias,
    proj_weight,
    proj_bias,
    fc1_weight,
    fc1_bias,
    fc2_weight,
    fc2_bias,
    bias_table,
    pair_index,
):
    vmem = pl.BlockSpec(memory_space=pltpu.VMEM)
    shape = jax.ShapeDtypeStruct
    dma = pltpu.SemaphoreType.DMA
    hbm = pl.BlockSpec(memory_space=pltpu.HBM)
    send_sel, gather_sel, label_sel, send_out_sel, place_sel = selectors()
    by_tile = lambda field: field.transpose(1, 2, 0, 3)
    fields = (by_tile(grid), by_tile(cotangent), region_ids.transpose(1, 0, 2))
    table = bias_table.transpose(0, 2, 1, 3)
    passed = (
        norm_gain,
        norm_shift,
        qkv_weight,
        qkv_bias,
        proj_weight,
        proj_bias,
        fc1_weight,
        fc1_bias,
        fc2_weight.T,
        fc2_bias,
        send_out_sel,
        place_sel,
    )
    held = lambda a: pltpu.VMEM(a.shape, a.dtype)
    bias, win, index, *passed = pl.pallas_call(
        halo_kernel,
        out_shape=(
            shape((HEADS, TOK, TOK), F32),
            shape((2, TOK, 256), BF16),
            shape((TOK, TOK), jnp.int32),
            *(shape(a.shape, a.dtype) for a in passed),
        ),
        in_specs=[hbm] * (8 + PASSED),
        out_specs=(vmem,) * (3 + PASSED),
        scratch_shapes=[
            *map(held, fields),
            held(send_sel),
            held(label_sel),
            held(table),
            held(gather_sel),
            pltpu.VMEM((2, 288, 256), BF16),
            pltpu.VMEM((2, 144, 256), BF16),
            pltpu.VMEM((16, 64), F32),
            pltpu.VMEM((NHI, HEADS, 8, 128), F32),
            pltpu.VMEM((TOK, 256), jnp.int32),
            pltpu.VMEM((16, 256), jnp.int32),
            pltpu.VMEM((HEADS, 128, 256), F32),
            dma((3,)),
            dma((3,)),
            dma((8 + PASSED,)),
        ],
        name="halo_and_bias",
        compiler_params=pltpu.CompilerParams(
            collective_id=0, has_side_effects=True, vmem_limit_bytes=32 * 1024 * 1024
        ),
    )(
        *(
            pltpu.with_memory_space_constraint(a, pltpu.HBM)
            for a in (*fields, send_sel, label_sel, table, pair_index, gather_sel, *passed)
        )
    )
    out, din, full, tgrad = pl.pallas_call(
        main_kernel,
        out_shape=(
            shape((TOK, C), BF16),
            shape((TOK, C), BF16),
            shape((2, 16, OWNED, 128), BF16),
            shape((32, 6, 128), F32),
        ),
        in_specs=[vmem] * 15,
        out_specs=(vmem,) * 4,
        scratch_shapes=[
            pltpu.VMEM((2, 288, 256), BF16),
            pltpu.VMEM((2, 144, 256), BF16),
            pltpu.VMEM((HEADS, TOK, TOK), F32),
            pltpu.VMEM((TOK, FF), BF16),
            pltpu.VMEM((TOK, FF), F32),
            pltpu.VMEM((HEADS, TOK, 256), F32),
            pltpu.VMEM((32, 128), F32),
            pltpu.VMEM((ROWS, 128), BF16),
            pltpu.VMEM((1024, 128), BF16),
            pltpu.VMEM((768, 128), BF16),
            pltpu.VMEM((16, 64, 128), BF16),
            pltpu.VMEM((16, 48, 128), BF16),
            pltpu.VMEM((2, 16, 4, 128), F32),
            pltpu.VMEM((2, 16, 4, 128), F32),
            pltpu.VMEM((2, 16, 4, 128), F32),
            pltpu.VMEM((64, 128), F32),
            pltpu.VMEM((32, 6, 128), F32),
            pltpu.VMEM((32, 6, 128), F32),
            dma((2, 3)),
            dma((2, 3)),
            dma((2,)),
            dma((2,)),
            dma((2, 16)),
            dma((2, 16)),
            dma((2, 16)),
            dma((2, 16)),
            dma((2, 16)),
            dma((2, 16)),
            dma((32,)),
            dma((32,)),
            dma((32,)),
            dma((32,)),
            dma((2, 16)),
            dma((2, 16)),
            dma((2, 16)),
            dma((2, 16)),
        ],
        name="window_block",
        compiler_params=pltpu.CompilerParams(
            collective_id=1, has_side_effects=True, vmem_limit_bytes=48 * 1024 * 1024
        ),
    )(
        win,
        *passed[0:10],
        bias,
        index,
        *passed[10:],
    )
    outs = pl.pallas_call(
        final_kernel,
        out_shape=(
            shape((6, 12, 2, C), BF16),
            shape((6, 12, 2, C), BF16),
            shape((2, C), F32),
            shape((2, C), F32),
            shape((C, 3 * C), F32),
            shape((3 * C,), F32),
            shape((C, C), F32),
            shape((C,), F32),
            shape((C, FF), F32),
            shape((FF,), F32),
            shape((C, FF), F32),
            shape((C,), F32),
            shape((1, HEADS, 1, NBIAS), F32),
        ),
        in_specs=[vmem] * 4,
        out_specs=(vmem,) * 13,
        name="outputs",
        compiler_params=pltpu.CompilerParams(vmem_limit_bytes=32 * 1024 * 1024),
    )(out, din, full, tgrad)
    outs = list(outs)
    for n in (0, 1):
        outs[n] = outs[n].transpose(2, 0, 1, 3)
    outs[10] = outs[10].T
    outs[12] = outs[12].transpose(0, 2, 1, 3)
    return tuple(outs)


def solution(mesh):
    field = P(None, "lat", "lon", None)
    table = P(None, "lat", None, None)
    return jax.shard_map(
        on_device,
        mesh=mesh,
        in_specs=(field, P(None, "lat", "lon"), field) + (P(),) * 10 + (table, P()),
        out_specs=(field, field) + (P(),) * 10 + (table,),
        check_vma=False,
    )
```

```python
import math

import jax
import jax.numpy as jnp
import numpy as np
from jax import lax
from jax.experimental import pallas as pl
from jax.experimental.pallas import tpu as pltpu
from jax.sharding import PartitionSpec as P

F32 = jnp.float32
BF16 = jnp.bfloat16
MESH = pl.DeviceIdType.MESH

C = 192
HEADS = 6
HEAD = 32
FF = 768
TOK = 144
NBIAS = 3312
NHI = 26
NEG_FILL = -1e30
NORM_EPS = 1e-05
ROOT_HALF = 1.0 / math.sqrt(2.0)
ROOT_TWOPI = 1.0 / math.sqrt(2.0 * math.pi)
SCALE = HEAD ** (-0.5)

ROWS = 3584
FC2_ROW = 0
FC1_ROW = 1152
QP_ROW = 2304
SMALL_ROW = 3456
CHUNKS = ((0, 64), (2048, 48))
OWNED = 112
STEPS = (
    ((1, 0), (3, 0), (0, 1), (0, 3))
    + ((1, 1), (1, 3), (3, 1), (3, 3), (2, 0), (0, 2))
    + ((2, 1), (2, 3), (1, 2), (3, 2), (2, 2))
)
PASSED = 12


def dot(a, b, ca=1, cb=0):
    return lax.dot_general(a, b, (((ca,), (cb,)), ((), ())), preferred_element_type=F32)


def selectors():
    held = lambda l, r, q: (r * 12 + q) * 2 + l
    send = np.zeros((144, 144), np.float32)
    gather = np.zeros((144, 288), np.float32)
    send_out = np.zeros((144, 144), np.float32)
    place = np.zeros((144, 288), np.float32)
    label = np.zeros((144, 16), np.float32)
    for l in range(2):
        for i in range(6):
            for j in range(12):
                label[held(l, i, j), i * 2 + l] = 1
                tok = l * 72 + i * 12 + j
                lev = (l + 1) % 2
                far_i, far_j = i >= 3, j >= 6
                r = i - 3 if far_i else i + 3
                q = j - 6 if far_j else j + 6
                if not far_i and not far_j:
                    gather[tok, held(lev, r, q)] = 1
                    place[held(lev, r, q), tok] = 1
                    continue
                d = 2 if (far_i and far_j) else (1 if far_i else 0)
                m = d * 48 + l * 18 + (i % 3) * 6 + (j % 6)
                send[m, held(lev, r, q)] = 1
                gather[tok, 144 + m] = 1
                send_out[m, tok] = 1
                place[held(lev, r, q), 144 + m] = 1
    return [jnp.asarray(a, BF16) for a in (send, gather, label, send_out, place)]


def look_up_bias(table_ref, index_ref, bias_ref, tab, idx, idx_t, left):
    for h in range(HEADS):
        for t in range(NHI):
            n = min(128, NBIAS - t * 128)
            row = table_ref[0, h, :, t * 128 : t * 128 + n]
            if n < 128:
                row = jnp.concatenate([row, jnp.zeros((1, 128 - n), F32)], 1)
            tab[t, h] = jnp.broadcast_to(row, (8, 128))
    idx[...] = jnp.zeros_like(idx)
    idx[:, 0:TOK] = index_ref[...]
    tail = idx[:, 128:256].astype(F32).T
    idx_t[:, 0:TOK] = tail[0:16].astype(jnp.int32)
    idx_t[:, TOK:256] = jnp.zeros((16, 256 - TOK), jnp.int32)
    left[...] = jnp.zeros_like(left)

    def look(flat, store):
        lo = flat & 127
        hi = flat >> 7
        acc = [jnp.zeros((8, 128), F32)] * HEADS
        for t in range(NHI):
            here = hi == t
            for h in range(HEADS):
                got = jnp.take_along_axis(tab[t, h], lo, axis=1, mode="promise_in_bounds")
                acc[h] = jnp.where(here, got, acc[h])
        for h in range(HEADS):
            store(h, acc[h])

    def body(b, carry):
        at = pl.multiple_of(b * 8, 8)

        def store(h, acc):
            bias_ref[h, pl.ds(at, 8), 0:128] = acc

        look(idx[pl.ds(at, 8), 0:128], store)
        return carry

    lax.fori_loop(0, TOK // 8, body, 0)
    for a in range(2):
        for t in range(2):

            def store(h, acc, a=a, t=t):
                left[h, a * 8 : a * 8 + 8, t * 128 : (t + 1) * 128] = acc

            look(idx_t[a * 8 : a * 8 + 8, t * 128 : (t + 1) * 128], store)
    for h in range(HEADS):
        bias_ref[h, :, 128:TOK] = left[h].T[0:TOK, 0:16]


def rem(a, b):
    return lax.rem(a, b)


def half(a):
    return lax.div(a, 2)


def around():
    lat = lax.axis_index("lat")
    lon = lax.axis_index("lon")
    return lat, lon, rem(lat + 1, 16), rem(lat + 15, 16), rem(lon + 1, 32), rem(lon + 31, 32)


def greet(device):
    pl.semaphore_signal(pltpu.get_barrier_semaphore(), inc=1, device_id=device, device_id_type=MESH)


def greet_halo():
    lat, lon, lat_up, lat_dn, lon_up, lon_dn = around()
    for device in (
        (lat_up, lon),
        (lat_dn, lon),
        (lat, lon_up),
        (lat, lon_dn),
        (lat_up, lon_up),
        (lat_dn, lon_dn),
    ):
        greet(device)


def halo_kernel(*refs):
    grid_hbm, cot_hbm, ids_hbm, send_hbm, label_hbm, table_hbm, index_hbm, gather_hbm = refs[0:8]
    weights_hbm = refs[8 : 8 + PASSED]
    bias_ref, win_ref, index_ref = refs[8 + PASSED : 11 + PASSED]
    weights_ref = refs[11 + PASSED : 11 + 2 * PASSED]
    (
        grid_ref,
        cot_ref,
        ids_ref,
        send_sel,
        label_sel,
        table_ref,
        gather_sel,
        stack,
        halo_msg,
        labels,
        tab,
        idx,
        idx_t,
        left,
        halo_s,
        halo_r,
        load_s,
    ) = refs[11 + 2 * PASSED :]
    loads = [
        pltpu.make_async_copy(src, dst, load_s.at[n])
        for n, (src, dst) in enumerate(
            (
                (grid_hbm, grid_ref),
                (cot_hbm, cot_ref),
                (ids_hbm, ids_ref),
                (send_hbm, send_sel),
                (label_hbm, label_sel),
                (table_hbm, table_ref),
                (index_hbm, index_ref),
                (gather_hbm, gather_sel),
                *zip(weights_hbm, weights_ref),
            )
        )
    ]
    for load in loads[0:8]:
        load.start()
    lat, lon, lat_up, lat_dn, lon_up, lon_dn = around()
    greet_halo()
    for load in loads[8:]:
        load.start()
    for load in loads[0:5]:
        load.wait()
    labels[...] = jnp.zeros_like(labels)
    for r in range(6):
        labels[2 * r : 2 * r + 2, :] = jnp.broadcast_to(ids_ref[r, :, 0:1].astype(F32), (2, 64))
    stack[0, 0:TOK, C:256] = dot(label_sel[...], labels[...].astype(BF16)).astype(BF16)
    stack[1, 0:TOK, C:256] = jnp.zeros((TOK, 64), BF16)
    for r in range(6):
        for q in range(12):
            at = (r * 12 + q) * 2
            stack[0, at : at + 2, 0:C] = grid_ref[r, q]
            stack[1, at : at + 2, 0:C] = cot_ref[r, q]
    for n in range(2):
        halo_msg[n] = dot(send_sel[...], stack[n, 0:TOK, :]).astype(BF16)
    pl.semaphore_wait(pltpu.get_barrier_semaphore(), 6)
    halo_to = ((lat, lon_dn), (lat_dn, lon), (lat_dn, lon_dn))
    halo = [
        pltpu.make_async_remote_copy(
            src_ref=halo_msg.at[:, d * 48 : (d + 1) * 48, :],
            dst_ref=stack.at[:, TOK + d * 48 : TOK + (d + 1) * 48, :],
            send_sem=halo_s.at[d],
            recv_sem=halo_r.at[d],
            device_id=halo_to[d],
            device_id_type=MESH,
        )
        for d in range(3)
    ]
    for copy in halo:
        copy.start()
    for load in loads[5:8]:
        load.wait()
    look_up_bias(table_ref, index_ref, bias_ref, tab, idx, idx_t, left)
    for load in loads[8:]:
        load.wait()
    for copy in halo:
        copy.wait()
    for n in range(2):
        win_ref[n] = dot(gather_sel[...], stack[n]).astype(BF16)


def layer_norm(values, gain_row, shift_row):
    centred = values - jnp.mean(values, -1, keepdims=True)
    inv_std = lax.rsqrt(jnp.mean(centred * centred, -1, keepdims=True) + NORM_EPS)
    normed = centred * inv_std
    return normed * gain_row + shift_row, normed, inv_std


def norm_back(incoming, normed, inv_std, gain_row):
    scaled = incoming * gain_row
    outgoing = inv_std * (
        scaled
        - jnp.mean(scaled, -1, keepdims=True)
        - normed * jnp.mean(scaled * normed, -1, keepdims=True)
    )
    return (
        outgoing,
        jnp.sum(incoming * normed, 0, keepdims=True),
        jnp.sum(incoming, 0, keepdims=True),
    )


def main_kernel(
    win_ref,
    gain_ref,
    shift_ref,
    wqkv_ref,
    bqkv_ref,
    wproj_ref,
    bproj_ref,
    w1_ref,
    b1_ref,
    w2_ref,
    b2_ref,
    bias_ref,
    index_ref,
    send_out_sel,
    place_sel,
    out_ref,
    din_ref,
    full_ref,
    tgrad_ref,
    out_stack,
    out_msg,
    probs,
    act,
    dfac,
    dsc,
    small,
    grads,
    core_in1,
    core_in2,
    plane_in1,
    plane_in2,
    z_out,
    z_in,
    z_all,
    owned,
    t_out,
    t_in,
    oh_s,
    oh_r,
    core_s,
    core_r,
    plane_s,
    plane_r,
    zs,
    zr,
    zgs,
    zgr,
    ts,
    tr,
    tgs,
    tgr,
    ags,
    agr,
    fs,
    fr,
):
    lat, lon, lat_up, lat_dn, lon_up, lon_dn = around()
    core = rem(lat, 2)
    pair_lat = lat + 1 - 2 * core
    ylo = rem(lon, 2)
    z = half(lon)
    k = half(lat) * 2 + ylo

    def plane_device(kk):
        return (half(kk) * 2 + core, z * 2 + rem(kk, 2))

    def each(first_d, last_d, body):
        def step(d, carry):
            body(d)
            return carry

        lax.fori_loop(first_d, last_d, step, 0, unroll=True)

    def far_first(count, body):
        first, last = count // 2 - 3, count // 2 + 4
        each(first, last, body)
        each(1, first, body)
        each(last, count, body)

    far_first(32, lambda d: greet((lat, rem(lon + d, 32))))
    each(1, 16, lambda d: greet(plane_device(rem(k + d, 16))))
    greet((pair_lat, lon))
    greet_halo()

    x = win_ref[0, :, 0:C].astype(F32)
    g_b = win_ref[1, :, 0:C]
    label_lane = win_ref[0, :, 128:256]
    pick = (lax.broadcasted_iota(jnp.int32, (8, 128), 1) == 64).astype(F32).astype(BF16)
    ids_row = dot(pick, label_lane, 1, 1)[0:1]
    ids_col = label_lane[:, 64:65].astype(F32)
    allowed = ids_row == ids_col

    gain0, gain1 = gain_ref[0:1, :], gain_ref[1:2, :]
    shift0, shift1 = shift_ref[0:1, :], shift_ref[1:2, :]
    first, hat1, inv1 = layer_norm(x, gain0, shift0)
    first_b = first.astype(BF16)
    bqkv = bqkv_ref[...].reshape(1, 3 * C)
    b1 = b1_ref[...].reshape(1, FF)
    wq = wqkv_ref[:, 0:C]
    wk = wqkv_ref[:, C : 2 * C]
    wv = wqkv_ref[:, 2 * C : 3 * C]
    q = (dot(first_b, wq) + bqkv[:, 0:C]).astype(BF16)
    key = (dot(first_b, wk) + bqkv[:, C : 2 * C]).astype(BF16)
    v = (dot(first_b, wv) + bqkv[:, 2 * C : 3 * C]).astype(BF16)
    lane = lax.broadcasted_iota(jnp.int32, (TOK, C), 1)

    def only(h, values):
        return jnp.where((lane >> 5) == h, values, jnp.zeros_like(values))

    mixed = jnp.zeros((TOK, C), F32)
    for h in range(HEADS):
        s = dot(only(h, q), key, 1, 1) * SCALE + bias_ref[h]
        s = jnp.where(allowed, s, NEG_FILL)
        e = jnp.exp(s - jnp.max(s, -1, keepdims=True))
        p = e * (1.0 / jnp.sum(e, -1, keepdims=True))
        probs[h] = p
        mixed = mixed + dot(p.astype(BF16), only(h, v))
    mixed_b = mixed.astype(BF16)
    attended = x + dot(mixed_b, wproj_ref[...]) + bproj_ref[...].reshape(1, C)

    second, hat2, inv2 = layer_norm(attended, gain1, shift1)
    second_b = second.astype(BF16)
    for b in range(FF // 128):
        cols = slice(b * 128, (b + 1) * 128)
        hidden = dot(second_b, w1_ref[:, cols]) + b1[:, cols]
        cumul = 0.5 * (1.0 + lax.erf(hidden * ROOT_HALF))
        act[:, cols] = (hidden * cumul).astype(BF16)
        dfac[:, cols] = cumul + hidden * jnp.exp(-0.5 * hidden * hidden) * ROOT_TWOPI
    result = (attended + dot(act[...], w2_ref[...], 1, 1) + b2_ref[...].reshape(1, C)).astype(BF16)

    halo_out_to = ((lat, lon_up), (lat_up, lon), (lat_up, lon_up))

    def send_back(n, values):
        out_stack[n, 0:TOK, 0:C] = values
        out_msg[n, :, 0:C] = dot(send_out_sel[...], values).astype(BF16)
        copies = [
            pltpu.make_async_remote_copy(
                src_ref=out_msg.at[n, d * 48 : (d + 1) * 48, :],
                dst_ref=out_stack.at[n, TOK + d * 48 : TOK + (d + 1) * 48, :],
                send_sem=oh_s.at[n, d],
                recv_sem=oh_r.at[n, d],
                device_id=halo_out_to[d],
                device_id_type=MESH,
            )
            for d in range(3)
        ]
        for copy in copies:
            copy.start()
        return copies

    small[...] = jnp.zeros_like(small)

    def keep(row, vector):
        width = vector.shape[1]
        for at in range(0, width, 128):
            n = min(128, width - at)
            small[row + at // 128 : row + at // 128 + 1, 0:n] = vector[:, at : at + n]

    gf = g_b.astype(F32)
    keep(21, jnp.sum(gf, 0, keepdims=True))
    d_second = jnp.zeros((TOK, C), F32)
    for b in range(FF // 128):
        cols = slice(b * 128, (b + 1) * 128)
        grads[FC2_ROW + b * C : FC2_ROW + (b + 1) * C, :] = dot(g_b, act[:, cols], 0, 0).astype(BF16)
        d_hidden = dot(g_b, w2_ref[:, cols]) * dfac[:, cols]
        d_hidden_b = d_hidden.astype(BF16)
        keep(15 + b, jnp.sum(d_hidden, 0, keepdims=True))
        grads[FC1_ROW + b * C : FC1_ROW + (b + 1) * C, :] = dot(second_b, d_hidden_b, 0, 0).astype(BF16)
        d_second = d_second + dot(d_hidden_b, w1_ref[:, cols], 1, 1)

    z_out[...] = jnp.zeros_like(z_out)
    core_in = (core_in1, core_in2)
    plane_in = (plane_in1, plane_in2)

    def core_copy(n):
        base, rows = CHUNKS[n]
        return pltpu.make_async_remote_copy(
            src_ref=grads.at[pl.ds(pl.multiple_of(base + (1 - core) * 16 * rows, 16), 16 * rows), :],
            dst_ref=core_in[n],
            send_sem=core_s.at[n],
            recv_sem=core_r.at[n],
            device_id=(pair_lat, lon),
            device_id_type=MESH,
        )

    def plane_copy(n, d):
        base, rows = CHUNKS[n]
        kk = rem(k + d, 16)
        return pltpu.make_async_remote_copy(
            src_ref=grads.at[pl.ds(pl.multiple_of(base + (core * 16 + kk) * rows, 16), rows), :],
            dst_ref=plane_in[n].at[d],
            send_sem=plane_s.at[n, d],
            recv_sem=plane_r.at[n, d],
            device_id=plane_device(kk),
            device_id_type=MESH,
        )

    def z_device(d):
        return (lat, rem(z + d, 16) * 2 + ylo)

    def z_copy(n, d):
        return pltpu.make_async_remote_copy(
            src_ref=z_out.at[n, rem(z + d, 16)],
            dst_ref=z_in.at[n, d],
            send_sem=zs.at[n, d],
            recv_sem=zr.at[n, d],
            device_id=z_device(d),
            device_id_type=MESH,
        )

    def z_gather(n, d):
        return pltpu.make_async_remote_copy(
            src_ref=z_all.at[n, z],
            dst_ref=z_all.at[n, z],
            send_sem=zgs.at[n, d],
            recv_sem=zgr.at[n, d],
            device_id=z_device(d),
            device_id_type=MESH,
        )

    def owner_rows(n):
        return slice(0, 64) if n == 0 else slice(64, OWNED)

    x_at, y_at = rem(half(lat), 4), lax.div(lat, 8) * 2 + ylo

    def plane_gather(n, d):
        xx, yy = rem(x_at + STEPS[d][0], 4), rem(y_at + STEPS[d][1], 4)
        return pltpu.make_async_remote_copy(
            src_ref=full_ref.at[core, k, owner_rows(n)],
            dst_ref=full_ref.at[core, k, owner_rows(n)],
            send_sem=ags.at[n, d],
            recv_sem=agr.at[n, d],
            device_id=((half(yy) * 4 + xx) * 2 + core, z * 2 + rem(yy, 2)),
            device_id_type=MESH,
        )

    def forward(n, d):
        dx, dy = STEPS[d] if d < 15 else (0, 0)
        xx, yy = rem(x_at + 4 - dx, 4), rem(y_at + 4 - dy, 4)
        kk = (half(yy) * 4 + xx) * 2 + rem(yy, 2)
        return pltpu.make_async_remote_copy(
            src_ref=full_ref.at[core, kk, owner_rows(n)],
            dst_ref=full_ref.at[core, kk, owner_rows(n)],
            send_sem=fs.at[n, d],
            recv_sem=fr.at[n, d],
            device_id=(pair_lat, lon),
            device_id_type=MESH,
        )

    def scatter_plane(n):
        base, rows = CHUNKS[n]
        core_copy(n).wait()
        mine = pl.ds(pl.multiple_of(base + core * 16 * rows, 16), 16 * rows)
        grads[mine, :] = (grads[mine, :].astype(F32) + core_in[n][...].astype(F32)).astype(BF16)
        each(1, 16, lambda d: plane_copy(n, d).start())

    def plane_total(n):
        base, rows = CHUNKS[n]
        each(1, 16, lambda d: plane_copy(n, d).wait())
        total = grads[pl.ds(pl.multiple_of(base + (core * 16 + k) * rows, 16), rows), :].astype(F32)
        for d in range(1, 16):
            total = total + plane_in[n][d].astype(F32)
        return total

    def scatter_z(n):
        per = CHUNKS[n][1] // 16
        total = plane_total(n)
        for m in range(16):
            z_out[n, m, 0:per] = total[m * per : (m + 1) * per]
        far_first(16, lambda d: z_copy(n, d).start())

    def gather_z(n):
        each(1, 16, lambda d: z_copy(n, d).wait())
        total = z_out[n, z]
        for d in range(1, 16):
            total = total + z_in[n, d]
        z_all[n, z] = total
        far_first(16, lambda d: z_gather(n, d).start())

    def gather_plane(n):
        rows = CHUNKS[n][1]
        per = rows // 16
        each(1, 16, lambda d: z_gather(n, d).wait())
        for m in range(16):
            owned[m * per : (m + 1) * per, :] = z_all[n, m, 0:per]
        full_ref[core, k, owner_rows(n)] = owned[0:rows, :].astype(BF16)
        for d in reversed(range(15)):
            plane_gather(n, d).start()
        forward(n, 15).start()

    def pass_on(n):
        for d in range(15):
            plane_gather(n, d).wait()
            forward(n, d).start()

    back2, dgain1, dshift1 = norm_back(d_second, hat2, inv2, gain1)
    keep(2, dgain1)
    keep(6, dshift1)
    d_att = gf + back2
    d_att_b = d_att.astype(BF16)

    def put_pair(at, left, right):
        grads[at : at + C, :] = left[:, 0:128].astype(BF16)
        grads[at + C : at + 2 * C, :] = right[:, 0:128].astype(BF16)
        grads[at + 2 * C : at + 3 * C, :] = jnp.concatenate([left[:, 128:C], right[:, 128:C]], 1).astype(BF16)

    dw_proj = dot(mixed_b, d_att_b, 0, 0)
    keep(13, jnp.sum(d_att, 0, keepdims=True))
    dm = dot(d_att_b, wproj_ref[...], 1, 1).astype(BF16)

    dq = jnp.zeros((TOK, C), F32)
    dk = jnp.zeros((TOK, C), F32)
    dv = jnp.zeros((TOK, C), F32)
    for h in range(HEADS):
        p = probs[h]
        dm_h = only(h, dm)
        dp = dot(dm_h, v, 1, 1)
        ds = p * (dp - jnp.sum(dp * p, -1, keepdims=True))
        dsc[h, :, 0:128] = ds[:, 0:128]
        dsc[h, :, 128:256] = jnp.concatenate([ds[:, 128:TOK], jnp.zeros((TOK, 112), F32)], 1)
        ds_b = (ds * SCALE).astype(BF16)
        dq = dq + dot(ds_b, only(h, key))
        dk = dk + dot(ds_b, only(h, q), 0, 0)
        dv = dv + dot(p.astype(BF16), dm_h, 0, 0)
    dq_b, dk_b, dv_b = dq.astype(BF16), dk.astype(BF16), dv.astype(BF16)
    pl.semaphore_wait(pltpu.get_barrier_semaphore(), 53)
    core_copy(0).start()
    put_pair(QP_ROW, dot(first_b, dq_b, 0, 0), dot(first_b, dk_b, 0, 0))
    put_pair(QP_ROW + 3 * C, dot(first_b, dv_b, 0, 0), dw_proj)
    d_bias = jnp.concatenate(
        [jnp.sum(dq, 0, keepdims=True), jnp.sum(dk, 0, keepdims=True), jnp.sum(dv, 0, keepdims=True)], 1
    )
    keep(8, d_bias)
    d_first = dot(dq_b, wq, 1, 1) + dot(dk_b, wk, 1, 1) + dot(dv_b, wv, 1, 1)
    back1, dgain0, dshift0 = norm_back(d_first, hat1, inv1, gain0)
    keep(0, dgain0)
    keep(4, dshift0)
    grads[SMALL_ROW : SMALL_ROW + 32, :] = small[...].astype(BF16)
    grads[SMALL_ROW + 32 : ROWS, :] = jnp.zeros((ROWS - SMALL_ROW - 32, 128), BF16)
    core_copy(1).start()
    scatter_plane(0)
    scatter_plane(1)
    out_copies = send_back(0, result)
    din_copies = send_back(1, (d_att + back1).astype(BF16))

    hi_iota = lax.broadcasted_iota(jnp.int32, (32, 256), 0).astype(F32).astype(BF16)
    lo_iota = lax.broadcasted_iota(jnp.int32, (128, 256), 0).astype(F32).astype(BF16)

    def spread(row, count):
        return jnp.concatenate([jnp.broadcast_to(row, (16, row.shape[1])).astype(BF16)] * (count // 16), 0)

    def factors(flat, rows):
        width = flat.shape[1]
        is_hi = hi_iota[:, 0:width] == spread((flat >> 7).astype(F32), 32)
        is_lo = lo_iota[:, 0:width] == spread((flat & 127).astype(F32), 128)
        zero = jnp.zeros((), BF16)
        left = jnp.concatenate([jnp.where(is_hi, spread(row, 32), zero) for row in rows], 0)
        return left, jnp.where(is_lo, jnp.ones((), BF16), zero)

    def pairs(b, total):
        block = pl.ds(pl.multiple_of(b * 8, 8), 8)
        flat = index_ref[block, 0:128]
        rows = [dsc[h, block, 0:128] for h in range(HEADS)]
        two = lambda values, r: jnp.concatenate([values[r : r + 1], values[r + 1 : r + 2]], 1)
        parts = [factors(two(flat, r), [two(values, r) for values in rows]) for r in range(0, 8, 2)]
        left = jnp.concatenate([part[0] for part in parts], 1)
        right = jnp.concatenate([part[1] for part in parts], 1)
        return total + dot(left, right, 1, 1)

    table = lax.fori_loop(0, 11, pairs, jnp.zeros((HEADS * 32, 128), F32))
    scatter_z(0)
    table = lax.fori_loop(11, 14, pairs, table)
    scatter_z(1)
    table = lax.fori_loop(14, TOK // 8, pairs, table)
    flat_tail = jnp.concatenate([index_ref[:, 128:TOK].astype(F32), jnp.zeros((TOK, 112), F32)], 1).T[0:16]
    flat_tail = flat_tail.astype(jnp.int32)
    ds_tail = [dsc[h, :, 128:256].T for h in range(HEADS)]
    for r in range(16):
        table = table + dot(*factors(flat_tail[r : r + 1], [t[r : r + 1] for t in ds_tail]), 1, 1)
    for n in range(32):
        t_out[n] = table[n * 6 : (n + 1) * 6]

    def t_copy(d):
        to = rem(lon + d, 32)
        return pltpu.make_async_remote_copy(
            src_ref=t_out.at[to],
            dst_ref=t_in.at[d],
            send_sem=ts.at[d],
            recv_sem=tr.at[d],
            device_id=(lat, to),
            device_id_type=MESH,
        )

    def t_gather(d):
        return pltpu.make_async_remote_copy(
            src_ref=tgrad_ref.at[lon],
            dst_ref=tgrad_ref.at[lon],
            send_sem=tgs.at[d],
            recv_sem=tgr.at[d],
            device_id=(lat, rem(lon + d, 32)),
            device_id_type=MESH,
        )

    far_first(32, lambda d: t_copy(d).start())
    gather_z(0)
    gather_z(1)
    each(1, 32, lambda d: t_copy(d).wait())
    t_total = t_out[lon]
    for d in range(1, 32):
        t_total = t_total + t_in[d]
    tgrad_ref[lon] = t_total
    far_first(32, lambda d: t_gather(d).start())
    gather_plane(0)
    gather_plane(1)
    for n, copies, ref in ((0, out_copies, out_ref), (1, din_copies, din_ref)):
        for copy in copies:
            copy.wait()
        ref[...] = dot(place_sel[...], out_stack[n, :, 0:C]).astype(BF16)
    pass_on(0)
    pass_on(1)
    each(1, 32, lambda d: t_gather(d).wait())
    for n in range(2):
        for d in range(16):
            forward(n, d).wait()


def final_kernel(
    out_ref,
    din_ref,
    full_ref,
    tgrad_ref,
    output,
    grid_grad,
    gain_grad,
    shift_grad,
    dwqkv,
    dbqkv,
    dwproj,
    dbproj,
    dw1,
    db1,
    dw2,
    db2,
    dtable,
):
    for r in range(6):
        for q in range(12):
            at = (r * 12 + q) * 2
            output[r, q] = out_ref[at : at + 2, :]
            grid_grad[r, q] = din_ref[at : at + 2, :]

    def rows(start, count):
        parts = []
        at = start
        while at < start + count:
            n = 0 if at < CHUNKS[1][0] else 1
            base, size = CHUNKS[n]
            owner, inside = divmod(at - base, size)
            take = min(size - inside, start + count - at)
            first = inside + (0 if n == 0 else CHUNKS[0][1])
            parts.append(full_ref[owner // 16, owner % 16, first : first + take, :])
            at += take
        return jnp.concatenate(parts, 0).astype(F32) if len(parts) > 1 else parts[0].astype(F32)

    for b in range(FF // 128):
        cols = slice(b * 128, (b + 1) * 128)
        dw2[:, cols] = rows(FC2_ROW + b * C, C)
        dw1[:, cols] = rows(FC1_ROW + b * C, C)
    qa, ka, qk = (rows(QP_ROW + n * C, C) for n in range(3))
    va, pa, vp = (rows(QP_ROW + n * C, C) for n in range(3, 6))
    dwqkv[:, 0:128] = qa
    dwqkv[:, 128:C] = qk[:, 0:64]
    dwqkv[:, C : C + 128] = ka
    dwqkv[:, C + 128 : 2 * C] = qk[:, 64:128]
    dwqkv[:, 2 * C : 2 * C + 128] = va
    dwqkv[:, 2 * C + 128 : 3 * C] = vp[:, 0:64]
    dwproj[:, 0:128] = pa
    dwproj[:, 128:C] = vp[:, 64:128]
    vec = rows(SMALL_ROW, 32)

    def load(row, width, ref, at=0):
        for n in range(0, width, 128):
            m = min(128, width - n)
            ref[at : at + 1, n : n + m] = vec[row + n // 128 : row + n // 128 + 1, 0:m]

    load(0, C, gain_grad, 0)
    load(2, C, gain_grad, 1)
    load(4, C, shift_grad, 0)
    load(6, C, shift_grad, 1)
    for row, ref in ((8, dbqkv), (13, dbproj), (15, db1), (21, db2)):
        width = ref.shape[0]
        for n in range(0, width, 128):
            m = min(128, width - n)
            ref[n : n + m] = vec[row + n // 128, 0:m]
    for h in range(HEADS):
        for t in range(NHI):
            n = h * 32 + t
            m = min(128, NBIAS - t * 128)
            dtable[0, h, :, t * 128 : t * 128 + m] = tgrad_ref[n // 6, n % 6 : n % 6 + 1, 0:m]


def on_device(
    grid,
    region_ids,
    cotangent,
    norm_gain,
    norm_shift,
    qkv_weight,
    qkv_bias,
    proj_weight,
    proj_bias,
    fc1_weight,
    fc1_bias,
    fc2_weight,
    fc2_bias,
    bias_table,
    pair_index,
):
    vmem = pl.BlockSpec(memory_space=pltpu.VMEM)
    shape = jax.ShapeDtypeStruct
    dma = pltpu.SemaphoreType.DMA
    hbm = pl.BlockSpec(memory_space=pltpu.HBM)
    send_sel, gather_sel, label_sel, send_out_sel, place_sel = selectors()
    by_tile = lambda field: field.transpose(1, 2, 0, 3)
    fields = (by_tile(grid), by_tile(cotangent), region_ids.transpose(1, 0, 2))
    table = bias_table.transpose(0, 2, 1, 3)
    passed = (
        norm_gain,
        norm_shift,
        qkv_weight,
        qkv_bias,
        proj_weight,
        proj_bias,
        fc1_weight,
        fc1_bias,
        fc2_weight.T,
        fc2_bias,
        send_out_sel,
        place_sel,
    )
    held = lambda a: pltpu.VMEM(a.shape, a.dtype)
    bias, win, index, *passed = pl.pallas_call(
        halo_kernel,
        out_shape=(
            shape((HEADS, TOK, TOK), F32),
            shape((2, TOK, 256), BF16),
            shape((TOK, TOK), jnp.int32),
            *(shape(a.shape, a.dtype) for a in passed),
        ),
        in_specs=[hbm] * (8 + PASSED),
        out_specs=(vmem,) * (3 + PASSED),
        scratch_shapes=[
            *map(held, fields),
            held(send_sel),
            held(label_sel),
            held(table),
            held(gather_sel),
            pltpu.VMEM((2, 288, 256), BF16),
            pltpu.VMEM((2, 144, 256), BF16),
            pltpu.VMEM((16, 64), F32),
            pltpu.VMEM((NHI, HEADS, 8, 128), F32),
            pltpu.VMEM((TOK, 256), jnp.int32),
            pltpu.VMEM((16, 256), jnp.int32),
            pltpu.VMEM((HEADS, 128, 256), F32),
            dma((3,)),
            dma((3,)),
            dma((8 + PASSED,)),
        ],
        name="halo_and_bias",
        compiler_params=pltpu.CompilerParams(
            collective_id=0, has_side_effects=True, vmem_limit_bytes=32 * 1024 * 1024
        ),
    )(
        *(
            pltpu.with_memory_space_constraint(a, pltpu.HBM)
            for a in (*fields, send_sel, label_sel, table, pair_index, gather_sel, *passed)
        )
    )
    out, din, full, tgrad = pl.pallas_call(
        main_kernel,
        out_shape=(
            shape((TOK, C), BF16),
            shape((TOK, C), BF16),
            shape((2, 16, OWNED, 128), BF16),
            shape((32, 6, 128), F32),
        ),
        in_specs=[vmem] * 15,
        out_specs=(vmem,) * 4,
        scratch_shapes=[
            pltpu.VMEM((2, 288, 256), BF16),
            pltpu.VMEM((2, 144, 256), BF16),
            pltpu.VMEM((HEADS, TOK, TOK), F32),
            pltpu.VMEM((TOK, FF), BF16),
            pltpu.VMEM((TOK, FF), F32),
            pltpu.VMEM((HEADS, TOK, 256), F32),
            pltpu.VMEM((32, 128), F32),
            pltpu.VMEM((ROWS, 128), BF16),
            pltpu.VMEM((1024, 128), BF16),
            pltpu.VMEM((768, 128), BF16),
            pltpu.VMEM((16, 64, 128), BF16),
            pltpu.VMEM((16, 48, 128), BF16),
            pltpu.VMEM((2, 16, 4, 128), F32),
            pltpu.VMEM((2, 16, 4, 128), F32),
            pltpu.VMEM((2, 16, 4, 128), F32),
            pltpu.VMEM((64, 128), F32),
            pltpu.VMEM((32, 6, 128), F32),
            pltpu.VMEM((32, 6, 128), F32),
            dma((2, 3)),
            dma((2, 3)),
            dma((2,)),
            dma((2,)),
            dma((2, 16)),
            dma((2, 16)),
            dma((2, 16)),
            dma((2, 16)),
            dma((2, 16)),
            dma((2, 16)),
            dma((32,)),
            dma((32,)),
            dma((32,)),
            dma((32,)),
            dma((2, 16)),
            dma((2, 16)),
            dma((2, 16)),
            dma((2, 16)),
        ],
        name="window_block",
        compiler_params=pltpu.CompilerParams(
            collective_id=1, has_side_effects=True, vmem_limit_bytes=48 * 1024 * 1024
        ),
    )(
        win,
        *passed[0:10],
        bias,
        index,
        *passed[10:],
    )
    outs = pl.pallas_call(
        final_kernel,
        out_shape=(
            shape((6, 12, 2, C), BF16),
            shape((6, 12, 2, C), BF16),
            shape((2, C), F32),
            shape((2, C), F32),
            shape((C, 3 * C), F32),
            shape((3 * C,), F32),
            shape((C, C), F32),
            shape((C,), F32),
            shape((C, FF), F32),
            shape((FF,), F32),
            shape((C, FF), F32),
            shape((C,), F32),
            shape((1, HEADS, 1, NBIAS), F32),
        ),
        in_specs=[vmem] * 4,
        out_specs=(vmem,) * 13,
        name="outputs",
        compiler_params=pltpu.CompilerParams(vmem_limit_bytes=32 * 1024 * 1024),
    )(out, din, full, tgrad)
    outs = list(outs)
    for n in (0, 1):
        outs[n] = outs[n].transpose(2, 0, 1, 3)
    outs[10] = outs[10].T
    outs[12] = outs[12].transpose(0, 2, 1, 3)
    return tuple(outs)


def solution(mesh):
    field = P(None, "lat", "lon", None)
    table = P(None, "lat", None, None)
    return jax.shard_map(
        on_device,
        mesh=mesh,
        in_specs=(field, P(None, "lat", "lon"), field) + (P(),) * 10 + (table, P()),
        out_specs=(field, field) + (P(),) * 10 + (table,),
        check_vma=False,
    )
```
